32 devices in a mesh: dp: 8 (over z, x), tensor: 4 (over y, core).
Axes of the slice: x: 2, y: 2, z: 4, core: 2. Of those that a mesh axis runs over, the one named last changes fastest.
Arguments:
- tokens: bfloat16 [16384, 768], P(('dp', 'tensor')), may hold values from -6 to 6
- prefix: int32 [16], P('dp'), may hold values from 102 to 512
- cotangent: bfloat16 [16384, 768], P(('dp', 'tensor')), may hold values from -6 to 6
- first_gain: float32 [768], P('dp'), may hold values from 0.1 to 1.9
- first_shift: float32 [768], P('dp'), may hold values from -2 to 2
- qkv_weight: float32 [3, 768, 768], P(None, 'dp', 'tensor'), may hold values from -0.21875 to 0.21875
- qv_bias: float32 [2, 768], P(None, 'dp'), may hold values from -1.2 to 1.2
- out_weight: float32 [768, 768], P(None, 'dp'), may hold values from -0.875 to 0.875
- out_bias: float32 [768], P('dp'), may hold values from -2 to 2
- second_gain: float32 [768], P('dp'), may hold values from 0.1 to 1.9
- second_shift: float32 [768], P('dp'), may hold values from -2 to 2
- fc_weight: float32 [768, 3072], P('dp', 'tensor'), may hold values from -0.21875 to 0.21875
- fc_bias: float32 [3072], P('dp'), may hold values from -3 to 3
- proj_weight: float32 [3072, 768], P('tensor', 'dp'), may hold values from -0.109375 to 0.109375
- proj_bias: float32 [768], P('dp'), may hold values from -2 to 2
Outputs:
- block_out: bfloat16 [16384, 768], P(('dp', 'tensor'))
- input_grad: bfloat16 [16384, 768], P(('dp', 'tensor'))
- first_gain_grad: float32 [768], P('dp')
- first_shift_grad: float32 [768], P('dp')
- qkv_weight_grad: float32 [3, 768, 768], P(None, 'dp', 'tensor')
- qv_bias_grad: float32 [2, 768], P(None, 'dp')
- out_weight_grad: float32 [768, 768], P(None, 'dp')
- out_bias_grad: float32 [768], P('dp')
- second_gain_grad: float32 [768], P('dp')
- second_shift_grad: float32 [768], P('dp')
- fc_weight_grad: float32 [768, 3072], P('dp', 'tensor')
- fc_bias_grad: float32 [3072], P('dp')
- proj_weight_grad: float32 [3072, 768], P('tensor', 'dp')
- proj_bias_grad: float32 [768], P('dp')
The draws below stay inside these ranges and needn't reach their ends.
All inputs are finite; a program needn't handle non-finite values.
Results may differ from the reference program's by a relative error of at most 0.013.
The reference program's roundings to bfloat16 on the way count: a program that leaves them out, or rounds other values in their place, can miss the bound.
Values may be sent and summed in bfloat16 or wider, within the bound.
A program may use at most 128 MiB of HBM per device.

```python
import math
from functools import partial
import jax
import jax.numpy as jnp
from jax import lax

D = 768
HEADS = 12
HD = 64
FF = 3072
LEN = 1024
SEQS = 16
TOKENS = 16384


def set_ends(values, key, smallest, top_value):
    index_at = [jax.random.randint(jax.random.fold_in(key, axis), (), 0, length) for axis, length in enumerate(values.shape)]
    main_axis = values.shape.index(max(values.shape))
    next_to = index_at[:main_axis] + [(index_at[main_axis] + 1) % values.shape[main_axis]] + index_at[main_axis + 1:]
    return values.at[tuple(index_at)].set(smallest).at[tuple(next_to)].set(top_value)


def block_scale(own_key, shape, cuts, low, high):
    level, own = 1.0, jax.random.fold_in(own_key, 6)
    for position, shards_of in cuts:
        draws = jnp.exp(jax.random.uniform(jax.random.fold_in(own, position), (shards_of,), jnp.float32, low / len(cuts), high / len(cuts)))
        level = level * jnp.repeat(draws, shape[position] // shards_of).reshape([-1 if axis == position else 1 for axis in range(len(shape))])
    return level


def noise(rng, shape, spread, limit, cuts=(), dtype=jnp.bfloat16):
    array = jax.random.normal(rng, shape, jnp.float32) * spread
    if len(cuts) > 0:
        array = block_scale(rng, shape, cuts, -0.22, 0.18) * array
    return jnp.clip(array, min=-limit, max=limit).astype(dtype)


def setup_inputs(seed: int = 0) -> dict:
    streams_of = jax.random.split(jax.random.key(seed), 16)
    return {
        "tokens": noise(streams_of[0], (TOKENS, D), 1.0, 6.0, ((0, 32),)),
        "prefix": set_ends(jax.random.randint(streams_of[1], (SEQS,), LEN // 10, LEN // 2 + 1), jax.random.fold_in(streams_of[1], 1), LEN // 10, (LEN // 2 + 1) - 1).astype(jnp.int32),
        "cotangent": noise(streams_of[2], (TOKENS, D), 1.0, 6.0, ((0, 32),)),
        "first_gain": jnp.clip(1.0 + 0.18 * jax.random.normal(streams_of[3], (D,), jnp.float32), 0.1, 1.9),
        "first_shift": noise(streams_of[4], (D,), 0.3, 2.0, ((0, 8),), jnp.float32),
        "qkv_weight": noise(streams_of[5], (3, D, D), D ** -0.5, 0.21875, ((1, 8), (2, 4)), jnp.float32),
        "qv_bias": noise(streams_of[6], (2, D), 0.2, 1.2, ((1, 8),), jnp.float32),
        "out_weight": noise(streams_of[7], (D, D), (D // 16) ** -0.5, 0.875, ((1, 8),), jnp.float32),
        "out_bias": noise(streams_of[8], (D,), 0.3, 2.0, ((0, 8),), jnp.float32),
        "second_gain": jnp.clip(1.0 + 0.18 * jax.random.normal(streams_of[9], (D,), jnp.float32), 0.1, 1.9),
        "second_shift": noise(streams_of[10], (D,), 0.3, 2.0, ((0, 8),), jnp.float32),
        "fc_weight": noise(streams_of[11], (D, FF), D ** -0.5, 0.21875, ((0, 8), (1, 4)), jnp.float32),
        "fc_bias": noise(streams_of[12], (FF,), 0.5, 3.0, ((0, 8),), jnp.float32),
        "proj_weight": noise(streams_of[13], (FF, D), FF ** -0.5, 0.109375, ((0, 4), (1, 8)), jnp.float32),
        "proj_bias": noise(streams_of[14], (D,), 0.3, 2.0, ((0, 8),), jnp.float32),
    }


@jax.custom_vjp
def low(v):
    return lax.optimization_barrier(v.astype(jnp.bfloat16)).astype(jnp.float32)

@jax.custom_vjp
def low_back(v):
    return v

def low_keep(v):
    return (low(v), None)

def low_pass(kept, grad):
    return (grad,)

def back_keep(v):
    return (v, None)

def back_low(kept, grad):
    return (low(grad),)
low.defvjp(low_keep, low_pass)
low_back.defvjp(back_keep, back_low)
EPSILON = 1e-05

def product(left, right):
    return jnp.dot(left, right, precision=lax.Precision.HIGHEST)

def rounded_both(values):
    return low(low_back(values))

def layer_norm(values, norm_gain, norm_shift):
    average = lax.optimization_barrier(jnp.mean(values, axis=-1, keepdims=True))
    centred = values - average
    variance = lax.optimization_barrier(jnp.mean(centred * centred, axis=-1, keepdims=True))
    return centred * lax.rsqrt(variance + EPSILON) * norm_gain + norm_shift

def attend(queries, key_heads, value_heads, prefix_size):
    score_scale = 1.0 / math.sqrt(HD)
    scores = jnp.einsum('qhd,khd->hqk', queries, key_heads, precision=lax.Precision.HIGHEST) * score_scale
    scores = low_back(scores)
    row_pos = lax.broadcasted_iota(jnp.int32, (LEN, LEN), 0)
    col_pos = lax.broadcasted_iota(jnp.int32, (LEN, LEN), 1)
    allowed = (col_pos < prefix_size) | (col_pos <= row_pos)
    scores = jnp.where(allowed[None], scores, -1e+30)
    row_peak = lax.optimization_barrier(jnp.max(scores, axis=-1, keepdims=True))
    weights = jnp.exp(scores - row_peak)
    shares = low(weights / lax.optimization_barrier(jnp.sum(weights, axis=-1, keepdims=True)))
    context = jnp.einsum('hqk,khd->qhd', shares, value_heads, precision=lax.Precision.HIGHEST)
    return context.reshape(LEN, D)

def mapped_entry(entries):
    return jax.checkpoint(attend)(entries[0], entries[1], entries[2], entries[3])

def residual_block(prefix_block, params, inputs):
    rounded = [low(value) for value in params]
    first_gain, first_shift, qkv_weight, qv_bias, out_weight, out_bias = rounded[:6]
    second_gain, second_shift, fc_weight, fc_bias, proj_weight, proj_bias = rounded[6:]
    normed_one = low(layer_norm(inputs, first_gain, first_shift))
    queries = rounded_both(product(normed_one, qkv_weight[0]) + qv_bias[0])
    key_heads = rounded_both(product(normed_one, qkv_weight[1]))
    value_heads = rounded_both(product(normed_one, qkv_weight[2]) + qv_bias[1])
    seq_count = inputs.shape[0] // LEN
    head_shape = (seq_count, LEN, HEADS, HD)
    context = lax.map(mapped_entry, (queries.reshape(head_shape), key_heads.reshape(head_shape), value_heads.reshape(head_shape), prefix_block))
    context = rounded_both(context.reshape(inputs.shape[0], D))
    middle = inputs + low_back(product(context, out_weight) + out_bias)
    normed_two = low(layer_norm(middle, second_gain, second_shift))
    pre_act = low_back(product(normed_two, fc_weight) + fc_bias)
    hidden = low(jax.nn.gelu(pre_act, approximate=True))
    return middle + low_back(product(hidden, proj_weight) + proj_bias)

def reference(tokens, prefix, cotangent, first_gain, first_shift, qkv_weight, qv_bias, out_weight, out_bias, second_gain, second_shift, fc_weight, fc_bias, proj_weight, proj_bias):
    params = (first_gain, first_shift, qkv_weight, qv_bias, out_weight, out_bias, second_gain, second_shift, fc_weight, fc_bias, proj_weight, proj_bias)
    group_seqs = math.gcd(SEQS, max(1, 4096 // LEN))
    group_count = SEQS // group_seqs
    token_groups = tokens.astype(jnp.float32).reshape(group_count, group_seqs * LEN, D)
    cot_groups = cotangent.astype(jnp.float32).reshape(group_count, group_seqs * LEN, D)
    prefix_groups = prefix.reshape(group_count, group_seqs)

    def one_group(totals, entries):
        block_tokens, block_prefix, block_cot = entries
        outputs, pullback = jax.vjp(partial(residual_block, block_prefix), params, block_tokens)
        param_grads, token_grads = pullback(block_cot)
        totals = jax.tree.map(jnp.add, totals, param_grads)
        return (totals, (outputs.astype(jnp.bfloat16), token_grads.astype(jnp.bfloat16)))
    initial = jax.tree.map(jnp.zeros_like, params)
    totals, (outputs, token_grads) = lax.scan(one_group, initial, (token_groups, prefix_groups, cot_groups))
    block_out = outputs.reshape(TOKENS, D)
    input_grad = token_grads.reshape(TOKENS, D)
    return (block_out, input_grad, totals[0], totals[1], totals[2], totals[3], totals[4], totals[5], totals[6], totals[7], totals[8], totals[9], totals[10], totals[11])
```

```python
import functools
import math

import jax
import jax.numpy as jnp
from jax import lax
from jax.experimental import pallas as pl
from jax.experimental.pallas import tpu as pltpu
from jax.sharding import PartitionSpec as P

MESH = pl.DeviceIdType.MESH
LOW, FULL = jnp.bfloat16, jnp.float32
EPSILON = 1e-05
HD = 64
GROUPS, ZN, XN = 8, 4, 2
SEMS = 120
VEC = 16

GAIN1, SHIFT1, OUTB, GAIN2, SHIFT2, PROJB, QKVB, FCB = 0, 1, 2, 3, 4, 5, 6, 8


def dot(a, b):
    return jnp.dot(a, b, preferred_element_type=FULL)


def dot_nt(a, b):
    return lax.dot_general(a, b, (((1,), (1,)), ((), ())), preferred_element_type=FULL)


def dot_tn(a, b):
    return lax.dot_general(a, b, (((0,), (0,)), ((), ())), preferred_element_type=FULL)


def block_kernel(repeat, seq_len, *refs):
    (
        tok_h, cot_h, vec_h, wq_h, wo_h, wf_h, wp_h, prefix_s,
        bo_ref, ig_ref, gq_ref, go_ref, gf_ref, gp_ref, vo_ref,
        Wq, Wo, Wf, Wp, Go, Gp,
        RqA1, RqB1, RqA2, RqB2, Rq3,
        RfA1, RfB1, RfA2, RfB2, Rf3,
        RpA1, RpB1, RpA2, RpB2, Rp3,
        Ro1, Ro2, Ro3,
        TOK, COT, N1F, N2F, RS1, RS2, N1, N2, T0, T1,
        QP, KP, VP, CTX, DO, DQ, LSEC, LSER, DELR,
        MID, S0, V0, V1, H, GPR, PG,
        VR, VF, VG, VX, VR1, VR2,
        ss, rs, ls,
    ) = refs
    half = seq_len // 2
    width = TOK.shape[1]
    rblk = 256
    nrb = seq_len // rblk
    dp = lax.axis_index("dp")
    t = lax.axis_index("tensor")
    s, sub = dp // repeat, dp % repeat
    z, x = s // XN, s % XN
    y, c = t // 2, t % 2
    oy, oc, ox = 1 - y, 1 - c, 1 - x

    def at(zz, xx, tt):
        return ((zz * XN + xx) * repeat + sub, tt)

    def zdev(k):
        return at((z + k) % ZN, x, t)

    xdev = at(z, ox, t)
    ydev = at(z, x, oy * 2 + c)
    cdev = at(z, x, y * 2 + oc)
    gdev = at(z, x, oy * 2 + oc)
    others = [(((s + k) % GROUPS) * repeat + sub, t) for k in range(1, GROUPS)]

    made = []

    def copy(src, dst, dev):
        k = len(made)

        def make():
            return pltpu.make_async_remote_copy(
                src_ref=src, dst_ref=dst, send_sem=ss.at[k], recv_sem=rs.at[k],
                device_id=dev, device_id_type=MESH,
            )

        made.append(make)
        return make

    def start(makes):
        for m in makes:
            m().start()

    def landed(makes):
        for m in makes:
            m().wait_recv()

    def sent(makes):
        for m in makes:
            m().wait_send()

    barrier = pltpu.get_barrier_semaphore()
    peers = others + [cdev, ydev, gdev]
    for d in peers:
        pl.semaphore_signal(barrier, inc=1, device_id=d, device_id_type=MESH)

    local = [
        pltpu.make_async_copy(vec_h, VR.at[s], ls.at[0]),
        pltpu.make_async_copy(wo_h, Wo.at[z, x, y], ls.at[1]),
        pltpu.make_async_copy(wq_h, Wq.at[y, z, x], ls.at[2]),
        pltpu.make_async_copy(tok_h, TOK, ls.at[3]),
        pltpu.make_async_copy(cot_h, COT.at[c], ls.at[4]),
        pltpu.make_async_copy(wf_h, Wf.at[y, z, x], ls.at[5]),
        pltpu.make_async_copy(wp_h, Wp.at[y, z, x], ls.at[6]),
    ]
    for cp in local:
        cp.start()
    pl.semaphore_wait(barrier, len(peers))

    vec_c = [copy(VR.at[s], VR.at[s], d) for d in others]
    cot_c = [copy(COT.at[c], COT.at[c], cdev)]
    hr = wq_h.shape[0] // 2
    halves = (pl.ds(0, hr), pl.ds(hr, hr))

    def gather(W):
        zs = [[copy(W.at[y, z, x, r], W.at[y, z, x, r], zdev(k)) for k in range(1, ZN)] for r in halves]
        a, b = halves
        one = [
            [copy(W.at[y, :, x, a], W.at[y, :, x, a], xdev)],
            [copy(W.at[y, :, x, b], W.at[y, :, x, b], ydev)],
        ]
        two = [
            [copy(W.at[y, :, :, a], W.at[y, :, :, a], ydev)],
            [copy(W.at[:, :, x, b], W.at[:, :, x, b], xdev)],
        ]
        return zs, one, two

    ow = [
        [copy(Wo.at[z, x, y], Wo.at[z, x, y], xdev)],
        [copy(Wo.at[z, :, y], Wo.at[z, :, y], ydev)],
        [copy(Wo.at[z], Wo.at[z], zdev(k)) for k in range(1, ZN)],
    ]
    qw, pw, fw = gather(Wq), gather(Wp), gather(Wf)

    def z_go(w):
        for h in range(2):
            start(w[0][h])

    def one_go(w):
        for h in range(2):
            landed(w[0][h])
            start(w[1][h])

    def two_go(w):
        for h in range(2):
            landed(w[1][h])
            start(w[2][h])

    def all_in(w):
        for h in range(2):
            landed(w[2][h])

    local[0].wait()
    start(vec_c)
    local[1].wait()
    start(ow[0])
    local[2].wait()
    z_go(qw)
    local[4].wait()
    start(cot_c)
    local[3].wait()

    def row_tile(i, n=128):
        return pl.ds(pl.multiple_of(i * n, n), n)

    @pl.loop(0, half // 128)
    def _(i):
        r = row_tile(i)
        v = TOK[r, :].astype(FULL)
        v = v - jnp.mean(v, axis=-1, keepdims=True)
        rstd = lax.rsqrt(jnp.mean(v * v, axis=-1, keepdims=True) + EPSILON)
        N1F[r, :] = v * rstd
        RS1[r, :] = jnp.broadcast_to(rstd, (128, 128))

    local[5].wait()
    local[6].wait()
    landed(vec_c)
    vf = VR[0].astype(FULL)
    for g in range(1, GROUPS):
        vf = vf + VR[g].astype(FULL)
    VF[...] = vf
    VG[...] = jnp.zeros(VG.shape, FULL)

    def vrow(i):
        return VF[i : i + 1, :]

    @pl.loop(0, half // 128)
    def _(i):
        r = row_tile(i)
        N1[c, r, :] = (N1F[r, :] * vrow(GAIN1) + vrow(SHIFT1)).astype(LOW)

    n1_c = [copy(N1.at[c], N1.at[c], cdev)]
    start(n1_c)
    landed(ow[0])
    start(ow[1])
    landed(cot_c)

    def transpose_all(source, target):
        @pl.loop(0, nrb)
        def _(i):
            h, off = i // (half // rblk), i % (half // rblk)
            rows = pl.ds(pl.multiple_of(off * rblk, rblk), rblk)
            cols = pl.ds(pl.multiple_of(i * rblk, rblk), rblk)
            for k in range(width // rblk):
                target[k * rblk : (k + 1) * rblk, cols] = source[h, rows, k * rblk : (k + 1) * rblk].T

    transpose_all(COT, T0)
    one_go(qw)
    z_go(fw)
    two_go(qw)
    landed(n1_c)
    landed(ow[1])
    one_go(fw)
    z_go(pw)
    all_in(qw)

    def low_lanes(v):
        return lax.broadcasted_iota(jnp.int32, v.shape, 1) < HD

    def tile(v, i):
        return v[:, i * 128 : (i + 1) * 128]

    def roll(v):
        return pltpu.roll(v, HD, 1)

    @pl.loop(0, nrb)
    def _(i):
        h, off = i // (half // rblk), i % (half // rblk)
        rows = pl.ds(pl.multiple_of(off * rblk, rblk), rblk)
        out = pl.ds(pl.multiple_of(i * rblk, rblk), rblk)
        n = N1[h, rows, :]
        got = []
        for b in range(2):
            got.append(dot(n, Wq[b].reshape(width, Wq.shape[-1])) + VF[QKVB + b : QKVB + b + 1, : Wq.shape[-1]])
            QP[b, out, :] = (tile(got[b], 0).astype(LOW).astype(FULL) * 0.125).astype(LOW)
            KP[b, out, :] = tile(got[b], 1).astype(LOW)
            VP[b, out, :] = tile(got[b], 2).astype(LOW)
        first = low_lanes(tile(got[0], 3))
        q = jnp.where(first, tile(got[0], 3), roll(tile(got[1], 3)))
        QP[2, out, :] = (q.astype(LOW).astype(FULL) * 0.125).astype(LOW)
        KP[2, out, :] = jnp.where(first, roll(tile(got[0], 3)), tile(got[1], 3)).astype(LOW)
        VP[2, out, :] = jnp.where(first, tile(got[0], 4), roll(tile(got[1], 4))).astype(LOW)

    prefix = prefix_s[y]
    LSEC[...] = jnp.zeros(LSEC.shape, FULL)

    def lane_part(v, e):
        lane = lax.broadcasted_iota(jnp.int32, v.shape, 1)
        keep = lane < HD if e == 0 else lane >= HD
        return jnp.where(keep, v, jnp.zeros_like(v))

    @pl.loop(0, 3)
    def _(p):
        for b in range(nrb):
            rows = pl.ds(b * rblk, rblk)
            cols = max(half, (b + 1) * rblk)
            q = QP[p, rows, :]
            keys, values = KP[p, :cols, :], VP[p, :cols, :]
            query = b * rblk + lax.broadcasted_iota(jnp.int32, (rblk, 1), 0)
            limit = jnp.maximum(prefix - 1, query)
            key = lax.broadcasted_iota(jnp.int32, (rblk, cols), 1)
            parts = []
            for e in range(2):
                sc = dot_nt(lane_part(q, e), keys)
                sc = jnp.where(key <= limit, sc, -1e30)
                peak = jnp.max(sc, axis=-1, keepdims=True)
                w = jnp.exp(sc - peak)
                total = jnp.sum(w, axis=-1, keepdims=True)
                parts.append(dot(w.astype(LOW), values) * (1.0 / total))
                lane = lax.broadcasted_iota(jnp.int32, (rblk, 128), 1)
                LSEC[rows, :] = jnp.where(lane == 2 * p + e, peak + jnp.log(total), LSEC[rows, :])
            CTX[p, rows, :] = jnp.where(low_lanes(parts[0]), parts[0], parts[1]).astype(LOW)

        @pl.when(p == 0)
        def _():
            two_go(fw)

        @pl.when(p == 1)
        def _():
            one_go(pw)

    start(ow[2])
    two_go(pw)
    for b in range(nrb):
        lt = LSEC[b * rblk : (b + 1) * rblk, :].T
        for h in range(6):
            LSER[h, :, b * rblk : (b + 1) * rblk] = lt[h : h + 1, :]
    landed(ow[2])

    def wide(ref, rows):
        return jnp.concatenate([ref[0, rows, :], ref[1, rows, :], ref[2, rows, :]], axis=1)

    def split_rows(make_block, away, home, copies):
        per = half // rblk
        for which, target in ((oc, away), (c, home)):

            @pl.loop(0, per)
            def _(j):
                rows = pl.ds(pl.multiple_of(j * rblk, rblk), rblk)
                flat = pl.ds(pl.multiple_of((which * per + j) * rblk, rblk), rblk)
                target[rows, :] = make_block(which, rows, flat)

            if target is away:
                start(copies)

    po_c = [copy(S0, V0, cdev)]
    split_rows(
        lambda h, rows, flat: dot_nt(wide(CTX, flat), Wo[...].reshape(width, Wo.shape[-1])), S0, MID, po_c
    )
    landed(po_c)

    @pl.loop(0, half // 128)
    def _(i):
        r = row_tile(i)
        m = TOK[r, :].astype(FULL) + (MID[r, :] + V0[r, :] + vrow(OUTB))
        MID[r, :] = m
        v = m - jnp.mean(m, axis=-1, keepdims=True)
        rstd = lax.rsqrt(jnp.mean(v * v, axis=-1, keepdims=True) + EPSILON)
        n = v * rstd
        N2F[r, :] = n
        RS2[r, :] = jnp.broadcast_to(rstd, (128, 128))
        N2[c, r, :] = (n * vrow(GAIN2) + vrow(SHIFT2)).astype(LOW)

    n2_c = [copy(N2.at[c], N2.at[c], cdev)]
    start(n2_c)
    landed(n2_c)
    all_in(fw)

    root = math.sqrt(2.0 / math.pi)

    @pl.loop(0, nrb * 2)
    def _(k):
        b, i = k // nrb, k % nrb
        h, off = i // (half // rblk), i % (half // rblk)
        rows = pl.ds(pl.multiple_of(off * rblk, rblk), rblk)
        flat = pl.ds(pl.multiple_of(i * rblk, rblk), rblk)
        u = dot(N2[h, rows, :], Wf[b].reshape(width, width)) + VF[pl.ds(FCB + b, 1), :]
        uu = u * u
        th = jnp.tanh(root * u * (1.0 + 0.044715 * uu))
        H[b, flat, :] = (0.5 * u * (1.0 + th)).astype(LOW)
        GPR[b, flat, :] = 0.5 * (1.0 + th) + (0.5 * root) * u * (1.0 - th * th) * (1.0 + 0.134145 * uu)

    def weight_grad(left_t, right, G, columns):
        @pl.loop(0, 4)
        def _(k):
            b, m = k // 2, k % 2
            rows = pl.ds(pl.multiple_of(m * (width // 2), width // 2), width // 2)
            g = dot(left_t[rows, :], right[b, :, :columns])
            g = g.astype(LOW).reshape(ZN // 2, XN, width // GROUPS, columns)
            G[b, pl.ds(m * (ZN // 2), ZN // 2), :, :, :columns] = g

    def reduce_copies(G, cols, A1, B1, A2, B2, R3):
        a, b = halves
        one = [
            [copy(G.at[:, :, ox, a, cols], A1, xdev)],
            [copy(G.at[oy, :, :, b, cols], B1, ydev)],
        ]
        two = [
            [copy(G.at[oy, :, x, a, cols], A2, ydev)],
            [copy(G.at[y, :, ox, b, cols], B2, xdev)],
        ]
        three = [
            [copy(G.at[y, (z + k) % ZN, x, r, cols], R3.at[k - 1, r], zdev(k)) for k in range(1, ZN)]
            for r in halves
        ]

        def add(target, source):
            target[...] = (target[...].astype(FULL) + source[...].astype(FULL)).astype(LOW)

        def go():
            start(one[0])
            start(one[1])

        def second():
            landed(one[0])

            @pl.loop(0, ZN)
            def _(k):
                add(G.at[oy, k, x, a, cols], A1.at[oy, k])

            start(two[0])
            landed(one[1])

            @pl.loop(0, ZN)
            def _(k):
                add(G.at[y, k, ox, b, cols], B1.at[k, ox])

            start(two[1])

            @pl.loop(0, ZN)
            def _(k):
                add(G.at[y, k, x, a, cols], A1.at[y, k])
                add(G.at[y, k, x, b, cols], B1.at[k, x])

        def third():
            for h, R in ((0, A2), (1, B2)):
                landed(two[h])

                @pl.loop(0, ZN)
                def _(k):
                    add(G.at[y, k, x, halves[h], cols], R.at[k])

                start(three[h])

        def last(out):
            for h in range(2):
                landed(three[h])
                r = halves[h]
                v = G[y, z, x, r, cols].astype(FULL)
                for k in range(ZN - 1):
                    v = v + R3[k, r, :].astype(FULL)
                out[r, :] = v

        return go, second, third, last

    every = pl.ds(0, width)
    rp = reduce_copies(Gp, every, RpA1, RpB1, RpA2, RpB2, Rp3)
    weight_grad(T0, H, Gp, width)
    rp[0]()
    transpose_all(N2, T1)
    all_in(pw)

    @pl.loop(0, nrb * 2)
    def _(k):
        b, i = k // nrb, k % nrb
        h, off = i // (half // rblk), i % (half // rblk)
        rows = pl.ds(pl.multiple_of(off * rblk, rblk), rblk)
        flat = pl.ds(pl.multiple_of(i * rblk, rblk), rblk)
        g = (dot(COT[h, rows, :], Wp[b].reshape(width, width)) * GPR[b, flat, :]).astype(LOW)
        PG[b, flat, :] = g
        VG[pl.ds(FCB + b, 1), :] += jnp.sum(g.astype(FULL), axis=0, keepdims=True)

    p2_c = [copy(S0, V1, cdev)]
    home2, homem, home1 = GPR.at[0, pl.ds(0, half)], GPR.at[0, pl.ds(half, half)], GPR.at[1, pl.ds(0, half)]
    awaym = GPR.at[1, pl.ds(half, half)]

    def pair_nt(A, W, columns):
        def block(h, rows, flat):
            return dot_nt(A[0, flat, :columns], W[0].reshape(width, W.shape[-1])) + dot_nt(
                A[1, flat, :columns], W[1].reshape(width, W.shape[-1])
            )

        return block

    sent(po_c)
    split_rows(pair_nt(PG, Wf, width), S0, home2, p2_c)
    pm_c = [copy(awaym, V0, cdev)]
    split_rows(pair_nt(H, Wp, width), awaym, homem, pm_c)
    for group in pw[0] + pw[1] + pw[2]:
        sent(group)
    weight_grad(T1, PG, Wp, width)
    rf = reduce_copies(Wp, every, RfA1, RfB1, RfA2, RfB2, Rf3)
    rf[0]()
    landed(p2_c)

    sent(n2_c)

    def norm_back(dy, n, rstd, gain):
        e = dy * gain
        return (e - jnp.mean(e, axis=-1, keepdims=True) - n * jnp.mean(e * n, axis=-1, keepdims=True)) * rstd

    def add_row(i, v):
        VG[i : i + 1, :] += jnp.sum(v, axis=0, keepdims=True)

    @pl.loop(0, half // 128)
    def _(i):
        r = row_tile(i)
        dy = GPR[0, r, :] + V1[r, :]
        n = N2F[r, :]
        add_row(GAIN2, dy * n)
        add_row(SHIFT2, dy)
        cot = COT[c, r, :].astype(FULL)
        add_row(PROJB, cot)
        g = cot + norm_back(dy, n, RS2[r, 0:1], vrow(GAIN2))
        N2F[r, :] = g
        low = g.astype(LOW)
        add_row(OUTB, low.astype(FULL))
        N2[c, r, :] = low

    ag_c = [copy(N2.at[c], N2.at[c], cdev)]
    start(ag_c)
    rp[1]()
    landed(pm_c)

    @pl.loop(0, half // 128)
    def _(i):
        r = row_tile(i)
        far = row_tile(i + half // 128)
        bo_ref[r, :] = (MID[r, :] + (GPR[0, far, :] + V0[r, :] + vrow(PROJB))).astype(LOW)

    landed(ag_c)

    @pl.loop(0, nrb)
    def _(i):
        h, off = i // (half // rblk), i % (half // rblk)
        rows = pl.ds(pl.multiple_of(off * rblk, rblk), rblk)
        flat = pl.ds(pl.multiple_of(i * rblk, rblk), rblk)
        g = dot(N2[h, rows, :], Wo[...].reshape(width, Wo.shape[-1])).astype(LOW)
        row = lax.broadcasted_iota(jnp.int32, (8, 128), 0)
        lane = lax.broadcasted_iota(jnp.int32, (8, 128), 1)
        pick = jnp.where(lane // HD == row, 1.0, 0.0).astype(LOW)
        for p in range(3):
            gp = tile(g, p)
            DO[p, flat, :] = gp
            prod = gp.astype(FULL) * CTX[p, flat, :].astype(FULL)
            high = prod.astype(LOW)
            rest = (prod - high.astype(FULL)).astype(LOW)
            d = dot_nt(pick, high) + dot_nt(pick, rest)
            for e in range(2):
                DELR[2 * p + e, :, flat] = d[e : e + 1, :]

    transpose_all(N2, T0)

    @pl.loop(0, 2)
    def _(m):
        rows = pl.ds(pl.multiple_of(m * (width // 2), width // 2), width // 2)
        g = dot(T0[rows, :], wide(CTX, pl.ds(0, seq_len)))
        g = g.astype(LOW).reshape(ZN // 2, XN, 2, width // (2 * GROUPS), Wo.shape[-1])
        Go[pl.ds(m * (ZN // 2), ZN // 2)] = g

    ro = [
        [copy(Go.at[(z + k) % ZN], Ro1.at[k - 1], zdev(k)) for k in range(1, ZN)],
        [copy(Go.at[z, :, oy], Ro2, ydev)],
        [copy(Go.at[z, ox, y], Ro3, xdev)],
        [copy(go_ref.at[t], go_ref.at[t], d) for d in (cdev, ydev, gdev)],
    ]
    start(ro[0])

    @pl.loop(0, 3)
    def _(p):
        DQ[...] = jnp.zeros(DQ.shape, FULL)
        for b in range(nrb):
            rows = pl.ds(b * rblk, rblk)
            first = 0 if b * rblk < half else b * rblk
            n = seq_len - first
            keys, values = KP[p, rows, :], VP[p, rows, :]
            queries, grads = QP[p, first:, :], DO[p, first:, :]
            key = b * rblk + lax.broadcasted_iota(jnp.int32, (rblk, 1), 0)
            limit = jnp.where(key < prefix, 0, key)
            query = first + lax.broadcasted_iota(jnp.int32, (rblk, n), 1)
            dk, dv = [], []
            for e in range(2):
                ke, ve = lane_part(keys, e), lane_part(values, e)
                sc = dot_nt(ke, queries) - LSER[2 * p + e, :, first:]
                w = jnp.exp(jnp.where(query >= limit, sc, -1e30))
                dw = dot_nt(ve, grads) - DELR[2 * p + e, :, first:]
                ds = (w * dw).astype(LOW)
                dv.append(dot(w.astype(LOW), grads))
                dk.append(dot(ds, queries))
                DQ[first:, :] += dot_tn(ds, ke)
            KP[p, rows, :] = jnp.where(low_lanes(dk[0]), dk[0], dk[1]).astype(LOW)
            VP[p, rows, :] = jnp.where(low_lanes(dv[0]), dv[0], dv[1]).astype(LOW)
        QP[p, :, :] = (DQ[...] * 0.125).astype(LOW)

        @pl.when(p == 0)
        def _():
            rf[1]()
            rp[2]()

        @pl.when(p == 1)
        def _():
            rf[2]()

    landed(ro[0])
    for i in range(2):
        for j in range(2):
            v = Go[z, i, j].astype(FULL)
            for k in range(ZN - 1):
                v = v + Ro1[k, i, j].astype(FULL)
            Go[z, i, j] = v.astype(LOW)
    start(ro[1])

    @pl.loop(0, nrb)
    def _(i):
        flat = pl.ds(pl.multiple_of(i * rblk, rblk), rblk)
        for b in range(2):
            for k, ref in enumerate((QP, KP, VP)):
                H[b, flat, k * 128 : (k + 1) * 128] = ref[b, flat, :]
        q, k, v = (ref[2, flat, :].astype(FULL) for ref in (QP, KP, VP))
        first = low_lanes(q)
        H[0, flat, 384:512] = jnp.where(first, q, roll(k)).astype(LOW)
        H[1, flat, 384:512] = jnp.where(first, roll(q), k).astype(LOW)
        H[0, flat, 512:640] = jnp.where(first, v, 0.0).astype(LOW)
        H[1, flat, 512:640] = jnp.where(first, roll(v), 0.0).astype(LOW)
        for b in range(2):
            VG[QKVB + b : QKVB + b + 1, : Wq.shape[-1]] += jnp.sum(
                H[b, flat, : Wq.shape[-1]].astype(FULL), axis=0, keepdims=True
            )

    packed = Wq.shape[-1]
    for group in fw[0] + fw[1] + fw[2]:
        sent(group)
    transpose_all(N1, T1)
    weight_grad(T1, H, Wf, packed)
    rq = reduce_copies(Wf, pl.ds(0, packed), RqA1, RqB1, RqA2, RqB2, Rq3)
    rq[0]()
    p1_c = [copy(S0, V1, cdev)]
    sent(p2_c)
    split_rows(pair_nt(H, Wq, packed), S0, home1, p1_c)
    landed(ro[1])
    for i in range(2):
        Go[z, i, y] = (Go[z, i, y].astype(FULL) + Ro2[i].astype(FULL)).astype(LOW)
    start(ro[2])
    rp[3](gp_ref)
    landed(p1_c)

    @pl.loop(0, half // 128)
    def _(i):
        r = row_tile(i)
        dy = GPR[1, r, :] + V1[r, :]
        n = N1F[r, :]
        add_row(GAIN1, dy * n)
        add_row(SHIFT1, dy)
        ig_ref[r, :] = (N2F[r, :] + norm_back(dy, n, RS1[r, 0:1], vrow(GAIN1))).astype(LOW)

    hv = VEC // 2
    VX[...] = VG[...].reshape(2, hv, width)
    v_c = [copy(VX.at[oy], VR1, ydev)]
    start(v_c)
    rq[1]()
    landed(ro[2])
    go_ref[t] = Go[z, x, y].astype(FULL) + Ro3[...].astype(FULL)
    start(ro[3])
    landed(v_c)
    VR2[s] = VX[y] + VR1[...]
    v2_c = [copy(VR2.at[s], VR2.at[s], d) for d in others]
    start(v2_c)
    rf[3](gf_ref)
    landed(v2_c)
    total = VR2[0]
    for g in range(1, GROUPS):
        total = total + VR2[g]
    vo_ref[t] = total
    v3_c = [copy(vo_ref.at[t], vo_ref.at[t], d) for d in (cdev, ydev, gdev)]
    start(v3_c)
    rq[2]()
    landed(v3_c)
    landed(ro[3])
    rq[3](gq_ref)

    waited = {id(m) for m in po_c + n2_c + p2_c}
    for w in (pw, fw):
        for part in w:
            for group in part:
                waited |= {id(m) for m in group}
    sent([m for m in made if id(m) not in waited])


def gather_groups(v, axis, repeat, groups):
    if repeat == 1:
        return v
    return lax.all_gather(v, "dp", axis=axis, axis_index_groups=groups, tiled=True)


def scatter_groups(v, axis, repeat, groups):
    if repeat == 1:
        return v
    return lax.psum_scatter(v, "dp", scatter_dimension=axis, axis_index_groups=groups, tiled=True)


def on_device(
    dp_size,
    tokens,
    prefix,
    cotangent,
    first_gain,
    first_shift,
    qkv_weight,
    qv_bias,
    out_weight,
    out_bias,
    second_gain,
    second_shift,
    fc_weight,
    fc_bias,
    proj_weight,
    proj_bias,
):
    repeat = dp_size // GROUPS
    groups = [[g * repeat + i for i in range(repeat)] for g in range(GROUPS)]
    half, width = tokens.shape
    seq_len = 2 * half
    s = lax.axis_index("dp") // repeat
    t = lax.axis_index("tensor")
    y, c = t // 2, t % 2

    def whole(v, axis):
        return gather_groups(v.astype(LOW), axis, repeat, groups)

    wq, wo, wf, wp = whole(qkv_weight, 1), whole(out_weight, 1), whole(fc_weight, 0), whole(proj_weight, 1)
    rows = wf.shape[0]
    cols = wq.shape[2]
    pair = 2 * HD
    zero = jnp.zeros((rows, HD), LOW)
    wq = jnp.concatenate(
        [wq[0, :, :pair], wq[1, :, :pair], wq[2, :, :pair], wq[0, :, pair:], wq[1, :, pair:], wq[2, :, pair:], zero],
        axis=1,
    )
    low_rows = lax.dynamic_slice_in_dim(wo, c * cols, cols, 0)
    high_rows = lax.dynamic_slice_in_dim(wo, (2 + c) * cols, cols, 0)
    wo = jnp.concatenate([low_rows[:pair], high_rows[:pair], low_rows[pair:], high_rows[pair:]], axis=0)
    wo = lax.dynamic_slice_in_dim(wo, y * (rows // 2), rows // 2, 1).T
    wp = wp.T

    def spread(v):
        return lax.dynamic_update_slice_in_dim(jnp.zeros((v.shape[0] * GROUPS,), LOW), v, s * v.shape[0], 0)

    vectors = [spread(whole(v, 0)) for v in (first_gain, first_shift, out_bias, second_gain, second_shift, proj_bias)]
    qb = whole(qv_bias, 1)
    qb = [spread(qb[0]), spread(qb[1])]
    fb = spread(whole(fc_bias, 0)).reshape(4, width)
    fill = jnp.zeros((pair,), LOW)
    for b in range(2):
        q, v = (lax.dynamic_slice_in_dim(r, (2 * b + c) * cols, cols, 0) for r in qb)
        vectors.append(jnp.concatenate([q[:pair], fill, v[:pair], q[pair:], fill[:HD], v[pair:], fill[:HD], fill]))
    for b in range(2):
        vectors.append(lax.dynamic_index_in_dim(fb, 2 * b + c, 0, keepdims=False))
    vec = jnp.stack(vectors + [jnp.zeros((width,), LOW)] * (VEC - len(vectors)))

    packed, own = wq.shape[1], wo.shape[1]
    hr = rows // 2
    ANY = pl.BlockSpec(memory_space=pl.ANY)
    IN_VMEM = pl.BlockSpec(memory_space=pltpu.VMEM)

    def reduce_space(lanes):
        return [
            pltpu.VMEM((2, ZN, hr, lanes), LOW),
            pltpu.VMEM((ZN, XN, hr, lanes), LOW),
            pltpu.VMEM((ZN, hr, lanes), LOW),
            pltpu.VMEM((ZN, hr, lanes), LOW),
            pltpu.VMEM((ZN - 1, rows, lanes), LOW),
        ]

    token_low = pltpu.VMEM((2, half, width), LOW)
    token_full = pltpu.VMEM((half, width), FULL)
    units = pltpu.VMEM((2, seq_len, width), LOW)
    heads = pltpu.VMEM((3, seq_len, pair), LOW)
    scratch = (
        [
            pltpu.VMEM((2, ZN, XN, rows, packed), LOW),
            pltpu.VMEM((ZN, XN, 2, hr, own), LOW),
            pltpu.VMEM((2, ZN, XN, rows, width), LOW),
            pltpu.VMEM((2, ZN, XN, rows, width), LOW),
            pltpu.VMEM((ZN, XN, 2, hr, own), LOW),
            pltpu.VMEM((2, ZN, XN, rows, width), LOW),
        ]
        + reduce_space(packed)
        + reduce_space(width)
        + reduce_space(width)
        + [
            pltpu.VMEM((ZN - 1, XN, 2, hr, own), LOW),
            pltpu.VMEM((XN, hr, own), LOW),
            pltpu.VMEM((hr, own), LOW),
        ]
        + [
            pltpu.VMEM((half, width), LOW),
            token_low,
            token_full,
            token_full,
            pltpu.VMEM((half, 128), FULL),
            pltpu.VMEM((half, 128), FULL),
            token_low,
            token_low,
            pltpu.VMEM((width, seq_len), LOW),
            pltpu.VMEM((width, seq_len), LOW),
        ]
        + [heads] * 5
        + [
            pltpu.VMEM((seq_len, pair), FULL),
            pltpu.VMEM((seq_len, 128), FULL),
            pltpu.VMEM((6, 1, seq_len), FULL),
            pltpu.VMEM((6, 1, seq_len), FULL),
        ]
        + [token_full] * 4
        + [units, pltpu.VMEM((2, seq_len, width), FULL), units]
        + [
            pltpu.VMEM((GROUPS, VEC, width), LOW),
            pltpu.VMEM((VEC, width), FULL),
            pltpu.VMEM((VEC, width), FULL),
            pltpu.VMEM((2, VEC // 2, width), FULL),
            pltpu.VMEM((VEC // 2, width), FULL),
            pltpu.VMEM((GROUPS, VEC // 2, width), FULL),
        ]
        + [
            pltpu.SemaphoreType.DMA((SEMS,)),
            pltpu.SemaphoreType.DMA((SEMS,)),
            pltpu.SemaphoreType.DMA((8,)),
        ]
    )
    out_shape = [
        jax.ShapeDtypeStruct((half, width), LOW),
        jax.ShapeDtypeStruct((half, width), LOW),
        jax.ShapeDtypeStruct((rows, packed), FULL),
        jax.ShapeDtypeStruct((4, hr, own), FULL),
        jax.ShapeDtypeStruct((rows, width), FULL),
        jax.ShapeDtypeStruct((rows, width), FULL),
        jax.ShapeDtypeStruct((4, VEC // 2, width), FULL),
    ]
    bo, ig, gq, go, gf, gp, vo = pl.pallas_call(
        functools.partial(block_kernel, repeat, seq_len),
        out_shape=out_shape,
        in_specs=[ANY] * 7 + [pl.BlockSpec(memory_space=pltpu.SMEM)],
        out_specs=[IN_VMEM] * 7,
        scratch_shapes=scratch,
        compiler_params=pltpu.CompilerParams(
            collective_id=0, has_side_effects=True, vmem_limit_bytes=62 * 1024 * 1024
        ),
    )(tokens, cotangent, vec, wq, wo, wf, wp, prefix)

    def scatter(v, axis):
        return scatter_groups(v, axis, repeat, groups)

    def part(v):
        n = v.shape[-1] // GROUPS
        return lax.dynamic_slice_in_dim(v, s * n, n, v.ndim - 1)

    third = gq[:, 3 * pair :]
    gq = jnp.stack(
        [
            jnp.concatenate([gq[:, k * pair : (k + 1) * pair], third[:, k * HD : (k + 1) * HD]], axis=1)
            for k in range(3)
        ]
    )
    go = jnp.transpose(go.reshape(2, 2, hr, own), (1, 3, 0, 2)).reshape(2, own, rows)
    tail = own - 2 * pair
    go = jnp.concatenate(
        [
            v
            for b in range(2)
            for core in range(2)
            for v in (
                go[core, b * pair : (b + 1) * pair],
                go[core, 2 * pair + b * (tail // 2) : 2 * pair + (b + 1) * (tail // 2)],
            )
        ],
        axis=0,
    )
    both = vo[0] + vo[1]
    plain = [scatter(part(both[i]), 0) for i in (GAIN1, SHIFT1, OUTB, GAIN2, SHIFT2, PROJB)]

    def unpack(k):
        return jnp.concatenate(
            [
                v
                for b in range(2)
                for core in range(2)
                for v in (
                    vo[core, QKVB + b, k * pair : (k + 1) * pair],
                    vo[core, QKVB + b, 3 * pair + k * HD : 3 * pair + (k + 1) * HD],
                )
            ]
        )

    gqb = scatter(part(jnp.stack([unpack(0), unpack(2)])), 1)
    gfb = scatter(part(jnp.concatenate([vo[2, 0], vo[3, 0], vo[2, 1], vo[3, 1]])), 0)
    return (
        bo,
        ig,
        plain[0],
        plain[1],
        scatter(gq, 1),
        gqb,
        scatter(go, 1),
        plain[2],
        plain[3],
        plain[4],
        scatter(gf, 0),
        gfb,
        scatter(gp.T, 1),
        plain[5],
    )


def solution(mesh):
    placed = (
        P(("dp", "tensor"), None),
        P("dp"),
        P(("dp", "tensor"), None),
        P("dp"),
        P("dp"),
        P(None, "dp", "tensor"),
        P(None, "dp"),
        P(None, "dp"),
        P("dp"),
        P("dp"),
        P("dp"),
        P("dp", "tensor"),
        P("dp"),
        P("tensor", "dp"),
        P("dp"),
    )
    return jax.shard_map(
        functools.partial(on_device, mesh.shape["dp"]),
        mesh=mesh,
        in_specs=placed,
        out_specs=(placed[0], placed[0]) + placed[3:],
        check_vma=False,
    )
```

```python
import functools
import math

import jax
import jax.numpy as jnp
from jax import lax
from jax.experimental import pallas as pl
from jax.experimental.pallas import tpu as pltpu
from jax.sharding import PartitionSpec as P

MESH = pl.DeviceIdType.MESH
LOW, FULL = jnp.bfloat16, jnp.float32
EPSILON = 1e-05
HD = 64
GROUPS, ZN, XN = 8, 4, 2
SEMS = 200
VEC = 16

GAIN1, SHIFT1, QKVB, OUTB, GAIN2, SHIFT2, PROJB, FCB = 0, 1, 2, 8, 9, 10, 11, 12


def dot(a, b):
    return jnp.dot(a, b, preferred_element_type=FULL)


def dot_nt(a, b):
    return lax.dot_general(a, b, (((1,), (1,)), ((), ())), preferred_element_type=FULL)


def dot_tn(a, b):
    return lax.dot_general(a, b, (((0,), (0,)), ((), ())), preferred_element_type=FULL)


def block_kernel(repeat, seq_len, *refs):
    (
        tok_h, prefix_s, cot_h, gain1_h, shift1_h, wq_h, qvb_h, wo_h, outb_h,
        gain2_h, shift2_h, wf_h, fcb_h, wp_h, projb_h,
        bo_h, ig_h, gq_ref, go_ref, gf_ref, gp_ref, vo_ref,
        Wq, Wo, Wf, Wp, Go, Gp,
        RqA1, RqB1, RqA2, RqB2, Rq3,
        RfA1, RfB1, RfA2, RfB2, Rf3,
        RpA1, RpB1, RpA2, RpB2, RpA3, RpB3,
        Ro1, Ro2, Ro3,
        TOK, COT, N1F, N2F, RS1, RS2, N1, N2, T0, T1,
        QP, KP, VP, CTX, DO, DQ, LSEC, LSER, DELR,
        MID, S0, V0, V1, H, GPR, PG,
        SV, SB, SC, SQ, SO, SF, SP, SW,
        VR, VF, VG, VZ, VO,
        ss, rs, ls,
    ) = refs
    half = seq_len // 2
    width = TOK.shape[1]
    rblk = 256
    nrb = seq_len // rblk
    dp = lax.axis_index("dp")
    t = lax.axis_index("tensor")
    s, sub = dp // repeat, dp % repeat
    z, x = s // XN, s % XN
    y, c = t // 2, t % 2
    oy, oc, ox = 1 - y, 1 - c, 1 - x

    def at(zz, xx, tt):
        return ((zz * XN + xx) * repeat + sub, tt)

    def zdev(k):
        return at((z + k) % ZN, x, t)

    xdev = at(z, ox, t)
    ydev = at(z, x, oy * 2 + c)
    cdev = at(z, x, y * 2 + oc)
    gdev = at(z, x, oy * 2 + oc)
    near = [xdev, ydev, cdev, gdev] + [at(z, ox, i * 2 + j) for i, j in ((y, oc), (oy, c), (oy, oc))]
    others = [(((s + k) % GROUPS) * repeat + sub, t) for k in range(1, GROUPS)]

    made = []

    def copy(src, dst, dev):
        k = len(made)

        def make():
            return pltpu.make_async_remote_copy(
                src_ref=src, dst_ref=dst, send_sem=ss.at[k], recv_sem=rs.at[k],
                device_id=dev, device_id_type=MESH,
            )

        made.append(make)
        return make

    def start(makes):
        for m in makes:
            m().start()

    def landed(makes):
        for m in makes:
            m().wait_recv()

    def sent(makes):
        for m in makes:
            m().wait_send()

    barrier = pltpu.get_barrier_semaphore()
    peers = others + [d for i, d in enumerate(near) if i != 0]
    for d in peers:
        pl.semaphore_signal(barrier, inc=1, device_id=d, device_id_type=MESH)

    brought = [
        (wq_h, SQ), (qvb_h, SB), (fcb_h, SC.at[0]),
        (gain1_h, SV.at[0]), (shift1_h, SV.at[1]), (outb_h, SV.at[2]),
        (gain2_h, SV.at[3]), (shift2_h, SV.at[4]), (projb_h, SV.at[5]),
        (wo_h, SO), (tok_h, TOK), (cot_h, COT.at[c]), (wf_h, SF), (wp_h, SP),
    ]
    local = [pltpu.make_async_copy(a, b, ls.at[i]) for i, (a, b) in enumerate(brought)]
    for cp in local:
        cp.start()

    lanes96 = SV.shape[1]
    VG[...] = jnp.zeros(VG.shape, FULL)
    for cp in local[1:9]:
        cp.wait()
    VG[0:6, :lanes96] = SV[0:6, :]
    VG[6:8, :lanes96] = SB[...]
    for j in range(4):
        VG[8 + j : 9 + j, :lanes96] = SC[:, j * lanes96 : (j + 1) * lanes96]
    VR[s] = VG[:, :128].astype(LOW)
    VG[...] = jnp.zeros(VG.shape, FULL)
    local[0].wait()
    q3 = SQ[...]
    Wq[y, z, x] = jnp.concatenate(
        [q3[0, :, :128], q3[1, :, :128], q3[2, :, :128]]
        + [q3[k, :, 128:] for k in range(3)]
        + [jnp.zeros((q3.shape[1], HD), FULL)],
        axis=1,
    ).astype(LOW)
    local[9].wait()
    turned = pltpu.roll(SO[...], (width - c * (width // 4)) % width, 1)
    last = jnp.concatenate([turned[:, 128:192], turned[:, 512:576]], axis=1)
    mine = jnp.concatenate([turned[:, 0:128], turned[:, 384:512], last], axis=1).astype(LOW)
    SW[0] = mine[: SW.shape[1]]
    SW[1] = mine[SW.shape[1] :]
    Wo[z, x, y] = SW[y]
    local[12].wait()
    Wf[y, z, x] = SF[...].astype(LOW)
    local[13].wait()
    Wp[y, z, x] = SP[...].astype(LOW)
    local[10].wait()
    local[11].wait()
    pl.semaphore_wait(barrier, len(peers))

    vec_c = [copy(VR.at[s], VR.at[s], d) for d in others]
    cot_c = [copy(COT.at[c], COT.at[c], cdev)]
    hr = wq_h.shape[1] // 2
    third = hr // 3
    pairs = (
        (pl.ds(0, third), pl.ds(third, third)),
        (pl.ds(2 * third, 2 * third), pl.ds(4 * third, 2 * third)),
    )

    def gather(W):
        steps = []
        for a, b in pairs:
            zs = [copy(W.at[y, z, x, r], W.at[y, z, x, r], zdev(k)) for k in range(1, ZN) for r in (a, b)]
            one = [
                copy(W.at[y, :, x, a], W.at[y, :, x, a], xdev),
                copy(W.at[y, :, x, b], W.at[y, :, x, b], ydev),
            ]
            two = [
                copy(W.at[y, :, :, a], W.at[y, :, :, a], ydev),
                copy(W.at[:, :, x, b], W.at[:, :, x, b], xdev),
            ]
            steps.append((zs, one, two))
        return steps

    def gather_wide(W):
        steps = []
        for a, b in pairs:
            near = [
                copy(W.at[y, z, x, a], W.at[y, z, x, a], xdev),
                copy(W.at[y, z, x, b], W.at[y, z, x, b], ydev),
            ]
            zs = [copy(W.at[y, z, :, a], W.at[y, z, :, a], zdev(k)) for k in range(1, ZN)]
            zs += [copy(W.at[:, z, x, b], W.at[:, z, x, b], zdev(k)) for k in range(1, ZN)]
            far = [
                copy(W.at[y, :, :, a], W.at[y, :, :, a], ydev),
                copy(W.at[:, :, x, b], W.at[:, :, x, b], xdev),
            ]
            steps.append((near, zs, far))
        return steps

    ow = [
        (
            [copy(Wo.at[z, x, y], Wo.at[z, x, y], zdev(k)) for k in range(1, ZN)],
            [copy(Wo.at[:, x, y], Wo.at[:, x, y], xdev)],
            [copy(Wo.at[:, :, y], Wo.at[:, :, y], ydev)],
        )
    ]
    qw, pw, fw = gather(Wq), gather_wide(Wp), gather(Wf)

    def z_go(w, i):
        start(w[i][0])

    def one_go(w, i):
        landed(w[i][0])
        start(w[i][1])

    def two_go(w, i):
        landed(w[i][1])
        start(w[i][2])

    def all_in(w):
        for step in w:
            landed(step[2])

    def sent_all(w):
        for step in w:
            for group in step:
                sent(group)

    start(vec_c)
    z_go(qw, 0)
    z_go(pw, 0)
    z_go(pw, 1)
    start(cot_c)

    def row_tile(i, n=128):
        return pl.ds(pl.multiple_of(i * n, n), n)

    @pl.loop(0, half // 128)
    def _(i):
        r = row_tile(i)
        v = TOK[r, :].astype(FULL)
        v = v - jnp.mean(v, axis=-1, keepdims=True)
        rstd = lax.rsqrt(jnp.mean(v * v, axis=-1, keepdims=True) + EPSILON)
        N1F[r, :] = v * rstd
        RS1[r, :] = jnp.broadcast_to(rstd, (128, 128))

    landed(vec_c)

    def widen(v):
        return jnp.concatenate([v, jnp.zeros((v.shape[0], width - v.shape[1]), FULL)], axis=1)

    pieces = [widen(VR[g].astype(FULL)) for g in range(GROUPS)]
    plain = pieces[0]
    for g in range(1, GROUPS):
        plain = plain + pltpu.roll(pieces[g], g * lanes96, 1)
    VF[GAIN1 : SHIFT1 + 1, :] = plain[0:2]
    VF[OUTB : PROJB + 1, :] = plain[2:6]
    place = lax.broadcasted_iota(jnp.int32, (1, width), 1)

    def lanes(v, first, last, shift):
        v = jnp.where((place >= first) & (place < last), v, 0.0)
        return pltpu.roll(v, shift % width, 1) if shift % width else v

    for b in range(2):
        a0, a1 = (widen(VR[2 * (2 * b + c) + i].astype(FULL)) for i in range(2))
        a1 = pltpu.roll(a1, lanes96, 1)
        qb, vb = a0[6:7] + a1[6:7], a0[7:8] + a1[7:8]
        VF[QKVB + b : QKVB + b + 1, :] = (
            lanes(qb, 0, 128, 0) + lanes(qb, 128, 192, 256) + lanes(vb, 0, 128, 256) + lanes(vb, 128, 192, 384)
        )
        a1 = pltpu.roll(a1, 3 * lanes96, 1)
        row = a0[8:9] + a1[8:9]
        for j in range(1, 4):
            row = row + pltpu.roll(a0[8 + j : 9 + j] + a1[8 + j : 9 + j], j * lanes96, 1)
        VF[FCB + b : FCB + b + 1, :] = row

    def vrow(i):
        return VF[i : i + 1, :]

    @pl.loop(0, half // 128)
    def _(i):
        r = row_tile(i)
        N1[c, r, :] = (N1F[r, :] * vrow(GAIN1) + vrow(SHIFT1)).astype(LOW)

    n1_c = [copy(N1.at[c], N1.at[c], cdev)]
    start(n1_c)
    landed(cot_c)

    def transpose_all(source, target):
        @pl.loop(0, nrb)
        def _(i):
            h, off = i // (half // rblk), i % (half // rblk)
            rows = pl.ds(pl.multiple_of(off * rblk, rblk), rblk)
            cols = pl.ds(pl.multiple_of(i * rblk, rblk), rblk)
            for k in range(width // rblk):
                target[k * rblk : (k + 1) * rblk, cols] = source[h, rows, k * rblk : (k + 1) * rblk].T

    one_go(qw, 0)
    z_go(qw, 1)
    transpose_all(COT, T0)
    two_go(qw, 0)
    z_go(fw, 0)
    one_go(qw, 1)
    z_go(fw, 1)
    z_go(ow, 0)
    landed(n1_c)
    two_go(qw, 1)
    one_go(pw, 0)
    one_go(fw, 0)
    all_in(qw)
    one_go(pw, 1)

    def low_lanes(v):
        return lax.broadcasted_iota(jnp.int32, v.shape, 1) < HD

    def tile(v, i):
        return v[:, i * 128 : (i + 1) * 128]

    def roll(v):
        return pltpu.roll(v, HD, 1)

    @pl.loop(0, nrb)
    def _(i):
        h, off = i // (half // rblk), i % (half // rblk)
        rows = pl.ds(pl.multiple_of(off * rblk, rblk), rblk)
        out = pl.ds(pl.multiple_of(i * rblk, rblk), rblk)
        n = N1[h, rows, :]
        got = []
        for b in range(2):
            got.append(dot(n, Wq[b].reshape(width, Wq.shape[-1])) + VF[QKVB + b : QKVB + b + 1, : Wq.shape[-1]])
            QP[b, out, :] = (tile(got[b], 0).astype(LOW).astype(FULL) * 0.125).astype(LOW)
            KP[b, out, :] = tile(got[b], 1).astype(LOW)
            VP[b, out, :] = tile(got[b], 2).astype(LOW)
        first = low_lanes(tile(got[0], 3))
        q = jnp.where(first, tile(got[0], 3), roll(tile(got[1], 3)))
        QP[2, out, :] = (q.astype(LOW).astype(FULL) * 0.125).astype(LOW)
        KP[2, out, :] = jnp.where(first, roll(tile(got[0], 3)), tile(got[1], 3)).astype(LOW)
        VP[2, out, :] = jnp.where(first, tile(got[0], 4), roll(tile(got[1], 4))).astype(LOW)

    prefix = prefix_s[y]
    LSEC[...] = jnp.zeros(LSEC.shape, FULL)

    def lane_part(v, e):
        lane = lax.broadcasted_iota(jnp.int32, v.shape, 1)
        keep = lane < HD if e == 0 else lane >= HD
        return jnp.where(keep, v, jnp.zeros_like(v))

    def meanwhile(p, b, plan):
        for (pp, bb), steps in plan.items():
            if bb == b:

                @pl.when(p == pp)
                def _(steps=steps):
                    for step in steps:
                        step()

    fetch = {
        (0, 0): [lambda: one_go(fw, 1), lambda: one_go(ow, 0)],
        (0, 1): [lambda: two_go(fw, 0)],
        (1, 1): [lambda: two_go(fw, 1), lambda: two_go(ow, 0)],
        (2, 1): [lambda: two_go(pw, 0)],
    }

    @pl.loop(0, 3)
    def _(p):
        for b in range(nrb):
            rows = pl.ds(b * rblk, rblk)
            cols = max(half, (b + 1) * rblk)
            q = QP[p, rows, :]
            keys, values = KP[p, :cols, :], VP[p, :cols, :]
            query = b * rblk + lax.broadcasted_iota(jnp.int32, (rblk, 1), 0)
            limit = jnp.maximum(prefix - 1, query)
            key = lax.broadcasted_iota(jnp.int32, (rblk, cols), 1)
            parts = []
            for e in range(2):
                sc = dot_nt(lane_part(q, e), keys)
                sc = jnp.where(key <= limit, sc, -1e30)
                peak = jnp.max(sc, axis=-1, keepdims=True)
                w = jnp.exp(sc - peak)
                total = jnp.sum(w, axis=-1, keepdims=True)
                parts.append(dot(w.astype(LOW), values) * (1.0 / total))
                lane = lax.broadcasted_iota(jnp.int32, (rblk, 128), 1)
                LSEC[rows, :] = jnp.where(lane == 2 * p + e, peak + jnp.log(total), LSEC[rows, :])
            CTX[p, rows, :] = jnp.where(low_lanes(parts[0]), parts[0], parts[1]).astype(LOW)
            meanwhile(p, b, fetch)

    for b in range(nrb):
        lt = LSEC[b * rblk : (b + 1) * rblk, :].T
        for h in range(6):
            LSER[h, :, b * rblk : (b + 1) * rblk] = lt[h : h + 1, :]
    all_in(ow)

    def wide(ref, rows):
        return jnp.concatenate([ref[0, rows, :], ref[1, rows, :], ref[2, rows, :]], axis=1)

    def split_rows(make_block, away, home, copies):
        per = half // rblk
        for which, target in ((oc, away), (c, home)):

            @pl.loop(0, per)
            def _(j):
                rows = pl.ds(pl.multiple_of(j * rblk, rblk), rblk)
                flat = pl.ds(pl.multiple_of((which * per + j) * rblk, rblk), rblk)
                target[rows, :] = make_block(which, rows, flat)

            if target is away:
                start(copies)

    po_c = [copy(S0, V0, cdev)]
    split_rows(
        lambda h, rows, flat: dot_nt(wide(CTX, flat), Wo[...].reshape(width, Wo.shape[-1])), S0, MID, po_c
    )
    two_go(pw, 1)
    landed(po_c)

    @pl.loop(0, half // 128)
    def _(i):
        r = row_tile(i)
        m = TOK[r, :].astype(FULL) + (MID[r, :] + V0[r, :] + vrow(OUTB))
        MID[r, :] = m
        v = m - jnp.mean(m, axis=-1, keepdims=True)
        rstd = lax.rsqrt(jnp.mean(v * v, axis=-1, keepdims=True) + EPSILON)
        n = v * rstd
        N2F[r, :] = n
        RS2[r, :] = jnp.broadcast_to(rstd, (128, 128))
        N2[c, r, :] = (n * vrow(GAIN2) + vrow(SHIFT2)).astype(LOW)

    n2_c = [copy(N2.at[c], N2.at[c], cdev)]
    start(n2_c)
    landed(n2_c)
    all_in(fw)

    root = math.sqrt(2.0 / math.pi)

    @pl.loop(0, nrb * 2)
    def _(k):
        b, i = k // nrb, k % nrb
        h, off = i // (half // rblk), i % (half // rblk)
        rows = pl.ds(pl.multiple_of(off * rblk, rblk), rblk)
        flat = pl.ds(pl.multiple_of(i * rblk, rblk), rblk)
        u = dot(N2[h, rows, :], Wf[b].reshape(width, width)) + VF[pl.ds(FCB + b, 1), :]
        uu = u * u
        th = jnp.tanh(root * u * (1.0 + 0.044715 * uu))
        H[b, flat, :] = (0.5 * u * (1.0 + th)).astype(LOW)
        GPR[b, flat, :] = 0.5 * (1.0 + th) + (0.5 * root) * u * (1.0 - th * th) * (1.0 + 0.134145 * uu)

    def weight_grad(left_t, right, G, first, last):
        @pl.loop(0, 4)
        def _(k):
            b, m = k // 2, k % 2
            rows = pl.ds(pl.multiple_of(m * (width // 2), width // 2), width // 2)
            g = dot(left_t[rows, :], right[b, :, first:last])
            g = g.astype(LOW).reshape(ZN // 2, XN, width // GROUPS, last - first)
            G[b, pl.ds(m * (ZN // 2), ZN // 2), :, :, first:last] = g

    every = pl.ds(0, width)
    by_rows = [pairs[0] + (pl.ds(0, third), every), pairs[1] + (pl.ds(third, 2 * third), every)]

    def reduce_copies(G, plan, A1, B1, A2, B2, R3):
        steps = []
        for a, b, r, cols in plan:
            one = [
                copy(G.at[:, :, ox, a, cols], A1.at[:, :, r, cols], xdev),
                copy(G.at[oy, :, :, b, cols], B1.at[:, :, r, cols], ydev),
            ]
            two = [
                copy(G.at[oy, :, x, a, cols], A2.at[:, r, cols], ydev),
                copy(G.at[y, :, ox, b, cols], B2.at[:, r, cols], xdev),
            ]
            three = [
                copy(G.at[y, (z + k) % ZN, x, q, cols], R3.at[k - 1, q, cols], zdev(k))
                for k in range(1, ZN)
                for q in (a, b)
            ]
            steps.append((a, b, r, cols, one, two, three))

        def add(target, source):
            target[...] = (target[...].astype(FULL) + source[...].astype(FULL)).astype(LOW)

        def go(i):
            start(steps[i][4])

        def second(i):
            a, b, r, cols, one, two, three = steps[i]
            landed(one[:1])

            @pl.loop(0, ZN)
            def _(k):
                add(G.at[oy, k, x, a, cols], A1.at[oy, k, r, cols])

            start(two[:1])
            landed(one[1:])

            @pl.loop(0, ZN)
            def _(k):
                add(G.at[y, k, ox, b, cols], B1.at[k, ox, r, cols])

            start(two[1:])

            @pl.loop(0, ZN)
            def _(k):
                add(G.at[y, k, x, a, cols], A1.at[y, k, r, cols])
                add(G.at[y, k, x, b, cols], B1.at[k, x, r, cols])

        def third_step(i):
            a, b, r, cols, one, two, three = steps[i]
            landed(two)

            @pl.loop(0, ZN)
            def _(k):
                add(G.at[y, k, x, a, cols], A2.at[k, r, cols])
                add(G.at[y, k, x, b, cols], B2.at[k, r, cols])

            start(three)

        def last(i, out):
            a, b, r, cols, one, two, three = steps[i]
            landed(three)
            for q in (a, b):
                v = G[y, z, x, q, cols].astype(FULL)
                for k in range(ZN - 1):
                    v = v + R3[k, q, cols].astype(FULL)
                out[q, cols] = v

        return go, second, third_step, last

    def reduce_wide(G, plan, A1, B1, A2, B2, A3, B3):
        steps = []
        for a, b, r, cols in plan:
            one = [
                copy(G.at[oy, :, :, a, cols], A1.at[:, :, r, cols], ydev),
                copy(G.at[:, :, ox, b, cols], B1.at[:, :, r, cols], xdev),
            ]
            two = [copy(G.at[y, (z + k) % ZN, :, a, cols], A2.at[k - 1, :, r, cols], zdev(k)) for k in range(1, ZN)]
            two += [copy(G.at[:, (z + k) % ZN, x, b, cols], B2.at[k - 1, :, r, cols], zdev(k)) for k in range(1, ZN)]
            three = [
                copy(G.at[y, z, ox, a, cols], A3.at[r, cols], xdev),
                copy(G.at[oy, z, x, b, cols], B3.at[r, cols], ydev),
            ]
            steps.append((a, b, r, cols, one, two, three))

        def add(target, sources):
            v = target[...].astype(FULL)
            for source in sources:
                v = v + source[...].astype(FULL)
            target[...] = v.astype(LOW)

        def go(i):
            start(steps[i][4])

        def second(i):
            a, b, r, cols, one, two, three = steps[i]
            landed(one)

            @pl.loop(0, ZN)
            def _(k):
                for j in range(2):
                    add(G.at[y, k, j, a, cols], [A1.at[k, j, r, cols]])
                    add(G.at[j, k, x, b, cols], [B1.at[j, k, r, cols]])

            start(two)

        def third_step(i):
            a, b, r, cols, one, two, three = steps[i]
            landed(two)
            for j in range(2):
                add(G.at[y, z, j, a, cols], [A2.at[k, j, r, cols] for k in range(ZN - 1)])
                add(G.at[j, z, x, b, cols], [B2.at[k, j, r, cols] for k in range(ZN - 1)])
            start(three)

        def last(i, out):
            a, b, r, cols, one, two, three = steps[i]
            landed(three)
            for q, R in ((a, A3), (b, B3)):
                out[q, cols] = G[y, z, x, q, cols].astype(FULL) + R[r, cols].astype(FULL)

        return go, second, third_step, last

    rp = reduce_wide(Gp, by_rows, RpA1, RpB1, RpA2, RpB2, RpA3, RpB3)
    weight_grad(T0, H, Gp, 0, width)
    transpose_all(N2, T1)
    all_in(pw)
    rp[0](0)
    rp[0](1)

    @pl.loop(0, nrb * 2)
    def _(k):
        b, i = k // nrb, k % nrb
        h, off = i // (half // rblk), i % (half // rblk)
        rows = pl.ds(pl.multiple_of(off * rblk, rblk), rblk)
        flat = pl.ds(pl.multiple_of(i * rblk, rblk), rblk)
        g = (dot(COT[h, rows, :], Wp[b].reshape(width, width)) * GPR[b, flat, :]).astype(LOW)
        PG[b, flat, :] = g
        VG[pl.ds(FCB + b, 1), :] += jnp.sum(g.astype(FULL), axis=0, keepdims=True)

    p2_c = [copy(S0, V1, cdev)]
    home2, homem, home1 = GPR.at[0, pl.ds(0, half)], GPR.at[0, pl.ds(half, half)], GPR.at[1, pl.ds(0, half)]
    awaym = GPR.at[1, pl.ds(half, half)]

    def pair_nt(A, W, columns):
        def block(h, rows, flat):
            return dot_nt(A[0, flat, :columns], W[0].reshape(width, W.shape[-1])) + dot_nt(
                A[1, flat, :columns], W[1].reshape(width, W.shape[-1])
            )

        return block

    sent(po_c)
    split_rows(pair_nt(PG, Wf, width), S0, home2, p2_c)
    pm_c = [copy(awaym, V0, cdev)]
    split_rows(pair_nt(H, Wp, width), awaym, homem, pm_c)
    sent_all(pw)
    rp[1](0)
    weight_grad(T1, PG, Wp, 0, width)
    rf = reduce_copies(Wp, by_rows, RfA1, RfB1, RfA2, RfB2, Rf3)
    rf[0](0)
    rf[0](1)
    landed(p2_c)

    sent(n2_c)

    def norm_back(dy, n, rstd, gain):
        e = dy * gain
        return (e - jnp.mean(e, axis=-1, keepdims=True) - n * jnp.mean(e * n, axis=-1, keepdims=True)) * rstd

    def add_row(i, v):
        VG[i : i + 1, :] += jnp.sum(v, axis=0, keepdims=True)

    @pl.loop(0, half // 128)
    def _(i):
        r = row_tile(i)
        dy = GPR[0, r, :] + V1[r, :]
        n = N2F[r, :]
        add_row(GAIN2, dy * n)
        add_row(SHIFT2, dy)
        cot = COT[c, r, :].astype(FULL)
        add_row(PROJB, cot)
        g = cot + norm_back(dy, n, RS2[r, 0:1], vrow(GAIN2))
        N2F[r, :] = g
        low = g.astype(LOW)
        add_row(OUTB, low.astype(FULL))
        N2[c, r, :] = low

    ag_c = [copy(N2.at[c], N2.at[c], cdev)]
    start(ag_c)

    def vector_copies(first, last):
        r = pl.ds(first, last - first)
        over_z = [copy(VG.at[r], VZ.at[k - 1, r], zdev(k)) for k in range(1, ZN)]
        mine = VO.at[y * 2 + x, c, r]
        return r, over_z, mine, [copy(mine, mine, d) for d in near]

    def vector_second(v):
        r, over_z, mine, over_near = v
        landed(over_z)
        mine[...] = VG[r, :] + VZ[0, r, :] + VZ[1, r, :] + VZ[2, r, :]
        start(over_near)

    def vector_last(v):
        r, over_z, mine, over_near = v
        landed(over_near)
        for core in range(2):
            vo_ref[core, r, :] = VO[0, core, r, :] + VO[1, core, r, :] + VO[2, core, r, :] + VO[3, core, r, :]

    late, early = vector_copies(0, 8), vector_copies(8, VEC)
    start(early[1])
    transpose_all(N1, T1)
    rp[1](1)
    landed(pm_c)

    @pl.loop(0, half // 128)
    def _(i):
        r = row_tile(i)
        far = row_tile(i + half // 128)
        TOK[r, :] = (MID[r, :] + (GPR[0, far, :] + V0[r, :] + vrow(PROJB))).astype(LOW)

    out_c = [pltpu.make_async_copy(TOK, bo_h, ls.at[0]), pltpu.make_async_copy(N1.at[c], ig_h, ls.at[1])]
    out_c[0].start()
    landed(ag_c)

    @pl.loop(0, nrb)
    def _(i):
        h, off = i // (half // rblk), i % (half // rblk)
        rows = pl.ds(pl.multiple_of(off * rblk, rblk), rblk)
        flat = pl.ds(pl.multiple_of(i * rblk, rblk), rblk)
        g = dot(N2[h, rows, :], Wo[...].reshape(width, Wo.shape[-1])).astype(LOW)
        row = lax.broadcasted_iota(jnp.int32, (8, 128), 0)
        lane = lax.broadcasted_iota(jnp.int32, (8, 128), 1)
        pick = jnp.where(lane // HD == row, 1.0, 0.0).astype(LOW)
        for p in range(3):
            gp = tile(g, p)
            DO[p, flat, :] = gp
            prod = gp.astype(FULL) * CTX[p, flat, :].astype(FULL)
            high = prod.astype(LOW)
            rest = (prod - high.astype(FULL)).astype(LOW)
            d = dot_nt(pick, high) + dot_nt(pick, rest)
            for e in range(2):
                DELR[2 * p + e, :, flat] = d[e : e + 1, :]

    transpose_all(N2, T0)

    @pl.loop(0, 2)
    def _(m):
        rows = pl.ds(pl.multiple_of(m * (width // 2), width // 2), width // 2)
        g = dot(T0[rows, :], wide(CTX, pl.ds(0, seq_len)))
        g = g.astype(LOW).reshape(ZN // 2, XN, 2, width // (2 * GROUPS), Wo.shape[-1])
        Go[pl.ds(m * (ZN // 2), ZN // 2)] = g

    ro = [
        [copy(Go.at[:, :, oy], Ro1, ydev)],
        [copy(Go.at[:, ox, y], Ro2, xdev)],
        [copy(Go.at[(z + k) % ZN, x, y], Ro3.at[k - 1], zdev(k)) for k in range(1, ZN)],
        [copy(go_ref.at[t], go_ref.at[t], d) for d in (cdev, ydev, gdev)],
    ]
    start(ro[0])

    def ro_second():
        landed(ro[0])

        @pl.loop(0, ZN)
        def _(k):
            for i in range(XN):
                Go[k, i, y] = (Go[k, i, y].astype(FULL) + Ro1[k, i].astype(FULL)).astype(LOW)

        start(ro[1])

    def ro_third():
        landed(ro[1])

        @pl.loop(0, ZN)
        def _(k):
            Go[k, x, y] = (Go[k, x, y].astype(FULL) + Ro2[k].astype(FULL)).astype(LOW)

        start(ro[2])

    def ro_last():
        landed(ro[2])
        v = Go[z, x, y].astype(FULL)
        for k in range(ZN - 1):
            v = v + Ro3[k].astype(FULL)
        go_ref[t] = v
        start(ro[3])

    def attention_back(p, plan):
        DQ[...] = jnp.zeros(DQ.shape, FULL)
        for b in range(nrb):
            rows = pl.ds(b * rblk, rblk)
            first = 0 if b * rblk < half else b * rblk
            n = seq_len - first
            keys, values = KP[p, rows, :], VP[p, rows, :]
            queries, grads = QP[p, first:, :], DO[p, first:, :]
            key = b * rblk + lax.broadcasted_iota(jnp.int32, (rblk, 1), 0)
            limit = jnp.where(key < prefix, 0, key)
            query = first + lax.broadcasted_iota(jnp.int32, (rblk, n), 1)
            dk, dv = [], []
            for e in range(2):
                ke, ve = lane_part(keys, e), lane_part(values, e)
                sc = dot_nt(ke, queries) - LSER[2 * p + e, :, first:]
                w = jnp.exp(jnp.where(query >= limit, sc, -1e30))
                dw = dot_nt(ve, grads) - DELR[2 * p + e, :, first:]
                ds = (w * dw).astype(LOW)
                dv.append(dot(w.astype(LOW), grads))
                dk.append(dot(ds, queries))
                DQ[first:, :] += dot_tn(ds, ke)
            KP[p, rows, :] = jnp.where(low_lanes(dk[0]), dk[0], dk[1]).astype(LOW)
            VP[p, rows, :] = jnp.where(low_lanes(dv[0]), dv[0], dv[1]).astype(LOW)
            meanwhile(p, b, plan)
        QP[p, :, :] = (DQ[...] * 0.125).astype(LOW)

    away = {
        (0, 3): [lambda: rf[1](0), ro_second],
        (1, 2): [lambda: rf[1](1), ro_third],
        (2, 0): [lambda: rp[2](0)],
        (2, 1): [lambda: rf[2](0)],
        (2, 3): [lambda: rf[2](1)],
    }

    @pl.loop(0, 2)
    def _(p):
        attention_back(p, away)

    packed = Wq.shape[-1]
    sent_all(fw)

    @pl.loop(0, nrb)
    def _(i):
        flat = pl.ds(pl.multiple_of(i * rblk, rblk), rblk)
        for b in range(2):
            for k, ref in enumerate((QP, KP, VP)):
                g = ref[b, flat, :]
                H[b, flat, k * 128 : (k + 1) * 128] = g
                VG[QKVB + b : QKVB + b + 1, k * 128 : (k + 1) * 128] += jnp.sum(g.astype(FULL), axis=0, keepdims=True)

    both = (pl.ds(0, hr), pl.ds(hr, hr), pl.ds(0, hr))
    by_lanes = [both + (pl.ds(0, 384),), both + (pl.ds(384, packed - 384),)]
    weight_grad(T1, H, Wf, 0, 384)
    rq = reduce_copies(Wf, by_lanes, RqA1, RqB1, RqA2, RqB2, Rq3)
    rq[0](0)
    attention_back(2, away)

    @pl.loop(0, nrb)
    def _(i):
        flat = pl.ds(pl.multiple_of(i * rblk, rblk), rblk)
        q, k, v = (ref[2, flat, :].astype(FULL) for ref in (QP, KP, VP))
        first = low_lanes(q)
        packs = (
            (jnp.where(first, q, roll(k)), jnp.where(first, v, 0.0)),
            (jnp.where(first, roll(q), k), jnp.where(first, roll(v), 0.0)),
        )
        for b in range(2):
            for j in range(2):
                at_j = slice(384 + 128 * j, 512 + 128 * j)
                H[b, flat, at_j] = packs[b][j].astype(LOW)
                VG[QKVB + b : QKVB + b + 1, at_j] += jnp.sum(packs[b][j], axis=0, keepdims=True)

    weight_grad(T1, H, Wf, 384, packed)
    rq[0](1)

    p1_c = [copy(S0, V1, cdev)]
    sent(p2_c)
    split_rows(pair_nt(H, Wq, packed), S0, home1, p1_c)
    rq[1](0)
    rp[2](1)
    vector_second(early)
    landed(p1_c)

    sent(n1_c)

    @pl.loop(0, half // 128)
    def _(i):
        r = row_tile(i)
        dy = GPR[1, r, :] + V1[r, :]
        n = N1F[r, :]
        add_row(GAIN1, dy * n)
        add_row(SHIFT1, dy)
        N1[c, r, :] = (N2F[r, :] + norm_back(dy, n, RS1[r, 0:1], vrow(GAIN1))).astype(LOW)

    out_c[1].start()

    start(late[1])
    rq[1](1)
    rq[2](0)
    ro_last()
    vector_second(late)
    rp[3](0, gp_ref)
    rp[3](1, gp_ref)
    rq[2](1)
    rf[3](0, gf_ref)
    rf[3](1, gf_ref)
    vector_last(early)
    landed(ro[3])
    rq[3](0, gq_ref)
    vector_last(late)
    rq[3](1, gq_ref)

    waited = {id(m) for m in po_c + n2_c + p2_c + n1_c}
    for w in (pw, fw):
        for step in w:
            for group in step:
                waited |= {id(m) for m in group}
    sent([m for m in made if id(m) not in waited])
    for cp in out_c:
        cp.wait()


def gather_groups(v, axis, repeat, groups):
    if repeat == 1:
        return v
    return lax.all_gather(v, "dp", axis=axis, axis_index_groups=groups, tiled=True)


def scatter_groups(v, axis, repeat, groups):
    if repeat == 1:
        return v
    return lax.psum_scatter(v, "dp", scatter_dimension=axis, axis_index_groups=groups, tiled=True)


def on_device(
    dp_size,
    tokens,
    prefix,
    cotangent,
    first_gain,
    first_shift,
    qkv_weight,
    qv_bias,
    out_weight,
    out_bias,
    second_gain,
    second_shift,
    fc_weight,
    fc_bias,
    proj_weight,
    proj_bias,
):
    repeat = dp_size // GROUPS
    groups = [[g * repeat + i for i in range(repeat)] for g in range(GROUPS)]
    half, width = tokens.shape
    seq_len = 2 * half

    def whole(v, axis):
        return gather_groups(v.astype(LOW), axis, repeat, groups).astype(FULL) if repeat > 1 else v

    params = [
        whole(first_gain, 0), whole(first_shift, 0), whole(qkv_weight, 1), whole(qv_bias, 1), whole(out_weight, 1),
        whole(out_bias, 0), whole(second_gain, 0), whole(second_shift, 0), whole(fc_weight, 0), whole(fc_bias, 0),
        whole(proj_weight, 1), whole(proj_bias, 0),
    ]
    params[4], params[10] = params[4].T, params[10].T
    rows = params[8].shape[0]
    cols = params[2].shape[2]
    units = params[8].shape[1]
    pair = 2 * HD
    packed, own = 3 * cols + HD, 2 * cols
    hr = rows // 2
    ANY = pl.BlockSpec(memory_space=pl.ANY)
    IN_VMEM = pl.BlockSpec(memory_space=pltpu.VMEM)

    def reduce_space(lanes):
        return [
            pltpu.VMEM((2, ZN, hr, lanes), LOW),
            pltpu.VMEM((ZN, XN, hr, lanes), LOW),
            pltpu.VMEM((ZN, hr, lanes), LOW),
            pltpu.VMEM((ZN, hr, lanes), LOW),
            pltpu.VMEM((ZN - 1, rows, lanes), LOW),
        ]

    token_low = pltpu.VMEM((2, half, width), LOW)
    token_full = pltpu.VMEM((half, width), FULL)
    unit_low = pltpu.VMEM((2, seq_len, width), LOW)
    heads = pltpu.VMEM((3, seq_len, pair), LOW)
    scratch = (
        [
            pltpu.VMEM((2, ZN, XN, rows, packed), LOW),
            pltpu.VMEM((ZN, XN, 2, hr, own), LOW),
            pltpu.VMEM((2, ZN, XN, rows, width), LOW),
            pltpu.VMEM((2, ZN, XN, rows, width), LOW),
            pltpu.VMEM((ZN, XN, 2, hr, own), LOW),
            pltpu.VMEM((2, ZN, XN, rows, width), LOW),
        ]
        + reduce_space(packed)
        + reduce_space(width)
        + [
            pltpu.VMEM((ZN, XN, hr, width), LOW),
            pltpu.VMEM((2, ZN, hr, width), LOW),
            pltpu.VMEM((ZN - 1, XN, hr, width), LOW),
            pltpu.VMEM((ZN - 1, 2, hr, width), LOW),
            pltpu.VMEM((hr, width), LOW),
            pltpu.VMEM((hr, width), LOW),
        ]
        + [
            pltpu.VMEM((ZN, XN, hr, own), LOW),
            pltpu.VMEM((ZN, hr, own), LOW),
            pltpu.VMEM((ZN - 1, hr, own), LOW),
        ]
        + [
            pltpu.VMEM((half, width), LOW),
            token_low,
            token_full,
            token_full,
            pltpu.VMEM((half, 128), FULL),
            pltpu.VMEM((half, 128), FULL),
            token_low,
            token_low,
            pltpu.VMEM((width, seq_len), LOW),
            pltpu.VMEM((width, seq_len), LOW),
        ]
        + [heads] * 5
        + [
            pltpu.VMEM((seq_len, pair), FULL),
            pltpu.VMEM((seq_len, 128), FULL),
            pltpu.VMEM((6, 1, seq_len), FULL),
            pltpu.VMEM((6, 1, seq_len), FULL),
        ]
        + [token_full] * 4
        + [unit_low, pltpu.VMEM((2, seq_len, width), FULL), unit_low]
        + [
            pltpu.VMEM((8, rows), FULL),
            pltpu.VMEM((2, rows), FULL),
            pltpu.VMEM((1, 4 * rows), FULL),
            pltpu.VMEM((3, rows, cols), FULL),
            pltpu.VMEM((rows, width), FULL),
            pltpu.VMEM((rows, units), FULL),
            pltpu.VMEM((rows, units), FULL),
            pltpu.VMEM((2, hr, own), LOW),
            pltpu.VMEM((GROUPS, VEC, 128), LOW),
            pltpu.VMEM((VEC, width), FULL),
            pltpu.VMEM((VEC, width), FULL),
            pltpu.VMEM((ZN - 1, VEC, width), FULL),
        ]
        + [pltpu.VMEM((4, 2, VEC, width), FULL)]
        + [
            pltpu.SemaphoreType.DMA((SEMS,)),
            pltpu.SemaphoreType.DMA((SEMS,)),
            pltpu.SemaphoreType.DMA((16,)),
        ]
    )
    out_shape = [
        jax.ShapeDtypeStruct((half, width), LOW),
        jax.ShapeDtypeStruct((half, width), LOW),
        jax.ShapeDtypeStruct((rows, packed), FULL),
        jax.ShapeDtypeStruct((4, hr, own), FULL),
        jax.ShapeDtypeStruct((rows, width), FULL),
        jax.ShapeDtypeStruct((rows, width), FULL),
        jax.ShapeDtypeStruct((2, VEC, width), FULL),
    ]
    grown = pl.pallas_call(
        functools.partial(block_kernel, repeat, seq_len),
        out_shape=out_shape,
        in_specs=[ANY, pl.BlockSpec(memory_space=pltpu.SMEM)] + [ANY] * 13,
        out_specs=[ANY] * 2 + [IN_VMEM] * 5,
        scratch_shapes=scratch,
        compiler_params=pltpu.CompilerParams(
            collective_id=0, has_side_effects=True, vmem_limit_bytes=62 * 1024 * 1024
        ),
    )(tokens, prefix, cotangent, *params)

    vector = jax.ShapeDtypeStruct((rows,), FULL)
    small = (2, 3, 5, 7, 8, 9, 11, 13)
    results = pl.pallas_call(
        functools.partial(unpack_kernel, repeat),
        out_shape=[
            out_shape[0],
            out_shape[1],
            vector,
            vector,
            jax.ShapeDtypeStruct((3, rows, cols), FULL),
            jax.ShapeDtypeStruct((2, rows), FULL),
            jax.ShapeDtypeStruct((rows, width), FULL),
            vector,
            vector,
            vector,
            jax.ShapeDtypeStruct((rows, units), FULL),
            jax.ShapeDtypeStruct((4 * rows,), FULL),
            jax.ShapeDtypeStruct((rows, units), FULL),
            vector,
        ],
        in_specs=[ANY] * 7,
        out_specs=[IN_VMEM if i in small else ANY for i in range(14)],
        scratch_shapes=[
            pltpu.VMEM((rows, packed), FULL),
            pltpu.VMEM((4, hr, own), FULL),
            pltpu.VMEM((2, VEC, width), FULL),
            pltpu.VMEM((3, rows, cols), FULL),
            pltpu.VMEM((rows, width), FULL),
            pltpu.VMEM((half, width), LOW),
            pltpu.VMEM((half, width), LOW),
            pltpu.VMEM((rows, units), FULL),
            pltpu.VMEM((rows, units), FULL),
            pltpu.SemaphoreType.DMA((13,)),
        ],
        compiler_params=pltpu.CompilerParams(vmem_limit_bytes=62 * 1024 * 1024),
    )(*grown)
    results = [v.T if i in (6, 12) else v for i, v in enumerate(results)]
    along = (None, None, 0, 0, 1, 1, 1, 0, 0, 0, 0, 0, 1, 0)
    return tuple(
        v if repeat == 1 or axis is None else scatter_groups(v, axis, repeat, groups)
        for v, axis in zip(results, along, strict=True)
    )


def unpack_kernel(
    repeat, bo, ig, gq_h, go_h, gf, gp, vo_h,
    bo_out, ig_out, gain1, shift1, wq_h, qvb, wo_h, outb, gain2, shift2, wf, fcb, wp, projb,
    gq, go, vo, wq, wo, b1, b2, w1, w2, sems,
):
    moves = [(vo_h, vo), (gq_h, gq), (go_h, go), (ig, b2), (bo, b1), (gf, w1), (gp, w2)]
    moves += [(wq, wq_h), (wo, wo_h), (b2, ig_out), (b1, bo_out), (w1, wf), (w2, wp)]
    moves = [pltpu.make_async_copy(a, b, sems.at[i]) for i, (a, b) in enumerate(moves)]
    for cp in moves[:7]:
        cp.start()
    for i in range(3, 7):
        moves[i].wait()
        moves[i + 6].start()
    moves[1].wait()
    for k in range(3):
        wq[k] = jnp.concatenate(
            [gq[:, k * 128 : (k + 1) * 128], gq[:, 384 + k * HD : 384 + (k + 1) * HD]], axis=1
        )
    moves[7].start()
    moves[2].wait()
    m = [jnp.concatenate([go[core], go[2 + core]], axis=0) for core in range(2)]
    wo[...] = jnp.concatenate(
        [
            v
            for b in range(2)
            for core in range(2)
            for v in (m[core][:, b * 128 : (b + 1) * 128], m[core][:, 256 + b * HD : 256 + (b + 1) * HD])
        ],
        axis=1,
    )
    moves[8].start()
    moves[0].wait()
    s = lax.axis_index("dp") // repeat
    width = vo.shape[2]
    n = gain1.shape[0]
    both = pltpu.roll(vo[0] + vo[1], (GROUPS - s) % GROUPS * n, 1)
    for i, out in ((GAIN1, gain1), (SHIFT1, shift1), (OUTB, outb), (GAIN2, gain2), (SHIFT2, shift2), (PROJB, projb)):
        out[...] = both[i, :n]
    owner = s // 2
    core, b, odd = owner % 2, owner // 2, s % 2
    place = lax.broadcasted_iota(jnp.int32, (1, width), 1)

    def lanes(v, first, last, shift):
        v = jnp.where((place >= first) & (place < last), v, 0.0)
        return pltpu.roll(v, shift % width, 1) if shift % width else v

    row = vo[core, pl.ds(QKVB + b, 1), :]
    q = lanes(row, 0, 128, 0) + lanes(row, 384, 448, -256)
    v = lanes(row, 256, 384, -256) + lanes(row, 512, 576, -384)
    back = (width - odd * n) % width
    qvb[0:1, :] = pltpu.roll(q, back, 1)[:, :n]
    qvb[1:2, :] = pltpu.roll(v, back, 1)[:, :n]
    row = vo[core, pl.ds(FCB + b, 1), :]
    fcb[...] = pltpu.roll(row, odd * (width // 2), 1)[0, : width // 2]
    for i in range(7, 13):
        moves[i].wait()


def solution(mesh):
    placed = (
        P(("dp", "tensor"), None),
        P("dp"),
        P(("dp", "tensor"), None),
        P("dp"),
        P("dp"),
        P(None, "dp", "tensor"),
        P(None, "dp"),
        P(None, "dp"),
        P("dp"),
        P("dp"),
        P("dp"),
        P("dp", "tensor"),
        P("dp"),
        P("tensor", "dp"),
        P("dp"),
    )
    return jax.shard_map(
        functools.partial(on_device, mesh.shape["dp"]),
        mesh=mesh,
        in_specs=placed,
        out_specs=(placed[0], placed[0]) + placed[3:],
        check_vma=False,
    )
```

```python
import functools
import math

import jax
import jax.numpy as jnp
from jax import lax
from jax.experimental import pallas as pl
from jax.experimental.pallas import tpu as pltpu
from jax.sharding import PartitionSpec as P

MESH = pl.DeviceIdType.MESH
LOW, FULL = jnp.bfloat16, jnp.float32
EPSILON = 1e-05
HD = 64
GROUPS, ZN, XN = 8, 4, 2
SEMS = 224
VEC = 16

GAIN1, SHIFT1, QKVB, OUTB, GAIN2, SHIFT2, PROJB, FCB = 0, 1, 2, 8, 9, 10, 11, 12


def dot(a, b):
    return jnp.dot(a, b, preferred_element_type=FULL)


def dot_nt(a, b):
    return lax.dot_general(a, b, (((1,), (1,)), ((), ())), preferred_element_type=FULL)


def dot_tn(a, b):
    return lax.dot_general(a, b, (((0,), (0,)), ((), ())), preferred_element_type=FULL)


def block_kernel(repeat, seq_len, *refs):
    (
        tok_h, prefix_s, cot_h, gain1_h, shift1_h, wq_h, qvb_h, wo_h, outb_h,
        gain2_h, shift2_h, wf_h, fcb_h, wp_h, projb_h,
        bo_h, ig_h, gq_ref, go_ref, gf_h, gp_h, vo_ref,
        Wq, Wo, Wf, Wp, Go, Gp, Gf,
        RqA1, RqB1, RqA2, RqB2, Rq3,
        RfA1, RfB1, RfA2, RfB2, Rf3,
        RpA1, RpB1, RpA2, RpB2, RpA3, RpB3,
        Ro1, Ro2, Ro3,
        TOK, COT, N1F, N2F, RS, N1, N2, T0, T1,
        QP, KP, VP, CTX, DO, DQ, LSER, DELR,
        MID, V0, V1, H, GPR, PG,
        SV, SB, SC, SQ, SW, CTXP, WOP,
        VR, VF, VG, VZ, VO,
        ss, rs, ls,
    ) = refs
    half = seq_len // 2
    width = TOK.shape[1]
    rblk = 256
    nrb = seq_len // rblk
    dp = lax.axis_index("dp")
    t = lax.axis_index("tensor")
    s, sub = dp // repeat, dp % repeat
    z, x = s // XN, s % XN
    y, c = t // 2, t % 2
    oy, oc, ox = 1 - y, 1 - c, 1 - x

    def at(zz, xx, tt):
        return ((zz * XN + xx) * repeat + sub, tt)

    def zdev(k):
        return at((z + k) % ZN, x, t)

    xdev = at(z, ox, t)
    ydev = at(z, x, oy * 2 + c)
    cdev = at(z, x, y * 2 + oc)
    gdev = at(z, x, oy * 2 + oc)
    near = [xdev, ydev, cdev, gdev] + [at(z, ox, i * 2 + j) for i, j in ((y, oc), (oy, c), (oy, oc))]
    others = [(((s + k) % GROUPS) * repeat + sub, t) for k in range(1, GROUPS)]

    made = []

    def copy(src, dst, dev):
        k = len(made)

        def make():
            return pltpu.make_async_remote_copy(
                src_ref=src, dst_ref=dst, send_sem=ss.at[k], recv_sem=rs.at[k],
                device_id=dev, device_id_type=MESH,
            )

        made.append(make)
        return make

    def start(makes):
        for m in makes:
            m().start()

    def landed(makes):
        for m in makes:
            m().wait_recv()

    def sent(makes):
        for m in makes:
            m().wait_send()

    barrier = pltpu.get_barrier_semaphore()
    peers = others + [d for i, d in enumerate(near) if i != 0]
    for d in peers:
        pl.semaphore_signal(barrier, inc=1, device_id=d, device_id_type=MESH)

    SO, SF, SP = (GPR.at[0, pl.ds(i * wo_h.shape[0], wo_h.shape[0])] for i in range(3))
    brought = [
        (wq_h, SQ), (qvb_h, SB), (fcb_h, SC.at[0]),
        (gain1_h, SV.at[0]), (shift1_h, SV.at[1]), (outb_h, SV.at[2]),
        (gain2_h, SV.at[3]), (shift2_h, SV.at[4]), (projb_h, SV.at[5]),
        (wo_h, SO), (tok_h, TOK), (cot_h, COT.at[c]), (wf_h, SF), (wp_h, SP),
    ]
    local = [pltpu.make_async_copy(a, b, ls.at[i]) for i, (a, b) in enumerate(brought)]
    for cp in local:
        cp.start()

    lanes96 = SV.shape[1]
    VG[...] = jnp.zeros(VG.shape, FULL)
    for cp in local[1:9]:
        cp.wait()
    VG[0:6, :lanes96] = SV[0:6, :]
    VG[6:8, :lanes96] = SB[...]
    for j in range(4):
        VG[8 + j : 9 + j, :lanes96] = SC[:, j * lanes96 : (j + 1) * lanes96]
    VR[s] = VG[:, :128].astype(LOW)
    VG[...] = jnp.zeros(VG.shape, FULL)
    local[0].wait()
    q3 = SQ[...]
    Wq[y, z, x] = jnp.concatenate(
        [q3[0, :, :128], q3[1, :, :128], q3[2, :, :128]]
        + [q3[k, :, 128:] for k in range(3)]
        + [jnp.zeros((q3.shape[1], HD), FULL)],
        axis=1,
    ).astype(LOW)
    local[9].wait()
    turned = pltpu.roll(SO[...], (width - c * (width // 4)) % width, 1)
    last = jnp.concatenate([turned[:, 128:192], turned[:, 512:576]], axis=1)
    mine = jnp.concatenate([turned[:, 0:128], turned[:, 384:512], last], axis=1).astype(LOW)
    SW[0] = mine[: SW.shape[1]]
    SW[1] = mine[SW.shape[1] :]
    Wo[z, x, y] = SW[y]
    local[12].wait()
    Wf[y, z, x] = SF[...].astype(LOW)
    local[13].wait()
    Wp[y, z, x] = SP[...].astype(LOW)
    local[10].wait()
    local[11].wait()
    pl.semaphore_wait(barrier, len(peers))

    vec_c = [copy(VR.at[s], VR.at[s], d) for d in others]
    cot_c = [copy(COT.at[c], COT.at[c], cdev)]
    hr = wq_h.shape[1] // 2
    third = hr // 3
    pairs = (
        (pl.ds(0, third), pl.ds(third, third)),
        (pl.ds(2 * third, 2 * third), pl.ds(4 * third, 2 * third)),
    )

    thin = [(pl.ds(2 * i * third, third), pl.ds((2 * i + 1) * third, third)) for i in range(3)]

    def gather(W, pairs):
        steps = []
        for a, b in pairs:
            zs = [copy(W.at[y, z, x, r], W.at[y, z, x, r], zdev(k)) for k in range(1, ZN) for r in (a, b)]
            one = [
                copy(W.at[y, :, x, a], W.at[y, :, x, a], xdev),
                copy(W.at[y, :, x, b], W.at[y, :, x, b], ydev),
            ]
            two = [
                copy(W.at[y, :, :, a], W.at[y, :, :, a], ydev),
                copy(W.at[:, :, x, b], W.at[:, :, x, b], xdev),
            ]
            steps.append((zs, one, two))
        return steps

    def gather_wide(W):
        steps = []
        for a, b in pairs:
            near = [
                copy(W.at[y, z, x, a], W.at[y, z, x, a], xdev),
                copy(W.at[y, z, x, b], W.at[y, z, x, b], ydev),
            ]
            zs = [copy(W.at[y, z, :, a], W.at[y, z, :, a], zdev(k)) for k in range(1, ZN)]
            zs += [copy(W.at[:, z, x, b], W.at[:, z, x, b], zdev(k)) for k in range(1, ZN)]
            far = [
                copy(W.at[y, :, :, a], W.at[y, :, :, a], ydev),
                copy(W.at[:, :, x, b], W.at[:, :, x, b], xdev),
            ]
            steps.append((near, zs, far))
        return steps

    ow = [
        (
            [copy(Wo.at[z, x, y], Wo.at[z, x, y], zdev(k)) for k in range(1, ZN)],
            [copy(Wo.at[:, x, y], Wo.at[:, x, y], xdev)],
            [copy(Wo.at[:, :, y], Wo.at[:, :, y], ydev)],
        )
    ]
    qw, pw, fw = gather(Wq, thin), gather_wide(Wp), gather(Wf, thin)

    def z_go(w, i):
        start(w[i][0])

    def one_go(w, i):
        landed(w[i][0])
        start(w[i][1])

    def two_go(w, i):
        n = len(w[i][1]) // len(w[i][2])
        for k, after in enumerate(w[i][2]):
            landed(w[i][1][k * n : (k + 1) * n])
            start([after])

    def all_in(w):
        for step in w:
            landed(step[2])

    def sent_all(w):
        for step in w:
            for group in step:
                sent(group)

    start(vec_c)
    z_go(qw, 0)
    z_go(pw, 0)
    z_go(pw, 1)
    start(cot_c)

    def row_tile(i, n=128):
        return pl.ds(pl.multiple_of(i * n, n), n)

    @pl.loop(0, half // 128)
    def _(i):
        r = row_tile(i)
        v = TOK[r, :].astype(FULL)
        v = v - jnp.mean(v, axis=-1, keepdims=True)
        rstd = lax.rsqrt(jnp.mean(v * v, axis=-1, keepdims=True) + EPSILON)
        N1F[r, :] = v * rstd
        RS[r, 0:1] = rstd

    landed(vec_c)
    z_go(qw, 1)

    def widen(v):
        return jnp.concatenate([v, jnp.zeros((v.shape[0], width - v.shape[1]), FULL)], axis=1)

    pieces = [widen(VR[g].astype(FULL)) for g in range(GROUPS)]
    plain = pieces[0]
    for g in range(1, GROUPS):
        plain = plain + pltpu.roll(pieces[g], g * lanes96, 1)
    VF[GAIN1 : SHIFT1 + 1, :] = plain[0:2]
    VF[OUTB : PROJB + 1, :] = plain[2:6]
    place = lax.broadcasted_iota(jnp.int32, (1, width), 1)

    def lanes(v, first, last, shift):
        v = jnp.where((place >= first) & (place < last), v, 0.0)
        return pltpu.roll(v, shift % width, 1) if shift % width else v

    for b in range(2):
        a0, a1 = (widen(VR[2 * (2 * b + c) + i].astype(FULL)) for i in range(2))
        a1 = pltpu.roll(a1, lanes96, 1)
        qb, vb = a0[6:7] + a1[6:7], a0[7:8] + a1[7:8]
        VF[QKVB + b : QKVB + b + 1, :] = (
            lanes(qb, 0, 128, 0) + lanes(qb, 128, 192, 256) + lanes(vb, 0, 128, 256) + lanes(vb, 128, 192, 384)
        )
        a1 = pltpu.roll(a1, 3 * lanes96, 1)
        row = a0[8:9] + a1[8:9]
        for j in range(1, 4):
            row = row + pltpu.roll(a0[8 + j : 9 + j] + a1[8 + j : 9 + j], j * lanes96, 1)
        VF[FCB + b : FCB + b + 1, :] = row

    def vrow(i):
        return VF[i : i + 1, :]

    @pl.loop(0, half // 128)
    def _(i):
        r = row_tile(i)
        N1[c, r, :] = (N1F[r, :] * vrow(GAIN1) + vrow(SHIFT1)).astype(LOW)

    n1_c = [copy(N1.at[c], N1.at[c], cdev)]
    start(n1_c)

    def transpose_all(source, target):
        @pl.loop(0, nrb)
        def _(i):
            h, off = i // (half // rblk), i % (half // rblk)
            rows = pl.ds(pl.multiple_of(off * rblk, rblk), rblk)
            cols = pl.ds(pl.multiple_of(i * rblk, rblk), rblk)
            for k in range(width // rblk):
                target[k * rblk : (k + 1) * rblk, cols] = source[h, rows, k * rblk : (k + 1) * rblk].T

    landed(cot_c)
    one_go(qw, 0)
    transpose_all(COT, T0)
    one_go(qw, 1)
    z_go(qw, 2)
    two_go(qw, 0)
    z_go(fw, 0)
    two_go(qw, 1)
    z_go(ow, 0)
    one_go(qw, 2)
    z_go(fw, 1)
    landed(n1_c)
    two_go(qw, 2)
    z_go(fw, 2)
    one_go(fw, 0)
    all_in(qw)

    def low_lanes(v):
        return lax.broadcasted_iota(jnp.int32, v.shape, 1) < HD

    def tile(v, i):
        return v[:, i * 128 : (i + 1) * 128]

    def roll(v):
        return pltpu.roll(v, HD, 1)

    @pl.loop(0, nrb)
    def _(i):
        h, off = i // (half // rblk), i % (half // rblk)
        rows = pl.ds(pl.multiple_of(off * rblk, rblk), rblk)
        out = pl.ds(pl.multiple_of(i * rblk, rblk), rblk)
        n = N1[h, rows, :]
        got = []
        for b in range(2):
            got.append(dot(n, Wq[b].reshape(width, Wq.shape[-1])) + VF[QKVB + b : QKVB + b + 1, : Wq.shape[-1]])
            QP[b, out, :] = (tile(got[b], 0).astype(LOW).astype(FULL) * 0.125).astype(LOW)
            KP[b, out, :] = tile(got[b], 1).astype(LOW)
            VP[b, out, :] = tile(got[b], 2).astype(LOW)
        first = low_lanes(tile(got[0], 3))
        q = jnp.where(first, tile(got[0], 3), roll(tile(got[1], 3)))
        QP[2, out, :] = (q.astype(LOW).astype(FULL) * 0.125).astype(LOW)
        KP[2, out, :] = jnp.where(first, roll(tile(got[0], 3)), tile(got[1], 3)).astype(LOW)
        VP[2, out, :] = jnp.where(first, tile(got[0], 4), roll(tile(got[1], 4))).astype(LOW)

        @pl.when(i == 0)
        def _():
            one_go(ow, 0)
            one_go(fw, 1)
            one_go(pw, 0)

        @pl.when(i == 2)
        def _():
            two_go(fw, 0)

    prefix = prefix_s[y]
    LSEC = DQ
    LSEC[...] = jnp.zeros(LSEC.shape, FULL)

    def lane_part(v, e):
        lane = lax.broadcasted_iota(jnp.int32, v.shape, 1)
        keep = lane < HD if e == 0 else lane >= HD
        return jnp.where(keep, v, jnp.zeros_like(v))

    def meanwhile(p, b, plan):
        for (pp, bb), steps in plan.items():
            if bb != b:
                continue
            if isinstance(p, int):
                for step in steps:
                    step()
            else:

                @pl.when(p == pp)
                def _(steps=steps):
                    for step in steps:
                        step()

    ctx_c = [copy(CTX.at[p, pl.ds(oc * half, half)], CTXP.at[p], cdev) for p in range(3)]
    wo_c = [copy(Wo, WOP, cdev)]

    def share_out():
        all_in(ow)
        start(wo_c)

    fetch = {
        (0, 0): [lambda: one_go(fw, 2), lambda: two_go(ow, 0)],
        (0, 1): [lambda: two_go(fw, 1), lambda: one_go(pw, 1)],
        (0, 3): [lambda: start(ctx_c[0:1])],
        (1, 2): [lambda: two_go(fw, 2)],
        (1, 3): [lambda: start(ctx_c[1:2]), lambda: two_go(pw, 0)],
        (2, 1): [share_out],
        (2, 3): [lambda: start(ctx_c[2:3])],
    }

    @pl.loop(0, 3)
    def _(p):
        for b in range(nrb):
            rows = pl.ds(b * rblk, rblk)
            cols = max(half, (b + 1) * rblk)
            q = QP[p, rows, :]
            keys, values = KP[p, :cols, :], VP[p, :cols, :]
            query = b * rblk + lax.broadcasted_iota(jnp.int32, (rblk, 1), 0)
            limit = jnp.maximum(prefix - 1, query)
            key = lax.broadcasted_iota(jnp.int32, (rblk, cols), 1)
            parts = []
            for e in range(2):
                sc = dot_nt(lane_part(q, e), keys)
                sc = jnp.where(key <= limit, sc, -1e30)
                peak = jnp.max(sc, axis=-1, keepdims=True)
                w = jnp.exp(sc - peak)
                total = jnp.sum(w, axis=-1, keepdims=True)
                parts.append(dot(w.astype(LOW), values) * (1.0 / total))
                lane = lax.broadcasted_iota(jnp.int32, (rblk, 128), 1)
                LSEC[rows, :] = jnp.where(lane == 2 * p + e, peak + jnp.log(total), LSEC[rows, :])
            CTX[p, rows, :] = jnp.where(low_lanes(parts[0]), parts[0], parts[1]).astype(LOW)
            meanwhile(p, b, fetch)

    for b in range(nrb):
        lt = LSEC[b * rblk : (b + 1) * rblk, :].T
        for h in range(6):
            LSER[h, :, b * rblk : (b + 1) * rblk] = lt[h : h + 1, :]
    def wide(ref, rows):
        return jnp.concatenate([ref[0, rows, :], ref[1, rows, :], ref[2, rows, :]], axis=1)

    def split_rows(make_block, away, home, copies, plus=None):
        per = half // rblk
        for which, target in ((oc, away), (c, home)):

            @pl.loop(0, per)
            def _(j):
                rows = pl.ds(pl.multiple_of(j * rblk, rblk), rblk)
                flat = pl.ds(pl.multiple_of((which * per + j) * rblk, rblk), rblk)
                block = make_block(which, rows, flat)
                target[rows, :] = block if plus is None or target is away else block + plus[rows, :]

            if target is away:
                start(copies)

    parts = [GPR.at[b, pl.ds(i * half, half)] for b in range(2) for i in range(2)]
    landed(wo_c)
    landed(ctx_c)

    @pl.loop(0, half // rblk)
    def _(j):
        r = pl.ds(pl.multiple_of(j * rblk, rblk), rblk)
        flat = pl.ds(pl.multiple_of((c * (half // rblk) + j) * rblk, rblk), rblk)
        o = dot_nt(wide(CTX, flat), Wo[...].reshape(width, Wo.shape[-1]))
        o = o + dot_nt(wide(CTXP, r), WOP[...].reshape(width, Wo.shape[-1]))
        m = TOK[r, :].astype(FULL) + (o + vrow(OUTB))
        MID[r, :] = m
        v = m - jnp.mean(m, axis=-1, keepdims=True)
        rstd = lax.rsqrt(jnp.mean(v * v, axis=-1, keepdims=True) + EPSILON)
        n = v * rstd
        N2F[r, :] = n
        RS[r, 1:2] = rstd
        N2[c, r, :] = (n * vrow(GAIN2) + vrow(SHIFT2)).astype(LOW)

    n2_c = [copy(N2.at[c], N2.at[c], cdev)]
    start(n2_c)
    two_go(pw, 1)
    landed(n2_c)
    all_in(fw)

    parts = [GPR.at[b, pl.ds(i * half, half)] for b in range(2) for i in range(2)]
    root = math.sqrt(2.0 / math.pi)

    @pl.loop(0, nrb * 2)
    def _(k):
        b, i = k // nrb, k % nrb
        h, off = i // (half // rblk), i % (half // rblk)
        rows = pl.ds(pl.multiple_of(off * rblk, rblk), rblk)
        flat = pl.ds(pl.multiple_of(i * rblk, rblk), rblk)
        u = dot(N2[h, rows, :], Wf[b].reshape(width, width)) + VF[pl.ds(FCB + b, 1), :]
        uu = u * u
        a = 0.5 * jnp.tanh(u * (root + (root * 0.044715) * uu)) + 0.5
        H[b, flat, :] = (u * a).astype(LOW)
        GPR[b, flat, :] = a * (1.0 + (1.0 - a) * (u * (2.0 * root + (2.0 * root * 0.134145) * uu)))

    def weight_grad(left_t, right, G, first, last):
        @pl.loop(0, 4)
        def _(k):
            b, m = k // 2, k % 2
            rows = pl.ds(pl.multiple_of(m * (width // 2), width // 2), width // 2)
            g = dot(left_t[rows, :], right[b, :, first:last])
            g = g.astype(LOW).reshape(ZN // 2, XN, width // GROUPS, last - first)
            G[b, pl.ds(m * (ZN // 2), ZN // 2), :, :, first:last] = g

    every = pl.ds(0, width)
    by_rows = [pairs[0] + (pl.ds(0, third), every), pairs[1] + (pl.ds(third, 2 * third), every)]

    def reduce_copies(G, plan, A1, B1, A2, B2, R3):
        steps = []
        for a, b, r, cols in plan:
            one = [
                copy(G.at[:, :, ox, a, cols], A1.at[:, :, r, cols], xdev),
                copy(G.at[oy, :, :, b, cols], B1.at[:, :, r, cols], ydev),
            ]
            two = [
                copy(G.at[oy, :, x, a, cols], A2.at[:, r, cols], ydev),
                copy(G.at[y, :, ox, b, cols], B2.at[:, r, cols], xdev),
            ]
            three = [
                copy(G.at[y, (z + k) % ZN, x, q, cols], R3.at[k - 1, q, cols], zdev(k))
                for k in range(1, ZN)
                for q in (a, b)
            ]
            steps.append((a, b, r, cols, one, two, three))

        def add(target, source):
            target[...] = (target[...].astype(FULL) + source[...].astype(FULL)).astype(LOW)

        def go(i):
            start(steps[i][4])

        def second(i):
            a, b, r, cols, one, two, three = steps[i]
            landed(one[:1])

            @pl.loop(0, ZN)
            def _(k):
                add(G.at[oy, k, x, a, cols], A1.at[oy, k, r, cols])

            start(two[:1])
            landed(one[1:])

            @pl.loop(0, ZN)
            def _(k):
                add(G.at[y, k, ox, b, cols], B1.at[k, ox, r, cols])

            start(two[1:])

            @pl.loop(0, ZN)
            def _(k):
                add(G.at[y, k, x, a, cols], A1.at[y, k, r, cols])
                add(G.at[y, k, x, b, cols], B1.at[k, x, r, cols])

        def third_step(i):
            a, b, r, cols, one, two, three = steps[i]
            landed(two)

            @pl.loop(0, ZN)
            def _(k):
                add(G.at[y, k, x, a, cols], A2.at[k, r, cols])
                add(G.at[y, k, x, b, cols], B2.at[k, r, cols])

            start(three)

        def last(i, out):
            a, b, r, cols, one, two, three = steps[i]
            landed(three)
            for q in (a, b):
                v = G[y, z, x, q, cols].astype(FULL)
                for k in range(ZN - 1):
                    v = v + R3[k, q, cols].astype(FULL)
                out[q, cols] = v

        return go, second, third_step, last

    def reduce_wide(G, plan, A1, B1, A2, B2, A3, B3):
        steps = []
        for a, b, r, cols in plan:
            one = [
                copy(G.at[oy, :, :, a, cols], A1.at[:, :, r, cols], ydev),
                copy(G.at[:, :, ox, b, cols], B1.at[:, :, r, cols], xdev),
            ]
            two = [copy(G.at[y, (z + k) % ZN, :, a, cols], A2.at[k - 1, :, r, cols], zdev(k)) for k in range(1, ZN)]
            two += [copy(G.at[:, (z + k) % ZN, x, b, cols], B2.at[k - 1, :, r, cols], zdev(k)) for k in range(1, ZN)]
            three = [
                copy(G.at[y, z, ox, a, cols], A3.at[r, cols], xdev),
                copy(G.at[oy, z, x, b, cols], B3.at[r, cols], ydev),
            ]
            steps.append((a, b, r, cols, one, two, three))

        def add(target, sources):
            v = target[...].astype(FULL)
            for source in sources:
                v = v + source[...].astype(FULL)
            target[...] = v.astype(LOW)

        def go(i):
            start(steps[i][4])

        def second(i):
            a, b, r, cols, one, two, three = steps[i]
            landed(one)

            @pl.loop(0, ZN)
            def _(k):
                for j in range(2):
                    add(G.at[y, k, j, a, cols], [A1.at[k, j, r, cols]])
                    add(G.at[j, k, x, b, cols], [B1.at[j, k, r, cols]])

            start(two)

        def third_step(i):
            a, b, r, cols, one, two, three = steps[i]
            landed(two)
            for j in range(2):
                add(G.at[y, z, j, a, cols], [A2.at[k, j, r, cols] for k in range(ZN - 1)])
                add(G.at[j, z, x, b, cols], [B2.at[k, j, r, cols] for k in range(ZN - 1)])
            start(three)

        def last(i, out):
            a, b, r, cols, one, two, three = steps[i]
            landed(three)
            for q, R in ((a, A3), (b, B3)):
                out[q, cols] = G[y, z, x, q, cols].astype(FULL) + R[r, cols].astype(FULL)

        return go, second, third_step, last

    rp = reduce_wide(Gp, by_rows, RpA1, RpB1, RpA2, RpB2, RpA3, RpB3)
    weight_grad(T0, H, Gp, 0, width)
    rp[0](0)
    transpose_all(N2, T1)
    all_in(pw)
    rp[0](1)


    def pair_nt(A, W, columns):
        def block(h, rows, flat):
            return dot_nt(A[0, flat, :columns], W[0].reshape(width, W.shape[-1])) + dot_nt(
                A[1, flat, :columns], W[1].reshape(width, W.shape[-1])
            )

        return block

    @pl.loop(0, nrb * 2)
    def _(k):
        b, i = k // nrb, k % nrb
        h, off = i // (half // rblk), i % (half // rblk)
        rows = pl.ds(pl.multiple_of(off * rblk, rblk), rblk)
        flat = pl.ds(pl.multiple_of(i * rblk, rblk), rblk)
        g = (dot(COT[h, rows, :], Wp[b].reshape(width, width)) * GPR[b, flat, :]).astype(LOW)
        PG[b, flat, :] = g
        VG[pl.ds(FCB + b, 1), :] += jnp.sum(g.astype(FULL), axis=0, keepdims=True)

    p2_c = [copy(parts[3], V1, cdev)]
    split_rows(pair_nt(PG, Wf, width), parts[3], parts[0], p2_c)
    rp[1](0)
    weight_grad(T1, PG, Gf, 0, width)
    rf = reduce_copies(Gf, by_rows, RfA1, RfB1, RfA2, RfB2, Rf3)
    rf[0](0)
    rf[0](1)
    landed(p2_c)

    sent(n2_c)

    def norm_back(dy, n, rstd, gain):
        e = dy * gain
        return (e - jnp.mean(e, axis=-1, keepdims=True) - n * jnp.mean(e * n, axis=-1, keepdims=True)) * rstd

    def add_row(i, v):
        VG[i : i + 1, :] += jnp.sum(v, axis=0, keepdims=True)

    @pl.loop(0, half // 128)
    def _(i):
        r = row_tile(i)
        dy = GPR[0, r, :] + V1[r, :]
        n = N2F[r, :]
        add_row(GAIN2, dy * n)
        add_row(SHIFT2, dy)
        cot = COT[c, r, :].astype(FULL)
        add_row(PROJB, cot)
        g = cot + norm_back(dy, n, RS[r, 1:2], vrow(GAIN2))
        N2F[r, :] = g
        low = g.astype(LOW)
        add_row(OUTB, low.astype(FULL))
        N2[c, r, :] = low

    ag_c = [copy(N2.at[c], N2.at[c], cdev)]
    start(ag_c)

    def vector_copies(first, last):
        r = pl.ds(first, last - first)
        over_z = [copy(VG.at[r], VZ.at[k - 1, r], zdev(k)) for k in range(1, ZN)]
        mine = VO.at[y * 2 + x, c, r]
        return r, over_z, mine, [copy(mine, mine, d) for d in near]

    def vector_second(v):
        r, over_z, mine, over_near = v
        landed(over_z)
        mine[...] = VG[r, :] + VZ[0, r, :] + VZ[1, r, :] + VZ[2, r, :]
        start(over_near)

    def vector_last(v):
        r, over_z, mine, over_near = v
        landed(over_near)
        for core in range(2):
            vo_ref[core, r, :] = VO[0, core, r, :] + VO[1, core, r, :] + VO[2, core, r, :] + VO[3, core, r, :]

    late, early = vector_copies(0, 4), vector_copies(8, VEC)
    start(early[1])
    pm_c = [copy(parts[1], V0, cdev)]
    split_rows(pair_nt(H, Wp, width), parts[1], MID, pm_c, MID)
    rp[1](1)
    transpose_all(N1, T1)
    landed(ag_c)
    landed(pm_c)

    @pl.loop(0, half // 128)
    def _(i):
        r = row_tile(i)
        TOK[r, :] = (MID[r, :] + (V0[r, :] + vrow(PROJB))).astype(LOW)

    out_c = [pltpu.make_async_copy(TOK, bo_h, ls.at[0]), pltpu.make_async_copy(N1.at[c], ig_h, ls.at[1])]
    out_c[0].start()

    @pl.loop(0, nrb)
    def _(i):
        h, off = i // (half // rblk), i % (half // rblk)
        rows = pl.ds(pl.multiple_of(off * rblk, rblk), rblk)
        flat = pl.ds(pl.multiple_of(i * rblk, rblk), rblk)
        g = dot(N2[h, rows, :], Wo[...].reshape(width, Wo.shape[-1])).astype(LOW)
        row = lax.broadcasted_iota(jnp.int32, (8, 128), 0)
        lane = lax.broadcasted_iota(jnp.int32, (8, 128), 1)
        pick = jnp.where(lane // HD == row, 1.0, 0.0).astype(LOW)
        for p in range(3):
            gp = tile(g, p)
            DO[p, flat, :] = gp
            prod = gp.astype(FULL) * CTX[p, flat, :].astype(FULL)
            high = prod.astype(LOW)
            rest = (prod - high.astype(FULL)).astype(LOW)
            d = dot_nt(pick, high) + dot_nt(pick, rest)
            for e in range(2):
                DELR[2 * p + e, :, flat] = d[e : e + 1, :]

    transpose_all(N2, T0)

    @pl.loop(0, 2)
    def _(m):
        rows = pl.ds(pl.multiple_of(m * (width // 2), width // 2), width // 2)
        g = dot(T0[rows, :], wide(CTX, pl.ds(0, seq_len)))
        g = g.astype(LOW).reshape(ZN // 2, XN, 2, width // (2 * GROUPS), Wo.shape[-1])
        Go[pl.ds(m * (ZN // 2), ZN // 2)] = g

    ro = [
        [copy(Go.at[:, :, oy], Ro1, ydev)],
        [copy(Go.at[:, ox, y], Ro2, xdev)],
        [copy(Go.at[(z + k) % ZN, x, y], Ro3.at[k - 1], zdev(k)) for k in range(1, ZN)],
        [copy(go_ref.at[t], go_ref.at[t], d) for d in (cdev, ydev, gdev)],
    ]
    start(ro[0])

    def ro_second():
        landed(ro[0])

        @pl.loop(0, ZN)
        def _(k):
            for i in range(XN):
                Go[k, i, y] = (Go[k, i, y].astype(FULL) + Ro1[k, i].astype(FULL)).astype(LOW)

        start(ro[1])

    def ro_third():
        landed(ro[1])

        @pl.loop(0, ZN)
        def _(k):
            Go[k, x, y] = (Go[k, x, y].astype(FULL) + Ro2[k].astype(FULL)).astype(LOW)

        start(ro[2])

    def ro_last():
        landed(ro[2])
        v = Go[z, x, y].astype(FULL)
        for k in range(ZN - 1):
            v = v + Ro3[k].astype(FULL)
        go_ref[t] = v
        start(ro[3])

    def attention_back(p, plan):
        DQ[...] = jnp.zeros(DQ.shape, FULL)
        for b in range(nrb):
            rows = pl.ds(b * rblk, rblk)
            first = 0 if b * rblk < half else b * rblk
            n = seq_len - first
            keys, values = KP[p, rows, :], VP[p, rows, :]
            queries, grads = QP[p, first:, :], DO[p, first:, :]
            key = b * rblk + lax.broadcasted_iota(jnp.int32, (rblk, 1), 0)
            limit = jnp.where(key < prefix, 0, key)
            query = first + lax.broadcasted_iota(jnp.int32, (rblk, n), 1)
            dk, dv = [], []
            for e in range(2):
                ke, ve = lane_part(keys, e), lane_part(values, e)
                sc = dot_nt(ke, queries) - LSER[2 * p + e, :, first:]
                w = jnp.exp(jnp.where(query >= limit, sc, -1e30))
                dw = dot_nt(ve, grads) - DELR[2 * p + e, :, first:]
                ds = (w * dw).astype(LOW)
                dv.append(dot(w.astype(LOW), grads))
                dk.append(dot(ds, queries))
                DQ[first:, :] += dot_tn(ds, ke)
            KP[p, rows, :] = jnp.where(low_lanes(dk[0]), dk[0], dk[1]).astype(LOW)
            VP[p, rows, :] = jnp.where(low_lanes(dv[0]), dv[0], dv[1]).astype(LOW)
            meanwhile(p, b, plan)
        QP[p, :, :] = (DQ[...] * 0.125).astype(LOW)

    away = {
        (0, 0): [lambda: rf[1](0)],
        (1, 0): [lambda: rf[1](1)],
        (1, 1): [lambda: rf[2](0)],
        (1, 2): [ro_second],
    }

    @pl.loop(0, 2)
    def _(p):
        attention_back(p, away)

    packed = Wq.shape[-1]
    sent_all(fw)

    @pl.loop(0, nrb)
    def _(i):
        flat = pl.ds(pl.multiple_of(i * rblk, rblk), rblk)
        for b in range(2):
            for k, ref in enumerate((QP, KP, VP)):
                g = ref[b, flat, :]
                H[b, flat, k * 128 : (k + 1) * 128] = g
                VG[QKVB + b : QKVB + b + 1, k * 128 : (k + 1) * 128] += jnp.sum(g.astype(FULL), axis=0, keepdims=True)

    by_lanes = [(pl.ds(0, hr), pl.ds(hr, hr), pl.ds(0, hr), pl.ds(0, 384))]
    rest = pl.ds(384, packed - 384)
    by_lanes += [pairs[1] + (pl.ds(third, 2 * third), rest), pairs[0] + (pl.ds(0, third), rest)]
    weight_grad(T1, H, Wf, 0, 384)
    rq = reduce_copies(Wf, by_lanes, RqA1, RqB1, RqA2, RqB2, Rq3)
    rq[0](0)
    away = {
        (2, 0): [lambda: rp[2](0), lambda: rf[2](1)],
        (2, 1): [ro_third],
        (2, 3): [lambda: rq[1](0)],
    }
    attention_back(2, away)

    @pl.loop(0, nrb)
    def _(i):
        flat = pl.ds(pl.multiple_of(i * rblk, rblk), rblk)
        q, k, v = (ref[2, flat, :].astype(FULL) for ref in (QP, KP, VP))
        first = low_lanes(q)
        packs = (
            (jnp.where(first, q, roll(k)), jnp.where(first, v, 0.0)),
            (jnp.where(first, roll(q), k), jnp.where(first, roll(v), 0.0)),
        )
        for b in range(2):
            for j in range(2):
                at_j = slice(384 + 128 * j, 512 + 128 * j)
                H[b, flat, at_j] = packs[b][j].astype(LOW)
                VG[QKVB + b : QKVB + b + 1, at_j] += jnp.sum(packs[b][j], axis=0, keepdims=True)

    weight_grad(T1, H, Wf, 384, packed)
    rq[0](1)
    rq[0](2)

    p1_c = [copy(parts[1], V1, cdev)]
    sent(pm_c)
    split_rows(pair_nt(H, Wq, packed), parts[1], parts[2], p1_c)
    rp[2](1)
    landed(p1_c)

    sent(n1_c)

    @pl.loop(0, half // 128)
    def _(i):
        r = row_tile(i)
        dy = GPR[1, r, :] + V1[r, :]
        n = N1F[r, :]
        add_row(GAIN1, dy * n)
        add_row(SHIFT1, dy)
        N1[c, r, :] = (N2F[r, :] + norm_back(dy, n, RS[r, 0:1], vrow(GAIN1))).astype(LOW)

    out_c[1].start()

    start(late[1])
    rq[2](0)
    vector_second(early)
    rq[1](1)
    rq[1](2)
    ro_last()
    gp_ref, gf_ref = MID.at[pl.ds(0, 2 * hr)], MID.at[pl.ds(2 * hr, 2 * hr)]
    out_c += [pltpu.make_async_copy(gp_ref, gp_h, ls.at[2]), pltpu.make_async_copy(gf_ref, gf_h, ls.at[3])]
    rp[3](0, gp_ref)
    rp[3](1, gp_ref)
    out_c[2].start()
    rf[3](0, gf_ref)
    rf[3](1, gf_ref)
    out_c[3].start()
    rq[2](1)
    rq[2](2)
    vector_second(late)
    vector_last(early)
    landed(ro[3])
    rq[3](0, gq_ref)
    vector_last(late)
    rq[3](1, gq_ref)
    rq[3](2, gq_ref)

    waited = {id(m) for m in n2_c + pm_c + n1_c}
    for step in fw:
        for group in step:
            waited |= {id(m) for m in group}
    sent([m for m in made if id(m) not in waited])
    for cp in out_c:
        cp.wait()


def gather_groups(v, axis, repeat, groups):
    if repeat == 1:
        return v
    return lax.all_gather(v, "dp", axis=axis, axis_index_groups=groups, tiled=True)


def scatter_groups(v, axis, repeat, groups):
    if repeat == 1:
        return v
    return lax.psum_scatter(v, "dp", scatter_dimension=axis, axis_index_groups=groups, tiled=True)


def on_device(
    dp_size,
    tokens,
    prefix,
    cotangent,
    first_gain,
    first_shift,
    qkv_weight,
    qv_bias,
    out_weight,
    out_bias,
    second_gain,
    second_shift,
    fc_weight,
    fc_bias,
    proj_weight,
    proj_bias,
):
    repeat = dp_size // GROUPS
    groups = [[g * repeat + i for i in range(repeat)] for g in range(GROUPS)]
    half, width = tokens.shape
    seq_len = 2 * half

    def whole(v, axis):
        return gather_groups(v.astype(LOW), axis, repeat, groups).astype(FULL) if repeat > 1 else v

    params = [
        whole(first_gain, 0), whole(first_shift, 0), whole(qkv_weight, 1), whole(qv_bias, 1), whole(out_weight, 1),
        whole(out_bias, 0), whole(second_gain, 0), whole(second_shift, 0), whole(fc_weight, 0), whole(fc_bias, 0),
        whole(proj_weight, 1), whole(proj_bias, 0),
    ]
    params[4], params[10] = params[4].T, params[10].T
    rows = params[8].shape[0]
    cols = params[2].shape[2]
    units = params[8].shape[1]
    pair = 2 * HD
    packed, own = 3 * cols + HD, 2 * cols
    hr = rows // 2
    ANY = pl.BlockSpec(memory_space=pl.ANY)
    IN_VMEM = pl.BlockSpec(memory_space=pltpu.VMEM)

    def reduce_space(lanes):
        return [
            pltpu.VMEM((2, ZN, hr, lanes), LOW),
            pltpu.VMEM((ZN, XN, hr, lanes), LOW),
            pltpu.VMEM((ZN, hr, lanes), LOW),
            pltpu.VMEM((ZN, hr, lanes), LOW),
            pltpu.VMEM((ZN - 1, rows, lanes), LOW),
        ]

    token_low = pltpu.VMEM((2, half, width), LOW)
    token_full = pltpu.VMEM((half, width), FULL)
    unit_low = pltpu.VMEM((2, seq_len, width), LOW)
    heads = pltpu.VMEM((3, seq_len, pair), LOW)
    scratch = (
        [
            pltpu.VMEM((2, ZN, XN, rows, packed), LOW),
            pltpu.VMEM((ZN, XN, 2, hr, own), LOW),
            pltpu.VMEM((2, ZN, XN, rows, width), LOW),
            pltpu.VMEM((2, ZN, XN, rows, width), LOW),
            pltpu.VMEM((ZN, XN, 2, hr, own), LOW),
            pltpu.VMEM((2, ZN, XN, rows, width), LOW),
            pltpu.VMEM((2, ZN, XN, rows, width), LOW),
        ]
        + reduce_space(packed)
        + reduce_space(width)
        + [
            pltpu.VMEM((ZN, XN, hr, width), LOW),
            pltpu.VMEM((2, ZN, hr, width), LOW),
            pltpu.VMEM((ZN - 1, XN, hr, width), LOW),
            pltpu.VMEM((ZN - 1, 2, hr, width), LOW),
            pltpu.VMEM((hr, width), LOW),
            pltpu.VMEM((hr, width), LOW),
        ]
        + [
            pltpu.VMEM((ZN, XN, hr, own), LOW),
            pltpu.VMEM((ZN, hr, own), LOW),
            pltpu.VMEM((ZN - 1, hr, own), LOW),
        ]
        + [
            pltpu.VMEM((half, width), LOW),
            token_low,
            token_full,
            token_full,
            pltpu.VMEM((half, 128), FULL),
            token_low,
            token_low,
            pltpu.VMEM((width, seq_len), LOW),
            pltpu.VMEM((width, seq_len), LOW),
        ]
        + [heads] * 5
        + [
            pltpu.VMEM((seq_len, pair), FULL),
            pltpu.VMEM((6, 1, seq_len), FULL),
            pltpu.VMEM((6, 1, seq_len), FULL),
        ]
        + [token_full] * 3
        + [unit_low, pltpu.VMEM((2, seq_len, width), FULL), unit_low]
        + [
            pltpu.VMEM((8, rows), FULL),
            pltpu.VMEM((2, rows), FULL),
            pltpu.VMEM((1, 4 * rows), FULL),
            pltpu.VMEM((3, rows, cols), FULL),
            pltpu.VMEM((2, hr, own), LOW),
            pltpu.VMEM((3, half, pair), LOW),
            pltpu.VMEM((ZN, XN, 2, hr, own), LOW),
            pltpu.VMEM((GROUPS, VEC, 128), LOW),
            pltpu.VMEM((VEC, width), FULL),
            pltpu.VMEM((VEC, width), FULL),
            pltpu.VMEM((ZN - 1, VEC, width), FULL),
        ]
        + [pltpu.VMEM((4, 2, VEC, width), FULL)]
        + [
            pltpu.SemaphoreType.DMA((SEMS,)),
            pltpu.SemaphoreType.DMA((SEMS,)),
            pltpu.SemaphoreType.DMA((16,)),
        ]
    )
    out_shape = [
        jax.ShapeDtypeStruct((half, width), LOW),
        jax.ShapeDtypeStruct((half, width), LOW),
        jax.ShapeDtypeStruct((rows, packed), FULL),
        jax.ShapeDtypeStruct((4, hr, own), FULL),
        jax.ShapeDtypeStruct((rows, width), FULL),
        jax.ShapeDtypeStruct((rows, width), FULL),
        jax.ShapeDtypeStruct((2, VEC, width), FULL),
    ]
    grown = pl.pallas_call(
        functools.partial(block_kernel, repeat, seq_len),
        out_shape=out_shape,
        in_specs=[ANY, pl.BlockSpec(memory_space=pltpu.SMEM)] + [ANY] * 13,
        out_specs=[ANY] * 2 + [IN_VMEM] * 2 + [ANY] * 2 + [IN_VMEM],
        scratch_shapes=scratch,
        compiler_params=pltpu.CompilerParams(
            collective_id=0, has_side_effects=True, vmem_limit_bytes=62 * 1024 * 1024
        ),
    )(tokens, prefix, cotangent, *params)

    vector = jax.ShapeDtypeStruct((rows,), FULL)
    small = (2, 3, 5, 7, 8, 9, 11, 13)
    results = pl.pallas_call(
        functools.partial(unpack_kernel, repeat),
        out_shape=[
            out_shape[0],
            out_shape[1],
            vector,
            vector,
            jax.ShapeDtypeStruct((3, rows, cols), FULL),
            jax.ShapeDtypeStruct((2, rows), FULL),
            jax.ShapeDtypeStruct((rows, width), FULL),
            vector,
            vector,
            vector,
            jax.ShapeDtypeStruct((rows, units), FULL),
            jax.ShapeDtypeStruct((4 * rows,), FULL),
            jax.ShapeDtypeStruct((rows, units), FULL),
            vector,
        ],
        in_specs=[ANY] * 7,
        out_specs=[IN_VMEM if i in small else ANY for i in range(14)],
        scratch_shapes=[
            pltpu.VMEM((rows, packed), FULL),
            pltpu.VMEM((4, hr, own), FULL),
            pltpu.VMEM((2, VEC, width), FULL),
            pltpu.VMEM((3, rows, cols), FULL),
            pltpu.VMEM((rows, width), FULL),
            pltpu.VMEM((half, width), LOW),
            pltpu.VMEM((half, width), LOW),
            pltpu.VMEM((rows, units), FULL),
            pltpu.VMEM((rows, units), FULL),
            pltpu.SemaphoreType.DMA((13,)),
        ],
        compiler_params=pltpu.CompilerParams(vmem_limit_bytes=62 * 1024 * 1024),
    )(*grown)
    results = [v.T if i in (6, 12) else v for i, v in enumerate(results)]
    along = (None, None, 0, 0, 1, 1, 1, 0, 0, 0, 0, 0, 1, 0)
    return tuple(
        v if repeat == 1 or axis is None else scatter_groups(v, axis, repeat, groups)
        for v, axis in zip(results, along, strict=True)
    )


def unpack_kernel(
    repeat, bo, ig, gq_h, go_h, gf, gp, vo_h,
    bo_out, ig_out, gain1, shift1, wq_h, qvb, wo_h, outb, gain2, shift2, wf, fcb, wp, projb,
    gq, go, vo, wq, wo, b1, b2, w1, w2, sems,
):
    moves = [(vo_h, vo), (gq_h, gq), (go_h, go), (ig, b2), (bo, b1), (gf, w1), (gp, w2)]
    moves += [(wq, wq_h), (wo, wo_h), (b2, ig_out), (b1, bo_out), (w1, wf), (w2, wp)]
    moves = [pltpu.make_async_copy(a, b, sems.at[i]) for i, (a, b) in enumerate(moves)]
    for cp in moves[:7]:
        cp.start()
    for i in range(3, 7):
        moves[i].wait()
        moves[i + 6].start()
    moves[1].wait()
    for k in range(3):
        wq[k] = jnp.concatenate(
            [gq[:, k * 128 : (k + 1) * 128], gq[:, 384 + k * HD : 384 + (k + 1) * HD]], axis=1
        )
    moves[7].start()
    moves[2].wait()
    m = [jnp.concatenate([go[core], go[2 + core]], axis=0) for core in range(2)]
    wo[...] = jnp.concatenate(
        [
            v
            for b in range(2)
            for core in range(2)
            for v in (m[core][:, b * 128 : (b + 1) * 128], m[core][:, 256 + b * HD : 256 + (b + 1) * HD])
        ],
        axis=1,
    )
    moves[8].start()
    moves[0].wait()
    s = lax.axis_index("dp") // repeat
    width = vo.shape[2]
    n = gain1.shape[0]
    both = pltpu.roll(vo[0] + vo[1], (GROUPS - s) % GROUPS * n, 1)
    for i, out in ((GAIN1, gain1), (SHIFT1, shift1), (OUTB, outb), (GAIN2, gain2), (SHIFT2, shift2), (PROJB, projb)):
        out[...] = both[i, :n]
    owner = s // 2
    core, b, odd = owner % 2, owner // 2, s % 2
    place = lax.broadcasted_iota(jnp.int32, (1, width), 1)

    def lanes(v, first, last, shift):
        v = jnp.where((place >= first) & (place < last), v, 0.0)
        return pltpu.roll(v, shift % width, 1) if shift % width else v

    row = vo[core, pl.ds(QKVB + b, 1), :]
    q = lanes(row, 0, 128, 0) + lanes(row, 384, 448, -256)
    v = lanes(row, 256, 384, -256) + lanes(row, 512, 576, -384)
    back = (width - odd * n) % width
    qvb[0:1, :] = pltpu.roll(q, back, 1)[:, :n]
    qvb[1:2, :] = pltpu.roll(v, back, 1)[:, :n]
    row = vo[core, pl.ds(FCB + b, 1), :]
    fcb[...] = pltpu.roll(row, odd * (width // 2), 1)[0, : width // 2]
    for i in range(7, 13):
        moves[i].wait()


def solution(mesh):
    placed = (
        P(("dp", "tensor"), None),
        P("dp"),
        P(("dp", "tensor"), None),
        P("dp"),
        P("dp"),
        P(None, "dp", "tensor"),
        P(None, "dp"),
        P(None, "dp"),
        P("dp"),
        P("dp"),
        P("dp"),
        P("dp", "tensor"),
        P("dp"),
        P("tensor", "dp"),
        P("dp"),
    )
    return jax.shard_map(
        functools.partial(on_device, mesh.shape["dp"]),
        mesh=mesh,
        in_specs=placed,
        out_specs=(placed[0], placed[0]) + placed[3:],
        check_vma=False,
    )
```

```python
import functools
import math

import jax
import jax.numpy as jnp
from jax import lax
from jax.experimental import pallas as pl
from jax.experimental.pallas import tpu as pltpu
from jax.sharding import PartitionSpec as P

MESH = pl.DeviceIdType.MESH
LOW, FULL = jnp.bfloat16, jnp.float32
EPSILON = 1e-05
HD = 64
GROUPS, ZN, XN = 8, 4, 2
SEMS = 134
VEC = 16

GAIN1, SHIFT1, QKVB, OUTB, GAIN2, SHIFT2, PROJB, FCB = 0, 1, 2, 8, 9, 10, 11, 12


def dot(a, b):
    return jnp.dot(a, b, preferred_element_type=FULL)


def dot_nt(a, b):
    return lax.dot_general(a, b, (((1,), (1,)), ((), ())), preferred_element_type=FULL)


def dot_tn(a, b):
    return lax.dot_general(a, b, (((0,), (0,)), ((), ())), preferred_element_type=FULL)


def block_kernel(repeat, seq_len, *refs):
    (
        tok_h, prefix_h, cot_h, gain1_h, shift1_h, wq_h, qvb_h, wo_h, outb_h,
        gain2_h, shift2_h, wf_h, fcb_h, wp_h, projb_h,
        bo_h, ig_h, gq_h, go_h, gf_h, gp_h, vo_h,
        Wq, Wo, Wf, Wp, Go, Gp, Gf,
        RqA1, RqB1, RqA2, RqB2, Rq3,
        RfA1, RfB1, RfA2, RfB2, Rf3,
        RpA1, RpB1, RpA2, RpB2, RpA3, RpB3, RpEA, RpEB,
        Ro1, Ro2, Ro3,
        TOK, COT, N1F, N2F, RS, N1, N2, T0, T1,
        QP, KP, VP, CTX, DO, DQ, LSER, DELR,
        MID, V0, V1, H, GPR, PG,
        SV, SB, SC, SQ, SW, CTXP, WOP,
        VR, VF, VG, VZ, VO, gq_ref, go_ref, vo_ref, prefix_s,
        ss, rs, ls,
    ) = refs
    half = seq_len // 2
    width = TOK.shape[1]
    rblk = 256
    nrb = seq_len // rblk
    dp = lax.axis_index("dp")
    t = lax.axis_index("tensor")
    s, sub = dp // repeat, dp % repeat
    z, x = s // XN, s % XN
    y, c = t // 2, t % 2
    oy, oc, ox = 1 - y, 1 - c, 1 - x

    def at(zz, xx, tt):
        return ((zz * XN + xx) * repeat + sub, tt)

    def zdev(k):
        return at((z + k) % ZN, x, t)

    xdev = at(z, ox, t)
    ydev = at(z, x, oy * 2 + c)
    cdev = at(z, x, y * 2 + oc)
    gdev = at(z, x, oy * 2 + oc)
    near = [xdev, ydev, cdev, gdev] + [at(z, ox, i * 2 + j) for i, j in ((y, oc), (oy, c), (oy, oc))]
    others = [(((s + k) % GROUPS) * repeat + sub, t) for k in range(1, GROUPS)]

    count = [0]
    pending = []

    class Copy:
        def __init__(self, src, dst, dev, recv=None, alone=True):
            self.k = count[0]
            count[0] += 1
            self.parts = src, dst, dev, self.k if recv is None else recv.k
            if alone:
                pending.append(self)

        def made(self):
            src, dst, dev, recv = self.parts
            return pltpu.make_async_remote_copy(
                src_ref=src, dst_ref=dst, send_sem=ss.at[self.k], recv_sem=rs.at[recv],
                device_id=dev, device_id_type=MESH,
            )

        def start(self):
            self.made().start()

        def landed(self):
            self.made().wait_recv()

        def sent(self):
            self.made().wait_send()

    class Group:
        def __init__(self, moves, every):
            k = count[0]
            count[0] += 1
            self.moves = [Copy(*m, alone=False) for m in moves]
            for m in self.moves:
                m.k, m.parts = k, m.parts[:3] + (k,)
            count[0] = k + 1
            self.every = Copy(every, every, moves[0][2], alone=False)
            self.every.k, self.every.parts = k, self.every.parts[:3] + (k,)
            count[0] = k + 1
            pending.append(self)

        def start(self):
            for m in self.moves:
                m.start()

        def landed(self):
            self.every.landed()

        def sent(self):
            self.every.sent()

    class ZGather:
        def __init__(self, block):
            self.to = [Copy(block(z), block(z), zdev(k), alone=False) for k in range(1, ZN)]
            self.up = Copy(block(0), block(0), at(3, x, t), self.to[2], False)
            self.down = Copy(block(3), block(3), at(0, x, t), self.to[0], False)
            pending.append(self)

        def each(self, act):
            act(self.to[1])
            pl.when(z != 3)(lambda: act(self.to[0]))
            pl.when(z != 0)(lambda: act(self.to[2]))

        def start(self):
            self.each(lambda m: m.start())

        def middle(self):
            def go_on(onward):
                landed(self.to[1:2])
                onward.start()

            pl.when(z == 2)(lambda: go_on(self.up))
            pl.when(z == 1)(lambda: go_on(self.down))

        def landed(self):
            pl.when((z == 0) | (z == 3))(self.to[1].landed)
            self.to[0].landed()
            self.to[2].landed()

        def sent(self):
            self.each(lambda m: m.sent())
            pl.when(z == 2)(self.up.sent)
            pl.when(z == 1)(self.down.sent)

    class ZReduce:
        def __init__(self, block, arrived, extra):
            self.block, self.extra = block, extra
            self.to = [Copy(block((z + k) % ZN), arrived(k - 1), zdev(k), alone=False) for k in range(1, ZN)]
            self.up = Copy(block(3), extra, at(1, x, t), alone=False)
            self.down = Copy(block(0), extra, at(2, x, t), alone=False)
            pending.append(self)

            def none(slot):
                arrived(slot)[...] = jnp.zeros(extra.shape, LOW)

            pl.when(z == 0)(lambda: none(0))
            pl.when(z == 3)(lambda: none(2))

        def start(self):
            pl.when(z != 3)(self.to[0].start)
            pl.when(z != 0)(self.to[2].start)
            pl.when(z == 0)(self.up.start)
            pl.when(z == 3)(self.down.start)
            pl.when((z == 0) | (z == 3))(self.to[1].start)

        def middle(self):
            def go_on(arrival, owner):
                landed([arrival])
                target = self.block(owner)
                target[...] = (target[...].astype(FULL) + self.extra[...].astype(FULL)).astype(LOW)
                self.to[1].start()

            pl.when(z == 1)(lambda: go_on(self.up, 3))
            pl.when(z == 2)(lambda: go_on(self.down, 0))

        def landed(self):
            self.to[1].landed()
            pl.when(z != 0)(self.to[0].landed)
            pl.when(z != 3)(self.to[2].landed)

        def sent(self):
            self.to[1].sent()
            pl.when(z != 3)(self.to[0].sent)
            pl.when(z != 0)(self.to[2].sent)
            pl.when(z == 0)(self.up.sent)
            pl.when(z == 3)(self.down.sent)

    def copy(src, dst, dev):
        return Copy(src, dst, dev)

    def start(moves):
        for m in moves:
            m.start()

    def landed(moves):
        for m in moves:
            m.landed()

    def sent(moves):
        for m in moves:
            m.sent()

    barrier = pltpu.get_barrier_semaphore()
    peers = others + [d for i, d in enumerate(near) if i != 0]
    for d in peers:
        pl.semaphore_signal(barrier, inc=1, device_id=d, device_id_type=MESH)

    SO, SF, SP = (GPR.at[0, pl.ds(i * wo_h.shape[0], wo_h.shape[0])] for i in range(3))
    brought = [
        (wq_h, SQ), (qvb_h, SB), (fcb_h, SC.at[0]),
        (gain1_h, SV.at[0]), (shift1_h, SV.at[1]), (outb_h, SV.at[2]),
        (gain2_h, SV.at[3]), (shift2_h, SV.at[4]), (projb_h, SV.at[5]),
        (wo_h, SO), (tok_h, TOK), (cot_h, COT.at[c]), (wf_h, SF), (wp_h, SP),
        (prefix_h, prefix_s),
    ]
    local = [pltpu.make_async_copy(a, b, ls.at[i]) for i, (a, b) in enumerate(brought)]
    for cp in local:
        cp.start()

    lanes96 = SV.shape[1]
    VG[...] = jnp.zeros(VG.shape, FULL)
    for cp in local[1:9]:
        cp.wait()
    VG[0:6, :lanes96] = SV[0:6, :]
    VG[6:8, :lanes96] = SB[...]
    for j in range(4):
        VG[8 + j : 9 + j, :lanes96] = SC[:, j * lanes96 : (j + 1) * lanes96]
    VR[s] = VG[:, :128].astype(LOW)
    VG[...] = jnp.zeros(VG.shape, FULL)
    local[0].wait()
    q3 = SQ[...]
    Wq[y, z, x] = jnp.concatenate(
        [q3[0, :, :128], q3[1, :, :128], q3[2, :, :128]]
        + [q3[k, :, 128:] for k in range(3)]
        + [jnp.zeros((q3.shape[1], HD), FULL)],
        axis=1,
    ).astype(LOW)
    pl.semaphore_wait(barrier, len(peers))

    vec_c = [Group([(VR.at[s], VR.at[s], d) for d in others], VR.at[pl.ds(0, GROUPS - 1)])]
    cot_c = [copy(COT.at[c], COT.at[c], cdev)]
    hr = wq_h.shape[1] // 2
    third = hr // 3
    pairs = (
        (pl.ds(0, third), pl.ds(third, third)),
        (pl.ds(2 * third, 2 * third), pl.ds(4 * third, 2 * third)),
    )

    thin = [(pl.ds(2 * i * third, third), pl.ds((2 * i + 1) * third, third)) for i in range(3)]

    def gather(W, pairs):
        steps = []
        for a, b in pairs:
            r = pl.ds(a.start, a.size + b.size)
            mine = W.at[y, z, x, r]
            zs = [Group([(mine, mine, zdev(k)) for k in range(1, ZN)], W.at[y, pl.ds(0, ZN - 1), x, r])]
            one = [
                copy(W.at[y, :, x, a], W.at[y, :, x, a], xdev),
                copy(W.at[y, :, x, b], W.at[y, :, x, b], ydev),
            ]
            two = [
                copy(W.at[y, :, :, a], W.at[y, :, :, a], ydev),
                copy(W.at[:, :, x, b], W.at[:, :, x, b], xdev),
            ]
            steps.append((zs, one, two))
        return steps

    def gather_wide(W):
        steps = []
        for a, b in pairs:
            near = [
                copy(W.at[y, z, x, a], W.at[y, z, x, a], xdev),
                copy(W.at[y, z, x, b], W.at[y, z, x, b], ydev),
            ]
            zs = [ZGather(lambda i, a=a: W.at[y, i, :, a]), ZGather(lambda i, b=b: W.at[:, i, x, b])]
            far = [
                copy(W.at[y, :, :, a], W.at[y, :, :, a], ydev),
                copy(W.at[:, :, x, b], W.at[:, :, x, b], xdev),
            ]
            steps.append((near, zs, far))
        return steps

    ow = [
        (
            [Group([(Wo.at[z, x, y], Wo.at[z, x, y], zdev(k)) for k in range(1, ZN)], Wo.at[pl.ds(0, ZN - 1), x, y])],
            [copy(Wo.at[:, x, y], Wo.at[:, x, y], xdev)],
            [copy(Wo.at[:, :, y], Wo.at[:, :, y], ydev)],
        )
    ]
    qw, pw, fw = gather(Wq, thin), gather_wide(Wp), gather(Wf, thin)

    def z_go(w, i):
        start(w[i][0])

    def one_go(w, i):
        landed(w[i][0])
        start(w[i][1])

    def two_go(w, i):
        n = len(w[i][1]) // len(w[i][2])
        for k, after in enumerate(w[i][2]):
            landed(w[i][1][k * n : (k + 1) * n])
            start([after])

    def all_in(w):
        for step in w:
            landed(step[2])

    def sent_all(w):
        for step in w:
            for group in step:
                sent(group)

    start(vec_c)
    z_go(qw, 0)
    local[9].wait()
    turned = pltpu.roll(SO[...], (width - c * (width // 4)) % width, 1)
    last = jnp.concatenate([turned[:, 128:192], turned[:, 512:576]], axis=1)
    mine = jnp.concatenate([turned[:, 0:128], turned[:, 384:512], last], axis=1).astype(LOW)
    SW[0] = mine[: SW.shape[1]]
    SW[1] = mine[SW.shape[1] :]
    Wo[z, x, y] = SW[y]
    local[12].wait()
    Wf[y, z, x] = SF[...].astype(LOW)
    local[13].wait()
    Wp[y, z, x] = SP[...].astype(LOW)
    local[10].wait()
    local[11].wait()
    local[14].wait()
    z_go(pw, 0)
    z_go(pw, 1)
    start(cot_c)

    def row_tile(i, n=128):
        return pl.ds(pl.multiple_of(i * n, n), n)

    @pl.loop(0, half // 128)
    def _(i):
        r = row_tile(i)
        v = TOK[r, :].astype(FULL)
        v = v - jnp.mean(v, axis=-1, keepdims=True)
        rstd = lax.rsqrt(jnp.mean(v * v, axis=-1, keepdims=True) + EPSILON)
        N1F[r, :] = v * rstd
        RS[r, 0:1] = rstd

    z_go(qw, 1)
    landed(vec_c)

    def widen(v):
        return jnp.concatenate([v, jnp.zeros((v.shape[0], width - v.shape[1]), FULL)], axis=1)

    pieces = [widen(VR[g].astype(FULL)) for g in range(GROUPS)]
    plain = pieces[0]
    for g in range(1, GROUPS):
        plain = plain + pltpu.roll(pieces[g], g * lanes96, 1)
    VF[GAIN1 : SHIFT1 + 1, :] = plain[0:2]
    VF[OUTB : PROJB + 1, :] = plain[2:6]
    place = lax.broadcasted_iota(jnp.int32, (1, width), 1)

    def lanes(v, first, last, shift):
        v = jnp.where((place >= first) & (place < last), v, 0.0)
        return pltpu.roll(v, shift % width, 1) if shift % width else v

    for b in range(2):
        a0, a1 = (widen(VR[2 * (2 * b + c) + i].astype(FULL)) for i in range(2))
        a1 = pltpu.roll(a1, lanes96, 1)
        qb, vb = a0[6:7] + a1[6:7], a0[7:8] + a1[7:8]
        VF[QKVB + b : QKVB + b + 1, :] = (
            lanes(qb, 0, 128, 0) + lanes(qb, 128, 192, 256) + lanes(vb, 0, 128, 256) + lanes(vb, 128, 192, 384)
        )
        a1 = pltpu.roll(a1, 3 * lanes96, 1)
        row = a0[8:9] + a1[8:9]
        for j in range(1, 4):
            row = row + pltpu.roll(a0[8 + j : 9 + j] + a1[8 + j : 9 + j], j * lanes96, 1)
        VF[FCB + b : FCB + b + 1, :] = row

    def vrow(i):
        return VF[i : i + 1, :]

    @pl.loop(0, half // 128)
    def _(i):
        r = row_tile(i)
        N1[c, r, :] = (N1F[r, :] * vrow(GAIN1) + vrow(SHIFT1)).astype(LOW)

    n1_c = [copy(N1.at[c], N1.at[c], cdev)]
    start(n1_c)

    def transpose_all(source, target):
        @pl.loop(0, nrb)
        def _(i):
            h, off = i // (half // rblk), i % (half // rblk)
            rows = pl.ds(pl.multiple_of(off * rblk, rblk), rblk)
            cols = pl.ds(pl.multiple_of(i * rblk, rblk), rblk)
            for k in range(width // rblk):
                target[k * rblk : (k + 1) * rblk, cols] = source[h, rows, k * rblk : (k + 1) * rblk].T

    landed(cot_c)
    one_go(qw, 0)
    transpose_all(COT, T0)
    one_go(qw, 1)
    z_go(qw, 2)
    two_go(qw, 0)
    z_go(fw, 0)
    two_go(qw, 1)
    z_go(ow, 0)
    one_go(qw, 2)
    z_go(fw, 1)
    landed(n1_c)
    two_go(qw, 2)
    z_go(fw, 2)
    one_go(fw, 0)
    all_in(qw)

    def low_lanes(v):
        return lax.broadcasted_iota(jnp.int32, v.shape, 1) < HD

    def tile(v, i):
        return v[:, i * 128 : (i + 1) * 128]

    def roll(v):
        return pltpu.roll(v, HD, 1)

    @pl.loop(0, nrb)
    def _(i):
        h, off = i // (half // rblk), i % (half // rblk)
        rows = pl.ds(pl.multiple_of(off * rblk, rblk), rblk)
        out = pl.ds(pl.multiple_of(i * rblk, rblk), rblk)
        n = N1[h, rows, :]
        got = []
        for b in range(2):
            got.append(dot(n, Wq[b].reshape(width, Wq.shape[-1])) + VF[QKVB + b : QKVB + b + 1, : Wq.shape[-1]])
            QP[b, out, :] = (tile(got[b], 0).astype(LOW).astype(FULL) * 0.125).astype(LOW)
            KP[b, out, :] = tile(got[b], 1).astype(LOW)
            VP[b, out, :] = tile(got[b], 2).astype(LOW)
        first = low_lanes(tile(got[0], 3))
        q = jnp.where(first, tile(got[0], 3), roll(tile(got[1], 3)))
        QP[2, out, :] = (q.astype(LOW).astype(FULL) * 0.125).astype(LOW)
        KP[2, out, :] = jnp.where(first, roll(tile(got[0], 3)), tile(got[1], 3)).astype(LOW)
        VP[2, out, :] = jnp.where(first, tile(got[0], 4), roll(tile(got[1], 4))).astype(LOW)

        @pl.when(i == 0)
        def _():
            one_go(ow, 0)
            one_go(fw, 1)
            one_go(pw, 0)

        @pl.when(i == 2)
        def _():
            two_go(fw, 0)

    prefix = prefix_s[y]
    LSEC = DQ
    LSEC[...] = jnp.zeros(LSEC.shape, FULL)

    def lane_part(v, e):
        lane = lax.broadcasted_iota(jnp.int32, v.shape, 1)
        keep = lane < HD if e == 0 else lane >= HD
        return jnp.where(keep, v, jnp.zeros_like(v))

    def meanwhile(p, b, plan):
        for (pp, bb), steps in plan.items():
            if bb != b:
                continue
            if isinstance(p, int):
                for step in steps:
                    step()
            else:

                @pl.when(p == pp)
                def _(steps=steps):
                    for step in steps:
                        step()

    ctx_c = [copy(CTX.at[p, pl.ds(oc * half, half)], CTXP.at[p], cdev) for p in range(3)]
    wo_c = [copy(Wo, WOP, cdev)]

    def share_out():
        all_in(ow)
        start(wo_c)

    def pass_on(i):
        for m in pw[i][1]:
            m.middle()

    fetch = {
        (0, 0): [lambda: one_go(fw, 2), lambda: two_go(ow, 0)],
        (0, 1): [lambda: two_go(fw, 1), lambda: one_go(pw, 1)],
        (0, 3): [lambda: start(ctx_c[0:1])],
        (1, 1): [lambda: pass_on(0)],
        (1, 2): [lambda: two_go(fw, 2)],
        (1, 3): [lambda: start(ctx_c[1:2])],
        (2, 0): [lambda: two_go(pw, 0)],
        (2, 1): [share_out],
        (2, 3): [lambda: start(ctx_c[2:3]), lambda: pass_on(1)],
    }

    @pl.loop(0, 3)
    def _(p):
        for b in range(nrb):
            rows = pl.ds(b * rblk, rblk)
            cols = max(half, (b + 1) * rblk)
            q = QP[p, rows, :]
            keys, values = KP[p, :cols, :], VP[p, :cols, :]
            query = b * rblk + lax.broadcasted_iota(jnp.int32, (rblk, 1), 0)
            limit = jnp.maximum(prefix - 1, query)
            free = b * rblk
            key = free + lax.broadcasted_iota(jnp.int32, (rblk, cols - free), 1)
            parts = []
            for e in range(2):
                sc = dot_nt(lane_part(q, e), keys)
                tail = jnp.where(key <= limit, sc[:, free:], -1e30)
                sc = jnp.concatenate([sc[:, :free], tail], axis=1) if free else tail
                peak = jnp.max(sc, axis=-1, keepdims=True)
                w = jnp.exp(sc - peak)
                total = jnp.sum(w, axis=-1, keepdims=True)
                parts.append(dot(w.astype(LOW), values) * (1.0 / total))
                lane = lax.broadcasted_iota(jnp.int32, (rblk, 128), 1)
                LSEC[rows, :] = jnp.where(lane == 2 * p + e, peak + jnp.log(total), LSEC[rows, :])
            CTX[p, rows, :] = jnp.where(low_lanes(parts[0]), parts[0], parts[1]).astype(LOW)
            meanwhile(p, b, fetch)

    for b in range(nrb):
        lt = LSEC[b * rblk : (b + 1) * rblk, :].T
        for h in range(6):
            LSER[h, :, b * rblk : (b + 1) * rblk] = lt[h : h + 1, :]
    def wide(ref, rows):
        return jnp.concatenate([ref[0, rows, :], ref[1, rows, :], ref[2, rows, :]], axis=1)

    def split_rows(make_block, away, home, copies, plus=None):
        per = half // rblk
        for which, target in ((oc, away), (c, home)):

            @pl.loop(0, per)
            def _(j):
                rows = pl.ds(pl.multiple_of(j * rblk, rblk), rblk)
                block = make_block(pl.ds(pl.multiple_of((which * per + j) * rblk, rblk), rblk))
                target[rows, :] = block if plus is None or target is away else block + plus[rows, :]

            if target is away:
                start(copies)

    parts = [GPR.at[b, pl.ds(i * half, half)] for b in range(2) for i in range(2)]
    landed(wo_c)
    landed(ctx_c)

    @pl.loop(0, half // rblk)
    def _(j):
        r = pl.ds(pl.multiple_of(j * rblk, rblk), rblk)
        flat = pl.ds(pl.multiple_of((c * (half // rblk) + j) * rblk, rblk), rblk)
        o = dot_nt(wide(CTX, flat), Wo[...].reshape(width, Wo.shape[-1]))
        o = o + dot_nt(wide(CTXP, r), WOP[...].reshape(width, Wo.shape[-1]))
        m = TOK[r, :].astype(FULL) + (o + vrow(OUTB))
        MID[r, :] = m
        v = m - jnp.mean(m, axis=-1, keepdims=True)
        rstd = lax.rsqrt(jnp.mean(v * v, axis=-1, keepdims=True) + EPSILON)
        n = v * rstd
        N2F[r, :] = n
        RS[r, 1:2] = rstd
        N2[c, r, :] = (n * vrow(GAIN2) + vrow(SHIFT2)).astype(LOW)

    n2_c = [copy(N2.at[c], N2.at[c], cdev)]
    start(n2_c)
    landed(n2_c)
    all_in(fw)

    parts = [GPR.at[b, pl.ds(i * half, half)] for b in range(2) for i in range(2)]
    root = math.sqrt(2.0 / math.pi)

    @pl.loop(0, nrb * 2)
    def _(k):
        @pl.when(k == 1)
        def _():
            two_go(pw, 1)

        b, i = k // nrb, k % nrb
        h, off = i // (half // rblk), i % (half // rblk)
        rows = pl.ds(pl.multiple_of(off * rblk, rblk), rblk)
        flat = pl.ds(pl.multiple_of(i * rblk, rblk), rblk)
        u = dot(N2[h, rows, :], Wf[b].reshape(width, width)) + VF[pl.ds(FCB + b, 1), :]
        uu = u * u
        a = 0.5 * jnp.tanh(u * (root + (root * 0.044715) * uu)) + 0.5
        H[b, flat, :] = (u * a).astype(LOW)
        GPR[b, flat, :] = a * (1.0 + (1.0 - a) * (u * (2.0 * root + (2.0 * root * 0.134145) * uu)))

    def weight_grad(left_t, right, G, first, last):
        @pl.loop(0, 2)
        def _(b):
            g = dot(left_t[...], right[b, :, first:last])
            G[b, :, :, :, first:last] = g.astype(LOW).reshape(ZN, XN, width // GROUPS, last - first)

    every = pl.ds(0, width)
    by_rows = [pairs[0] + (pl.ds(0, third), every), pairs[1] + (pl.ds(third, 2 * third), every)]

    def reduce_copies(G, plan, A1, B1, A2, B2, R3):
        steps = []
        for a, b, r, cols in plan:
            one = [
                copy(G.at[:, :, ox, a, cols], A1.at[:, :, r, cols], xdev),
                copy(G.at[oy, :, :, b, cols], B1.at[:, :, r, cols], ydev),
            ]
            two = [
                copy(G.at[oy, :, x, a, cols], A2.at[:, r, cols], ydev),
                copy(G.at[y, :, ox, b, cols], B2.at[:, r, cols], xdev),
            ]
            q = pl.ds(a.start, a.size + b.size)
            three = [
                Group(
                    [(G.at[y, (z + k) % ZN, x, q, cols], R3.at[k - 1, q, cols], zdev(k)) for k in range(1, ZN)],
                    R3.at[:, q, cols],
                )
            ]
            steps.append((a, b, r, cols, one, two, three))

        def add(target, source):
            target[...] = (target[...].astype(FULL) + source[...].astype(FULL)).astype(LOW)

        def go(i):
            start(steps[i][4])

        def second(i):
            a, b, r, cols, one, two, three = steps[i]
            landed(one[:1])

            @pl.loop(0, ZN)
            def _(k):
                add(G.at[oy, k, x, a, cols], A1.at[oy, k, r, cols])

            start(two[:1])
            landed(one[1:])

            @pl.loop(0, ZN)
            def _(k):
                add(G.at[y, k, ox, b, cols], B1.at[k, ox, r, cols])

            start(two[1:])

            @pl.loop(0, ZN)
            def _(k):
                add(G.at[y, k, x, a, cols], A1.at[y, k, r, cols])
                add(G.at[y, k, x, b, cols], B1.at[k, x, r, cols])

        def third_step(i):
            a, b, r, cols, one, two, three = steps[i]
            landed(two)

            @pl.loop(0, ZN)
            def _(k):
                add(G.at[y, k, x, a, cols], A2.at[k, r, cols])
                add(G.at[y, k, x, b, cols], B2.at[k, r, cols])

            start(three)

        def last(i, out):
            a, b, r, cols, one, two, three = steps[i]
            landed(three)
            for q in (a, b):
                v = G[y, z, x, q, cols].astype(FULL)
                for k in range(ZN - 1):
                    v = v + R3[k, q, cols].astype(FULL)
                out[q, cols] = v

        return go, second, third_step, last

    def reduce_wide(G, plan, A1, B1, A2, B2, A3, B3, EA, EB):
        steps = []
        for a, b, r, cols in plan:
            one = [
                copy(G.at[oy, :, :, a, cols], A1.at[:, :, r, cols], ydev),
                copy(G.at[:, :, ox, b, cols], B1.at[:, :, r, cols], xdev),
            ]
            two = [
                ZReduce(
                    lambda i, a=a, cols=cols: G.at[y, i, :, a, cols],
                    lambda k, r=r, cols=cols: A2.at[k, :, r, cols],
                    EA.at[:, r, cols],
                ),
                ZReduce(
                    lambda i, b=b, cols=cols: G.at[:, i, x, b, cols],
                    lambda k, r=r, cols=cols: B2.at[k, :, r, cols],
                    EB.at[:, r, cols],
                ),
            ]
            three = [
                copy(G.at[y, z, ox, a, cols], A3.at[r, cols], xdev),
                copy(G.at[oy, z, x, b, cols], B3.at[r, cols], ydev),
            ]
            steps.append((a, b, r, cols, one, two, three))

        def add(target, sources):
            v = target[...].astype(FULL)
            for source in sources:
                v = v + source[...].astype(FULL)
            target[...] = v.astype(LOW)

        def go(i):
            start(steps[i][4])

        def second(i):
            a, b, r, cols, one, two, three = steps[i]
            landed(one)

            @pl.loop(0, ZN)
            def _(k):
                for j in range(2):
                    add(G.at[y, k, j, a, cols], [A1.at[k, j, r, cols]])
                    add(G.at[j, k, x, b, cols], [B1.at[j, k, r, cols]])

            start(two)

        def middle(i):
            for m in steps[i][5]:
                m.middle()

        def third_step(i):
            a, b, r, cols, one, two, three = steps[i]
            landed(two)
            for j in range(2):
                add(G.at[y, z, j, a, cols], [A2.at[k, j, r, cols] for k in range(ZN - 1)])
                add(G.at[j, z, x, b, cols], [B2.at[k, j, r, cols] for k in range(ZN - 1)])
            start(three)

        def last(i, out):
            a, b, r, cols, one, two, three = steps[i]
            landed(three)
            for q, R in ((a, A3), (b, B3)):
                out[q, cols] = G[y, z, x, q, cols].astype(FULL) + R[r, cols].astype(FULL)

        return go, second, third_step, last, middle

    rp = reduce_wide(Gp, by_rows, RpA1, RpB1, RpA2, RpB2, RpA3, RpB3, RpEA, RpEB)
    rf = reduce_copies(Gf, by_rows, RfA1, RfB1, RfA2, RfB2, Rf3)
    weight_grad(T0, H, Gp, 0, width)
    rp[0](0)
    transpose_all(N2, T1)
    all_in(pw)
    rp[0](1)


    def pair_nt(A, W, columns):
        def block(flat):
            return dot_nt(A[0, flat, :columns], W[0].reshape(width, W.shape[-1])) + dot_nt(
                A[1, flat, :columns], W[1].reshape(width, W.shape[-1])
            )

        return block

    @pl.loop(0, 4)
    def _(k):
        b, h = k // 2, k % 2
        flat = pl.ds(pl.multiple_of(h * half, half), half)
        g = (dot(COT[h], Wp[b].reshape(width, width)) * GPR[b, flat, :]).astype(LOW)
        PG[b, flat, :] = g
        VG[pl.ds(FCB + b, 1), :] += jnp.sum(g.astype(FULL), axis=0, keepdims=True)

    p2_c = [copy(parts[3], V1, cdev)]
    split_rows(pair_nt(PG, Wf, width), parts[3], parts[0], p2_c)
    rp[1](0)
    weight_grad(T1, PG, Gf, 0, width)
    rf[0](0)
    rf[0](1)
    landed(p2_c)

    sent(n2_c)

    def norm_back(dy, n, rstd, gain):
        e = dy * gain
        return (e - jnp.mean(e, axis=-1, keepdims=True) - n * jnp.mean(e * n, axis=-1, keepdims=True)) * rstd

    def add_row(i, v):
        VG[i : i + 1, :] += jnp.sum(v, axis=0, keepdims=True)

    @pl.loop(0, half // 128)
    def _(i):
        r = row_tile(i)
        dy = GPR[0, r, :] + V1[r, :]
        n = N2F[r, :]
        add_row(GAIN2, dy * n)
        add_row(SHIFT2, dy)
        cot = COT[c, r, :].astype(FULL)
        add_row(PROJB, cot)
        g = cot + norm_back(dy, n, RS[r, 1:2], vrow(GAIN2))
        N2F[r, :] = g
        low = g.astype(LOW)
        add_row(OUTB, low.astype(FULL))
        N2[c, r, :] = low

    ag_c = [copy(N2.at[c], N2.at[c], cdev)]
    start(ag_c)

    def vector_copies(first, last):
        r = pl.ds(first, last - first)
        over_z = [Group([(VG.at[r], VZ.at[k - 1, r], zdev(k)) for k in range(1, ZN)], VZ.at[:, r])]
        mine = VO.at[(y * 2 + x) * 2 + c, r]
        return r, over_z, mine, [Group([(mine, mine, d) for d in near], VO.at[pl.ds(0, 7), r])]

    def vector_second(v):
        r, over_z, mine, over_near = v
        landed(over_z)
        mine[...] = VG[r, :] + VZ[0, r, :] + VZ[1, r, :] + VZ[2, r, :]
        start(over_near)

    def vector_last(v):
        r, over_z, mine, over_near = v
        landed(over_near)
        for core in range(2):
            vo_ref[core, r, :] = (VO[core, r, :] + VO[2 + core, r, :]) + (VO[4 + core, r, :] + VO[6 + core, r, :])

    late, early = vector_copies(0, 4), vector_copies(8, VEC)
    start(early[1])
    pm_c = [copy(parts[1], V0, cdev)]
    split_rows(pair_nt(H, Wp, width), parts[1], MID, pm_c, MID)
    rp[1](1)
    transpose_all(N1, T1)
    landed(ag_c)
    landed(pm_c)

    @pl.loop(0, half // 128)
    def _(i):
        r = row_tile(i)
        TOK[r, :] = (MID[r, :] + (V0[r, :] + vrow(PROJB))).astype(LOW)

    out_c = [pltpu.make_async_copy(TOK, bo_h, ls.at[0]), pltpu.make_async_copy(N1.at[c], ig_h, ls.at[1])]
    out_c[0].start()

    @pl.loop(0, nrb)
    def _(i):
        h, off = i // (half // rblk), i % (half // rblk)
        rows = pl.ds(pl.multiple_of(off * rblk, rblk), rblk)
        flat = pl.ds(pl.multiple_of(i * rblk, rblk), rblk)
        g = dot(N2[h, rows, :], Wo[...].reshape(width, Wo.shape[-1])).astype(LOW)
        row = lax.broadcasted_iota(jnp.int32, (8, 128), 0)
        lane = lax.broadcasted_iota(jnp.int32, (8, 128), 1)
        pick = jnp.where(lane // HD == row, 1.0, 0.0).astype(LOW)
        for p in range(3):
            gp = tile(g, p)
            DO[p, flat, :] = gp
            prod = gp.astype(FULL) * CTX[p, flat, :].astype(FULL)
            high = prod.astype(LOW)
            rest = (prod - high.astype(FULL)).astype(LOW)
            d = dot_nt(pick, high) + dot_nt(pick, rest)
            for e in range(2):
                DELR[2 * p + e, :, flat] = d[e : e + 1, :]

    transpose_all(N2, T0)

    @pl.loop(0, 2)
    def _(m):
        rows = pl.ds(pl.multiple_of(m * (width // 2), width // 2), width // 2)
        g = dot(T0[rows, :], wide(CTX, pl.ds(0, seq_len)))
        g = g.astype(LOW).reshape(ZN // 2, XN, 2, width // (2 * GROUPS), Wo.shape[-1])
        Go[pl.ds(m * (ZN // 2), ZN // 2)] = g

    ro = [
        [copy(Go.at[:, :, oy], Ro1, ydev)],
        [copy(Go.at[:, ox, y], Ro2, xdev)],
        [Group([(Go.at[(z + k) % ZN, x, y], Ro3.at[k - 1], zdev(k)) for k in range(1, ZN)], Ro3)],
        [Group([(go_ref.at[t], go_ref.at[t], d) for d in (cdev, ydev, gdev)], go_ref.at[pl.ds(0, 3)])],
    ]
    start(ro[0])

    def ro_second():
        landed(ro[0])

        @pl.loop(0, ZN)
        def _(k):
            for i in range(XN):
                Go[k, i, y] = (Go[k, i, y].astype(FULL) + Ro1[k, i].astype(FULL)).astype(LOW)

        start(ro[1])

    def ro_third():
        landed(ro[1])

        @pl.loop(0, ZN)
        def _(k):
            Go[k, x, y] = (Go[k, x, y].astype(FULL) + Ro2[k].astype(FULL)).astype(LOW)

        start(ro[2])

    def ro_last():
        landed(ro[2])
        v = Go[z, x, y].astype(FULL)
        for k in range(ZN - 1):
            v = v + Ro3[k].astype(FULL)
        go_ref[t] = v
        start(ro[3])

    def attention_back(p, plan):
        DQ[...] = jnp.zeros(DQ.shape, FULL)
        for b in range(nrb):
            rows = pl.ds(b * rblk, rblk)
            first = 0 if b * rblk < half else b * rblk
            n = seq_len - first
            keys, values = KP[p, rows, :], VP[p, rows, :]
            queries, grads = QP[p, first:, :], DO[p, first:, :]
            key = b * rblk + lax.broadcasted_iota(jnp.int32, (rblk, 1), 0)
            limit = jnp.where(key < prefix, 0, key)
            shut = (b + 1) * rblk - first
            query = first + lax.broadcasted_iota(jnp.int32, (rblk, shut), 1)
            dk, dv = [], []
            for e in range(2):
                ke, ve = lane_part(keys, e), lane_part(values, e)
                sc = dot_nt(ke, queries) - LSER[2 * p + e, :, first:]
                head = jnp.where(query >= limit, sc[:, :shut], -1e30)
                w = jnp.exp(jnp.concatenate([head, sc[:, shut:]], axis=1) if shut < n else head)
                dw = dot_nt(ve, grads) - DELR[2 * p + e, :, first:]
                ds = (w * dw).astype(LOW)
                dv.append(dot(w.astype(LOW), grads))
                dk.append(dot(ds, queries))
                DQ[first:, :] += dot_tn(ds, ke)
            KP[p, rows, :] = jnp.where(low_lanes(dk[0]), dk[0], dk[1]).astype(LOW)
            VP[p, rows, :] = jnp.where(low_lanes(dv[0]), dv[0], dv[1]).astype(LOW)
            meanwhile(p, b, plan)
        QP[p, :, :] = (DQ[...] * 0.125).astype(LOW)

    away = {
        (0, 0): [lambda: rp[4](0), lambda: rf[1](0)],
        (1, 0): [lambda: rf[1](1)],
        (1, 1): [lambda: rp[4](1)],
        (1, 2): [lambda: rf[2](0), ro_second],
    }

    @pl.loop(0, 2)
    def _(p):
        attention_back(p, away)

    packed = Wq.shape[-1]
    sent_all(fw)

    @pl.loop(0, nrb)
    def _(i):
        flat = pl.ds(pl.multiple_of(i * rblk, rblk), rblk)
        for b in range(2):
            for k, ref in enumerate((QP, KP, VP)):
                g = ref[b, flat, :]
                H[b, flat, k * 128 : (k + 1) * 128] = g
                VG[QKVB + b : QKVB + b + 1, k * 128 : (k + 1) * 128] += jnp.sum(g.astype(FULL), axis=0, keepdims=True)

    by_lanes = [(pl.ds(0, hr), pl.ds(hr, hr), pl.ds(0, hr), pl.ds(0, 384))]
    rest = pl.ds(384, packed - 384)
    by_lanes += [pairs[1] + (pl.ds(third, 2 * third), rest), pairs[0] + (pl.ds(0, third), rest)]
    weight_grad(T1, H, Wf, 0, 384)
    rq = reduce_copies(Wf, by_lanes, RqA1, RqB1, RqA2, RqB2, Rq3)
    rq[0](0)
    away = {
        (2, 0): [lambda: rf[2](1), lambda: rp[2](0)],
        (2, 1): [ro_third],
        (2, 3): [lambda: rq[1](0)],
    }
    attention_back(2, away)

    @pl.loop(0, nrb)
    def _(i):
        flat = pl.ds(pl.multiple_of(i * rblk, rblk), rblk)
        q, k, v = (ref[2, flat, :].astype(FULL) for ref in (QP, KP, VP))
        first = low_lanes(q)
        packs = (
            (jnp.where(first, q, roll(k)), jnp.where(first, v, 0.0)),
            (jnp.where(first, roll(q), k), jnp.where(first, roll(v), 0.0)),
        )
        for b in range(2):
            for j in range(2):
                at_j = slice(384 + 128 * j, 512 + 128 * j)
                H[b, flat, at_j] = packs[b][j].astype(LOW)
                VG[QKVB + b : QKVB + b + 1, at_j] += jnp.sum(packs[b][j], axis=0, keepdims=True)

    weight_grad(T1, H, Wf, 384, packed)
    rq[0](1)
    rq[0](2)

    p1_c = [copy(parts[1], V1, cdev)]
    sent(pm_c)
    split_rows(pair_nt(H, Wq, packed), parts[1], parts[2], p1_c)
    rp[2](1)
    landed(p1_c)

    sent(n1_c)

    @pl.loop(0, half // 128)
    def _(i):
        r = row_tile(i)
        dy = GPR[1, r, :] + V1[r, :]
        n = N1F[r, :]
        add_row(GAIN1, dy * n)
        add_row(SHIFT1, dy)
        N1[c, r, :] = (N2F[r, :] + norm_back(dy, n, RS[r, 0:1], vrow(GAIN1))).astype(LOW)

    out_c[1].start()

    start(late[1])
    rq[2](0)
    vector_second(early)
    rq[1](1)
    rq[1](2)
    ro_last()
    gp_ref, gf_ref = MID.at[pl.ds(0, 2 * hr)], MID.at[pl.ds(2 * hr, 2 * hr)]
    out_c += [pltpu.make_async_copy(gp_ref, gp_h, ls.at[2]), pltpu.make_async_copy(gf_ref, gf_h, ls.at[3])]
    rp[3](0, gp_ref)
    rp[3](1, gp_ref)
    out_c[2].start()
    rf[3](0, gf_ref)
    rf[3](1, gf_ref)
    out_c[3].start()
    rq[2](1)
    rq[2](2)
    vector_second(late)
    vector_last(early)
    landed(ro[3])
    out_c += [
        pltpu.make_async_copy(a, b, ls.at[4 + i]) for i, (a, b) in enumerate(((go_ref, go_h), (gq_ref, gq_h), (vo_ref, vo_h)))
    ]
    out_c[4].start()
    rq[3](0, gq_ref)
    vector_last(late)
    out_c[6].start()
    rq[3](1, gq_ref)
    rq[3](2, gq_ref)
    out_c[5].start()

    waited = {id(m) for m in n2_c + pm_c + n1_c}
    for step in fw:
        for group in step:
            waited |= {id(m) for m in group}
    sent([m for m in pending if id(m) not in waited])
    for cp in out_c:
        cp.wait()


def gather_groups(v, axis, repeat, groups):
    if repeat == 1:
        return v
    return lax.all_gather(v, "dp", axis=axis, axis_index_groups=groups, tiled=True)


def scatter_groups(v, axis, repeat, groups):
    if repeat == 1:
        return v
    return lax.psum_scatter(v, "dp", scatter_dimension=axis, axis_index_groups=groups, tiled=True)


def on_device(
    dp_size,
    tokens,
    prefix,
    cotangent,
    first_gain,
    first_shift,
    qkv_weight,
    qv_bias,
    out_weight,
    out_bias,
    second_gain,
    second_shift,
    fc_weight,
    fc_bias,
    proj_weight,
    proj_bias,
):
    repeat = dp_size // GROUPS
    groups = [[g * repeat + i for i in range(repeat)] for g in range(GROUPS)]
    half, width = tokens.shape
    seq_len = 2 * half

    def whole(v, axis):
        return gather_groups(v.astype(LOW), axis, repeat, groups).astype(FULL) if repeat > 1 else v

    params = [
        whole(first_gain, 0), whole(first_shift, 0), whole(qkv_weight, 1), whole(qv_bias, 1), whole(out_weight, 1),
        whole(out_bias, 0), whole(second_gain, 0), whole(second_shift, 0), whole(fc_weight, 0), whole(fc_bias, 0),
        whole(proj_weight, 1), whole(proj_bias, 0),
    ]
    params[4], params[10] = params[4].T, params[10].T
    rows = params[8].shape[0]
    cols = params[2].shape[2]
    units = params[8].shape[1]
    pair = 2 * HD
    packed, own = 3 * cols + HD, 2 * cols
    hr = rows // 2
    ANY = pl.BlockSpec(memory_space=pl.ANY)

    def reduce_space(lanes):
        return [
            pltpu.VMEM((2, ZN, hr, lanes), LOW),
            pltpu.VMEM((ZN, XN, hr, lanes), LOW),
            pltpu.VMEM((ZN, hr, lanes), LOW),
            pltpu.VMEM((ZN, hr, lanes), LOW),
            pltpu.VMEM((ZN - 1, rows, lanes), LOW),
        ]

    token_low = pltpu.VMEM((2, half, width), LOW)
    token_full = pltpu.VMEM((half, width), FULL)
    unit_low = pltpu.VMEM((2, seq_len, width), LOW)
    heads = pltpu.VMEM((3, seq_len, pair), LOW)
    scratch = (
        [
            pltpu.VMEM((2, ZN, XN, rows, packed), LOW),
            pltpu.VMEM((ZN, XN, 2, hr, own), LOW),
            pltpu.VMEM((2, ZN, XN, rows, width), LOW),
            pltpu.VMEM((2, ZN, XN, rows, width), LOW),
            pltpu.VMEM((ZN, XN, 2, hr, own), LOW),
            pltpu.VMEM((2, ZN, XN, rows, width), LOW),
            pltpu.VMEM((2, ZN, XN, rows, width), LOW),
        ]
        + reduce_space(packed)
        + reduce_space(width)
        + [
            pltpu.VMEM((ZN, XN, hr, width), LOW),
            pltpu.VMEM((2, ZN, hr, width), LOW),
            pltpu.VMEM((ZN - 1, XN, hr, width), LOW),
            pltpu.VMEM((ZN - 1, 2, hr, width), LOW),
            pltpu.VMEM((hr, width), LOW),
            pltpu.VMEM((hr, width), LOW),
            pltpu.VMEM((XN, hr, width), LOW),
            pltpu.VMEM((2, hr, width), LOW),
        ]
        + [
            pltpu.VMEM((ZN, XN, hr, own), LOW),
            pltpu.VMEM((ZN, hr, own), LOW),
            pltpu.VMEM((ZN - 1, hr, own), LOW),
        ]
        + [
            pltpu.VMEM((half, width), LOW),
            token_low,
            token_full,
            token_full,
            pltpu.VMEM((half, 128), FULL),
            token_low,
            token_low,
            pltpu.VMEM((width, seq_len), LOW),
            pltpu.VMEM((width, seq_len), LOW),
        ]
        + [heads] * 5
        + [
            pltpu.VMEM((seq_len, pair), FULL),
            pltpu.VMEM((6, 1, seq_len), FULL),
            pltpu.VMEM((6, 1, seq_len), FULL),
        ]
        + [token_full] * 3
        + [unit_low, pltpu.VMEM((2, seq_len, width), FULL), unit_low]
        + [
            pltpu.VMEM((8, rows), FULL),
            pltpu.VMEM((2, rows), FULL),
            pltpu.VMEM((1, 4 * rows), FULL),
            pltpu.VMEM((3, rows, cols), FULL),
            pltpu.VMEM((2, hr, own), LOW),
            pltpu.VMEM((3, half, pair), LOW),
            pltpu.VMEM((ZN, XN, 2, hr, own), LOW),
            pltpu.VMEM((GROUPS, VEC, 128), LOW),
            pltpu.VMEM((VEC, width), FULL),
            pltpu.VMEM((VEC, width), FULL),
            pltpu.VMEM((ZN - 1, VEC, width), FULL),
        ]
        + [
            pltpu.VMEM((8, VEC, width), FULL),
            pltpu.VMEM((rows, packed), FULL),
            pltpu.VMEM((4, hr, own), FULL),
            pltpu.VMEM((2, VEC, width), FULL),
            pltpu.SMEM(prefix.shape, prefix.dtype),
        ]
        + [
            pltpu.SemaphoreType.DMA((SEMS,)),
            pltpu.SemaphoreType.DMA((SEMS,)),
            pltpu.SemaphoreType.DMA((16,)),
        ]
    )
    out_shape = [
        jax.ShapeDtypeStruct((half, width), LOW),
        jax.ShapeDtypeStruct((half, width), LOW),
        jax.ShapeDtypeStruct((rows, packed), FULL),
        jax.ShapeDtypeStruct((4, hr, own), FULL),
        jax.ShapeDtypeStruct((rows, width), FULL),
        jax.ShapeDtypeStruct((rows, width), FULL),
        jax.ShapeDtypeStruct((2, VEC, width), FULL),
    ]
    grown = pl.pallas_call(
        functools.partial(block_kernel, repeat, seq_len),
        out_shape=out_shape,
        in_specs=[ANY] * 15,
        out_specs=[ANY] * 7,
        scratch_shapes=scratch,
        compiler_params=pltpu.CompilerParams(
            collective_id=0, has_side_effects=True, vmem_limit_bytes=62 * 1024 * 1024
        ),
    )(tokens, prefix, cotangent, *params)

    vector = jax.ShapeDtypeStruct((rows,), FULL)
    results = pl.pallas_call(
        functools.partial(unpack_kernel, repeat),
        out_shape=[
            out_shape[0],
            out_shape[1],
            vector,
            vector,
            jax.ShapeDtypeStruct((3, rows, cols), FULL),
            jax.ShapeDtypeStruct((2, rows), FULL),
            jax.ShapeDtypeStruct((rows, width), FULL),
            vector,
            vector,
            vector,
            jax.ShapeDtypeStruct((rows, units), FULL),
            jax.ShapeDtypeStruct((4 * rows,), FULL),
            jax.ShapeDtypeStruct((rows, units), FULL),
            vector,
        ],
        in_specs=[ANY] * 7,
        out_specs=[ANY] * 14,
        scratch_shapes=[
            pltpu.VMEM((rows, packed), FULL),
            pltpu.VMEM((4, hr, own), FULL),
            pltpu.VMEM((2, VEC, width), FULL),
            pltpu.VMEM((3, rows, cols), FULL),
            pltpu.VMEM((rows, width), FULL),
            pltpu.VMEM((half, width), LOW),
            pltpu.VMEM((half, width), LOW),
            pltpu.VMEM((rows, units), FULL),
            pltpu.VMEM((rows, units), FULL),
            pltpu.VMEM((8, rows), FULL),
            pltpu.VMEM((2, rows), FULL),
            pltpu.VMEM((1, 4 * rows), FULL),
            pltpu.SemaphoreType.DMA((21,)),
        ],
        compiler_params=pltpu.CompilerParams(vmem_limit_bytes=62 * 1024 * 1024),
    )(*grown)
    results = [v.T if i in (6, 12) else v for i, v in enumerate(results)]
    along = (None, None, 0, 0, 1, 1, 1, 0, 0, 0, 0, 0, 1, 0)
    return tuple(
        v if repeat == 1 or axis is None else scatter_groups(v, axis, repeat, groups)
        for v, axis in zip(results, along, strict=True)
    )


def unpack_kernel(
    repeat, bo, ig, gq_h, go_h, gf, gp, vo_h,
    bo_out, ig_out, gain1, shift1, wq_h, qvb_h, wo_h, outb, gain2, shift2, wf, fcb_h, wp, projb,
    gq, go, vo, wq, wo, b1, b2, w1, w2, sv, sq, sf, sems,
):
    moves = [(vo_h, vo), (gq_h, gq), (go_h, go), (ig, b2), (bo, b1), (gf, w1), (gp, w2)]
    moves += [(wq, wq_h), (wo, wo_h), (b2, ig_out), (b1, bo_out), (w1, wf), (w2, wp)]
    vectors = ((GAIN1, gain1), (SHIFT1, shift1), (OUTB, outb), (GAIN2, gain2), (SHIFT2, shift2), (PROJB, projb))
    moves += [(sv.at[j], out) for j, (_, out) in enumerate(vectors)] + [(sq, qvb_h), (sf.at[0], fcb_h)]
    moves = [pltpu.make_async_copy(a, b, sems.at[i]) for i, (a, b) in enumerate(moves)]
    for cp in moves[:7]:
        cp.start()
    for i in range(3, 7):
        moves[i].wait()
        moves[i + 6].start()
    moves[1].wait()
    for k in range(3):
        wq[k] = jnp.concatenate(
            [gq[:, k * 128 : (k + 1) * 128], gq[:, 384 + k * HD : 384 + (k + 1) * HD]], axis=1
        )
    moves[7].start()
    moves[2].wait()
    m = [jnp.concatenate([go[core], go[2 + core]], axis=0) for core in range(2)]
    wo[...] = jnp.concatenate(
        [
            v
            for b in range(2)
            for core in range(2)
            for v in (m[core][:, b * 128 : (b + 1) * 128], m[core][:, 256 + b * HD : 256 + (b + 1) * HD])
        ],
        axis=1,
    )
    moves[8].start()
    moves[0].wait()
    s = lax.axis_index("dp") // repeat
    width = vo.shape[2]
    n = sv.shape[1]
    both = pltpu.roll(vo[0] + vo[1], (GROUPS - s) % GROUPS * n, 1)
    for j, (i, _) in enumerate(vectors):
        sv[j : j + 1, :] = both[i : i + 1, :n]
    owner = s // 2
    core, b, odd = owner % 2, owner // 2, s % 2
    place = lax.broadcasted_iota(jnp.int32, (1, width), 1)

    def lanes(v, first, last, shift):
        v = jnp.where((place >= first) & (place < last), v, 0.0)
        return pltpu.roll(v, shift % width, 1) if shift % width else v

    row = vo[core, pl.ds(QKVB + b, 1), :]
    q = lanes(row, 0, 128, 0) + lanes(row, 384, 448, -256)
    v = lanes(row, 256, 384, -256) + lanes(row, 512, 576, -384)
    back = (width - odd * n) % width
    sq[0:1, :] = pltpu.roll(q, back, 1)[:, :n]
    sq[1:2, :] = pltpu.roll(v, back, 1)[:, :n]
    row = vo[core, pl.ds(FCB + b, 1), :]
    sf[...] = pltpu.roll(row, odd * (width // 2), 1)[:, : width // 2]
    for i in range(13, 21):
        moves[i].start()
    for i in range(7, 21):
        moves[i].wait()


def solution(mesh):
    placed = (
        P(("dp", "tensor"), None),
        P("dp"),
        P(("dp", "tensor"), None),
        P("dp"),
        P("dp"),
        P(None, "dp", "tensor"),
        P(None, "dp"),
        P(None, "dp"),
        P("dp"),
        P("dp"),
        P("dp"),
        P("dp", "tensor"),
        P("dp"),
        P("tensor", "dp"),
        P("dp"),
    )
    return jax.shard_map(
        functools.partial(on_device, mesh.shape["dp"]),
        mesh=mesh,
        in_specs=placed,
        out_specs=(placed[0], placed[0]) + placed[3:],
        check_vma=False,
    )
```

```python
import functools
import math

import jax
import jax.numpy as jnp
from jax import lax
from jax.experimental import pallas as pl
from jax.experimental.pallas import tpu as pltpu
from jax.sharding import PartitionSpec as P

MESH = pl.DeviceIdType.MESH
LOW, FULL = jnp.bfloat16, jnp.float32
EPSILON = 1e-05
HD = 64
GROUPS, ZN, XN = 8, 4, 2
SEMS = 140
VEC = 16

GAIN1, SHIFT1, QKVB, OUTB, GAIN2, SHIFT2, PROJB, FCB = 0, 1, 2, 8, 9, 10, 11, 12


def dot(a, b):
    return jnp.dot(a, b, preferred_element_type=FULL)


def dot_nt(a, b):
    return lax.dot_general(a, b, (((1,), (1,)), ((), ())), preferred_element_type=FULL)


def dot_tn(a, b):
    return lax.dot_general(a, b, (((0,), (0,)), ((), ())), preferred_element_type=FULL)


def block_kernel(repeat, seq_len, *refs):
    (
        tok_h, prefix_h, cot_h, gain1_h, shift1_h, wq_h, qvb_h, wo_h, outb_h,
        gain2_h, shift2_h, wf_h, fcb_h, wp_h, projb_h,
        bo_h, ig_h, gq_h, go_h, gf_h, gp_h, vo_h,
        Wq, Wo, Wf, Wp, Go, Gp, Gf,
        RqA1, RqB1, RqA2, RqB2, Rq3,
        RfA1, RfB1, RfA2, RfB2, Rf3,
        RpA1, RpB1, RpA2, RpB2, RpA3, RpB3, RpEA, RpEB,
        Ro1A, Ro1B, Ro2A, Ro2B, Ro3,
        TOK, COT, N1F, N2F, RS, N1, N2, T0, T1,
        QP, KP, VP, CTX, DO, DQ, LSER, DELR,
        MID, V0, V1, H, GPR, PG,
        SV, SB, SC, SQ, SW, CTXP, WOP,
        VR, VF, VG, VZ, VO, gq_ref, go_ref, vo_ref, prefix_s,
        ss, rs, ls,
    ) = refs
    half = seq_len // 2
    width = TOK.shape[1]
    rblk = 256
    nrb = seq_len // rblk
    dp = lax.axis_index("dp")
    t = lax.axis_index("tensor")
    s, sub = dp // repeat, dp % repeat
    z, x = s // XN, s % XN
    y, c = t // 2, t % 2
    oy, oc, ox = 1 - y, 1 - c, 1 - x

    def at(zz, xx, tt):
        return ((zz * XN + xx) * repeat + sub, tt)

    def zdev(k):
        return at((z + k) % ZN, x, t)

    xdev = at(z, ox, t)
    ydev = at(z, x, oy * 2 + c)
    cdev = at(z, x, y * 2 + oc)
    gdev = at(z, x, oy * 2 + oc)
    near = [xdev, ydev, cdev, gdev] + [at(z, ox, i * 2 + j) for i, j in ((y, oc), (oy, c), (oy, oc))]
    others = [(((s + k) % GROUPS) * repeat + sub, t) for k in range(1, GROUPS)]

    count = [0]
    pending = []

    class Copy:
        def __init__(self, src, dst, dev, recv=None, alone=True):
            self.k = count[0]
            count[0] += 1
            self.parts = src, dst, dev, self.k if recv is None else recv.k
            if alone:
                pending.append(self)

        def made(self):
            src, dst, dev, recv = self.parts
            return pltpu.make_async_remote_copy(
                src_ref=src, dst_ref=dst, send_sem=ss.at[self.k], recv_sem=rs.at[recv],
                device_id=dev, device_id_type=MESH,
            )

        def start(self):
            self.made().start()

        def landed(self):
            self.made().wait_recv()

        def sent(self):
            self.made().wait_send()

    class Group:
        def __init__(self, moves, every):
            k = count[0]
            count[0] += 1
            self.moves = [Copy(*m, alone=False) for m in moves]
            for m in self.moves:
                m.k, m.parts = k, m.parts[:3] + (k,)
            count[0] = k + 1
            self.every = Copy(every, every, moves[0][2], alone=False)
            self.every.k, self.every.parts = k, self.every.parts[:3] + (k,)
            count[0] = k + 1
            pending.append(self)

        def start(self):
            for m in self.moves:
                m.start()

        def landed(self):
            self.every.landed()

        def sent(self):
            self.every.sent()

    class ZGather:
        def __init__(self, block):
            self.to = [Copy(block(z), block(z), zdev(k), alone=False) for k in range(1, ZN)]
            self.up = Copy(block(0), block(0), at(3, x, t), self.to[2], False)
            self.down = Copy(block(3), block(3), at(0, x, t), self.to[0], False)
            pending.append(self)

        def each(self, act):
            act(self.to[1])
            pl.when(z != 3)(lambda: act(self.to[0]))
            pl.when(z != 0)(lambda: act(self.to[2]))

        def start(self):
            self.each(lambda m: m.start())

        def middle(self):
            def go_on(onward):
                landed(self.to[1:2])
                onward.start()

            pl.when(z == 2)(lambda: go_on(self.up))
            pl.when(z == 1)(lambda: go_on(self.down))

        def landed(self):
            pl.when((z == 0) | (z == 3))(self.to[1].landed)
            self.to[0].landed()
            self.to[2].landed()

        def sent(self):
            self.each(lambda m: m.sent())
            pl.when(z == 2)(self.up.sent)
            pl.when(z == 1)(self.down.sent)

    class ZReduce:
        def __init__(self, block, arrived, extra):
            self.block, self.extra = block, extra
            self.to = [Copy(block((z + k) % ZN), arrived(k - 1), zdev(k), alone=False) for k in range(1, ZN)]
            self.up = Copy(block(3), extra, at(1, x, t), alone=False)
            self.down = Copy(block(0), extra, at(2, x, t), alone=False)
            pending.append(self)

            def none(slot):
                arrived(slot)[...] = jnp.zeros(extra.shape, LOW)

            pl.when(z == 0)(lambda: none(0))
            pl.when(z == 3)(lambda: none(2))

        def start(self):
            pl.when(z != 3)(self.to[0].start)
            pl.when(z != 0)(self.to[2].start)
            pl.when(z == 0)(self.up.start)
            pl.when(z == 3)(self.down.start)
            pl.when((z == 0) | (z == 3))(self.to[1].start)

        def middle(self):
            def go_on(arrival, owner):
                landed([arrival])
                target = self.block(owner)
                target[...] = (target[...].astype(FULL) + self.extra[...].astype(FULL)).astype(LOW)
                self.to[1].start()

            pl.when(z == 1)(lambda: go_on(self.up, 3))
            pl.when(z == 2)(lambda: go_on(self.down, 0))

        def landed(self):
            self.to[1].landed()
            pl.when(z != 0)(self.to[0].landed)
            pl.when(z != 3)(self.to[2].landed)

        def sent(self):
            self.to[1].sent()
            pl.when(z != 3)(self.to[0].sent)
            pl.when(z != 0)(self.to[2].sent)
            pl.when(z == 0)(self.up.sent)
            pl.when(z == 3)(self.down.sent)

    def copy(src, dst, dev):
        return Copy(src, dst, dev)

    def start(moves):
        for m in moves:
            m.start()

    def landed(moves):
        for m in moves:
            m.landed()

    def sent(moves):
        for m in moves:
            m.sent()

    barrier = pltpu.get_barrier_semaphore()
    peers = others + [d for i, d in enumerate(near) if i != 0]
    for d in peers:
        pl.semaphore_signal(barrier, inc=1, device_id=d, device_id_type=MESH)

    SO, SF, SP = (GPR.at[0, pl.ds(i * wo_h.shape[0], wo_h.shape[0])] for i in range(3))
    brought = [
        (wq_h, SQ), (qvb_h, SB), (fcb_h, SC.at[0]),
        (gain1_h, SV.at[0]), (shift1_h, SV.at[1]), (outb_h, SV.at[2]),
        (gain2_h, SV.at[3]), (shift2_h, SV.at[4]), (projb_h, SV.at[5]),
        (wo_h, SO), (tok_h, TOK), (cot_h, COT.at[c]), (wf_h, SF), (wp_h, SP),
        (prefix_h, prefix_s),
    ]
    local = [pltpu.make_async_copy(a, b, ls.at[i]) for i, (a, b) in enumerate(brought)]
    for cp in local:
        cp.start()

    lanes96 = SV.shape[1]
    VG[...] = jnp.zeros(VG.shape, FULL)
    for cp in local[1:9]:
        cp.wait()
    VG[0:6, :lanes96] = SV[0:6, :]
    VG[6:8, :lanes96] = SB[...]
    for j in range(4):
        VG[8 + j : 9 + j, :lanes96] = SC[:, j * lanes96 : (j + 1) * lanes96]
    VR[s] = VG[:, :128].astype(LOW)
    VG[...] = jnp.zeros(VG.shape, FULL)
    local[0].wait()
    q3 = SQ[...]
    Wq[y, z, x] = jnp.concatenate(
        [q3[0, :, :128], q3[1, :, :128], q3[2, :, :128]]
        + [q3[k, :, 128:] for k in range(3)]
        + [jnp.zeros((q3.shape[1], HD), FULL)],
        axis=1,
    ).astype(LOW)
    pl.semaphore_wait(barrier, len(peers))

    vec_c = [Group([(VR.at[s], VR.at[s], d) for d in others], VR.at[pl.ds(0, GROUPS - 1)])]
    cot_c = [copy(COT.at[c], COT.at[c], cdev)]
    hr = wq_h.shape[1] // 2
    third = hr // 3
    pairs = (
        (pl.ds(0, third), pl.ds(third, third)),
        (pl.ds(2 * third, 2 * third), pl.ds(4 * third, 2 * third)),
    )

    thin = [(pl.ds(2 * i * third, third), pl.ds((2 * i + 1) * third, third)) for i in range(3)]

    def gather(W, pairs):
        steps = []
        for a, b in pairs:
            r = pl.ds(a.start, a.size + b.size)
            mine = W.at[y, z, x, r]
            zs = [Group([(mine, mine, zdev(k)) for k in range(1, ZN)], W.at[y, pl.ds(0, ZN - 1), x, r])]
            one = [
                copy(W.at[y, :, x, a], W.at[y, :, x, a], xdev),
                copy(W.at[y, :, x, b], W.at[y, :, x, b], ydev),
            ]
            two = [
                copy(W.at[y, :, :, a], W.at[y, :, :, a], ydev),
                copy(W.at[:, :, x, b], W.at[:, :, x, b], xdev),
            ]
            steps.append((zs, one, two))
        return steps

    def gather_wide(W):
        steps = []
        for a, b in pairs:
            near = [
                copy(W.at[y, z, x, a], W.at[y, z, x, a], xdev),
                copy(W.at[y, z, x, b], W.at[y, z, x, b], ydev),
            ]
            zs = [ZGather(lambda i, a=a: W.at[y, i, :, a]), ZGather(lambda i, b=b: W.at[:, i, x, b])]
            far = [
                copy(W.at[y, :, :, a], W.at[y, :, :, a], ydev),
                copy(W.at[:, :, x, b], W.at[:, :, x, b], xdev),
            ]
            steps.append((near, zs, far))
        return steps

    oa, ob = pl.ds(0, 2 * third), pl.ds(2 * third, third)
    ow = [
        (
            [Group([(Wo.at[z, x, y], Wo.at[z, x, y], zdev(k)) for k in range(1, ZN)], Wo.at[pl.ds(0, ZN - 1), x, y])],
            [
                copy(Wo.at[:, x, y, oa], Wo.at[:, x, y, oa], xdev),
                copy(Wo.at[:, x, y, ob], Wo.at[:, x, y, ob], ydev),
            ],
            [
                copy(Wo.at[:, :, y, oa], Wo.at[:, :, y, oa], ydev),
                copy(Wo.at[:, x, :, ob], Wo.at[:, x, :, ob], xdev),
            ],
        )
    ]
    qw, pw, fw = gather(Wq, thin), gather_wide(Wp), gather(Wf, thin)

    def z_go(w, i):
        start(w[i][0])

    def one_go(w, i):
        landed(w[i][0])
        start(w[i][1])

    def two_go(w, i):
        n = len(w[i][1]) // len(w[i][2])
        for k, after in enumerate(w[i][2]):
            landed(w[i][1][k * n : (k + 1) * n])
            start([after])

    def all_in(w):
        for step in w:
            landed(step[2])

    def sent_all(w):
        for step in w:
            for group in step:
                sent(group)

    start(vec_c)
    z_go(qw, 0)
    local[9].wait()
    turned = pltpu.roll(SO[...], (width - c * (width // 4)) % width, 1)
    last = jnp.concatenate([turned[:, 128:192], turned[:, 512:576]], axis=1)
    mine = jnp.concatenate([turned[:, 0:128], turned[:, 384:512], last], axis=1).astype(LOW)
    SW[0] = mine[: SW.shape[1]]
    SW[1] = mine[SW.shape[1] :]
    Wo[z, x, y] = SW[y]
    local[12].wait()
    Wf[y, z, x] = SF[...].astype(LOW)
    local[13].wait()
    Wp[y, z, x] = SP[...].astype(LOW)
    local[10].wait()
    local[11].wait()
    local[14].wait()
    z_go(pw, 0)
    z_go(pw, 1)
    start(cot_c)

    def row_tile(i, n=128):
        return pl.ds(pl.multiple_of(i * n, n), n)

    @pl.loop(0, half // 128)
    def _(i):
        r = row_tile(i)
        v = TOK[r, :].astype(FULL)
        v = v - jnp.mean(v, axis=-1, keepdims=True)
        rstd = lax.rsqrt(jnp.mean(v * v, axis=-1, keepdims=True) + EPSILON)
        N1F[r, :] = v * rstd
        RS[r, 0:1] = rstd

    z_go(qw, 1)
    landed(vec_c)

    def widen(v):
        return jnp.concatenate([v, jnp.zeros((v.shape[0], width - v.shape[1]), FULL)], axis=1)

    pieces = [widen(VR[g].astype(FULL)) for g in range(GROUPS)]
    plain = pieces[0]
    for g in range(1, GROUPS):
        plain = plain + pltpu.roll(pieces[g], g * lanes96, 1)
    VF[GAIN1 : SHIFT1 + 1, :] = plain[0:2]
    VF[OUTB : PROJB + 1, :] = plain[2:6]
    place = lax.broadcasted_iota(jnp.int32, (1, width), 1)

    def lanes(v, first, last, shift):
        v = jnp.where((place >= first) & (place < last), v, 0.0)
        return pltpu.roll(v, shift % width, 1) if shift % width else v

    for b in range(2):
        a0, a1 = (widen(VR[2 * (2 * b + c) + i].astype(FULL)) for i in range(2))
        a1 = pltpu.roll(a1, lanes96, 1)
        qb, vb = a0[6:7] + a1[6:7], a0[7:8] + a1[7:8]
        VF[QKVB + b : QKVB + b + 1, :] = (
            lanes(qb, 0, 128, 0) + lanes(qb, 128, 192, 256) + lanes(vb, 0, 128, 256) + lanes(vb, 128, 192, 384)
        )
        a1 = pltpu.roll(a1, 3 * lanes96, 1)
        row = a0[8:9] + a1[8:9]
        for j in range(1, 4):
            row = row + pltpu.roll(a0[8 + j : 9 + j] + a1[8 + j : 9 + j], j * lanes96, 1)
        VF[FCB + b : FCB + b + 1, :] = row

    def vrow(i):
        return VF[i : i + 1, :]

    @pl.loop(0, half // 128)
    def _(i):
        r = row_tile(i)
        N1[c, r, :] = (N1F[r, :] * vrow(GAIN1) + vrow(SHIFT1)).astype(LOW)

    n1_c = [copy(N1.at[c], N1.at[c], cdev)]
    start(n1_c)

    def transpose_all(source, target):
        @pl.loop(0, nrb)
        def _(i):
            h, off = i // (half // rblk), i % (half // rblk)
            rows = pl.ds(pl.multiple_of(off * rblk, rblk), rblk)
            cols = pl.ds(pl.multiple_of(i * rblk, rblk), rblk)
            for k in range(width // rblk):
                target[k * rblk : (k + 1) * rblk, cols] = source[h, rows, k * rblk : (k + 1) * rblk].T

    landed(cot_c)
    one_go(qw, 0)
    transpose_all(COT, T0)
    one_go(qw, 1)
    z_go(qw, 2)
    two_go(qw, 0)
    z_go(fw, 0)
    two_go(qw, 1)
    z_go(ow, 0)
    one_go(qw, 2)
    z_go(fw, 1)
    landed(n1_c)
    two_go(qw, 2)
    z_go(fw, 2)
    one_go(fw, 0)
    all_in(qw)

    def low_lanes(v):
        return lax.broadcasted_iota(jnp.int32, v.shape, 1) < HD

    def tile(v, i):
        return v[:, i * 128 : (i + 1) * 128]

    def roll(v):
        return pltpu.roll(v, HD, 1)

    @pl.loop(0, nrb)
    def _(i):
        h, off = i // (half // rblk), i % (half // rblk)
        rows = pl.ds(pl.multiple_of(off * rblk, rblk), rblk)
        out = pl.ds(pl.multiple_of(i * rblk, rblk), rblk)
        n = N1[h, rows, :]
        got = []
        for b in range(2):
            got.append(dot(n, Wq[b].reshape(width, Wq.shape[-1])) + VF[QKVB + b : QKVB + b + 1, : Wq.shape[-1]])
            QP[b, out, :] = (tile(got[b], 0).astype(LOW).astype(FULL) * 0.125).astype(LOW)
            KP[b, out, :] = tile(got[b], 1).astype(LOW)
            VP[b, out, :] = tile(got[b], 2).astype(LOW)
        first = low_lanes(tile(got[0], 3))
        q = jnp.where(first, tile(got[0], 3), roll(tile(got[1], 3)))
        QP[2, out, :] = (q.astype(LOW).astype(FULL) * 0.125).astype(LOW)
        KP[2, out, :] = jnp.where(first, roll(tile(got[0], 3)), tile(got[1], 3)).astype(LOW)
        VP[2, out, :] = jnp.where(first, tile(got[0], 4), roll(tile(got[1], 4))).astype(LOW)

        @pl.when(i == 0)
        def _():
            one_go(ow, 0)
            one_go(fw, 1)
            one_go(pw, 0)

        @pl.when(i == 2)
        def _():
            two_go(fw, 0)

    prefix = prefix_s[y]
    LSEC = DQ
    LSEC[...] = jnp.zeros(LSEC.shape, FULL)

    def lane_part(v, e):
        lane = lax.broadcasted_iota(jnp.int32, v.shape, 1)
        keep = lane < HD if e == 0 else lane >= HD
        return jnp.where(keep, v, jnp.zeros_like(v))

    def meanwhile(p, b, plan):
        for (pp, bb), steps in plan.items():
            if bb != b:
                continue
            if isinstance(p, int):
                for step in steps:
                    step()
            else:

                @pl.when(p == pp)
                def _(steps=steps):
                    for step in steps:
                        step()

    ctx_c = [copy(CTX.at[p, pl.ds(oc * half, half)], CTXP.at[p], cdev) for p in range(3)]
    wo_c = [copy(Wo, WOP, cdev)]

    def share_out():
        all_in(ow)
        start(wo_c)

    def pass_on(i):
        for m in pw[i][1]:
            m.middle()

    fetch = {
        (0, 0): [lambda: one_go(fw, 2), lambda: two_go(ow, 0)],
        (0, 1): [lambda: two_go(fw, 1), lambda: one_go(pw, 1)],
        (0, 3): [lambda: start(ctx_c[0:1])],
        (1, 1): [lambda: pass_on(0)],
        (1, 2): [lambda: two_go(fw, 2)],
        (1, 3): [lambda: start(ctx_c[1:2])],
        (2, 0): [lambda: two_go(pw, 0)],
        (2, 1): [share_out],
        (2, 3): [lambda: start(ctx_c[2:3]), lambda: pass_on(1)],
    }

    @pl.loop(0, 3)
    def _(p):
        for b in range(nrb):
            rows = pl.ds(b * rblk, rblk)
            cols = max(half, (b + 1) * rblk)
            q = QP[p, rows, :]
            keys, values = KP[p, :cols, :], VP[p, :cols, :]
            query = b * rblk + lax.broadcasted_iota(jnp.int32, (rblk, 1), 0)
            limit = jnp.maximum(prefix - 1, query)
            free = b * rblk
            key = free + lax.broadcasted_iota(jnp.int32, (rblk, cols - free), 1)
            parts = []
            for e in range(2):
                sc = dot_nt(lane_part(q, e), keys)
                tail = jnp.where(key <= limit, sc[:, free:], -1e30)
                sc = jnp.concatenate([sc[:, :free], tail], axis=1) if free else tail
                peak = jnp.max(sc, axis=-1, keepdims=True)
                w = jnp.exp(sc - peak)
                total = jnp.sum(w, axis=-1, keepdims=True)
                parts.append(dot(w.astype(LOW), values) * (1.0 / total))
                lane = lax.broadcasted_iota(jnp.int32, (rblk, 128), 1)
                LSEC[rows, :] = jnp.where(lane == 2 * p + e, peak + jnp.log(total), LSEC[rows, :])
            CTX[p, rows, :] = jnp.where(low_lanes(parts[0]), parts[0], parts[1]).astype(LOW)
            meanwhile(p, b, fetch)

    for b in range(nrb):
        lt = LSEC[b * rblk : (b + 1) * rblk, :].T
        for h in range(6):
            LSER[h, :, b * rblk : (b + 1) * rblk] = lt[h : h + 1, :]
    def wide(ref, rows):
        return jnp.concatenate([ref[0, rows, :], ref[1, rows, :], ref[2, rows, :]], axis=1)

    def split_rows(make_block, away, home, copies, plus=None):
        per = half // rblk
        for which, target in ((oc, away), (c, home)):

            @pl.loop(0, per)
            def _(j):
                rows = pl.ds(pl.multiple_of(j * rblk, rblk), rblk)
                block = make_block(pl.ds(pl.multiple_of((which * per + j) * rblk, rblk), rblk))
                target[rows, :] = block if plus is None or target is away else block + plus[rows, :]

            if target is away:
                start(copies)

    parts = [GPR.at[b, pl.ds(i * half, half)] for b in range(2) for i in range(2)]
    landed(wo_c)
    landed(ctx_c)

    @pl.loop(0, half // rblk)
    def _(j):
        r = pl.ds(pl.multiple_of(j * rblk, rblk), rblk)
        flat = pl.ds(pl.multiple_of((c * (half // rblk) + j) * rblk, rblk), rblk)
        o = dot_nt(wide(CTX, flat), Wo[...].reshape(width, Wo.shape[-1]))
        o = o + dot_nt(wide(CTXP, r), WOP[...].reshape(width, Wo.shape[-1]))
        m = TOK[r, :].astype(FULL) + (o + vrow(OUTB))
        MID[r, :] = m
        v = m - jnp.mean(m, axis=-1, keepdims=True)
        rstd = lax.rsqrt(jnp.mean(v * v, axis=-1, keepdims=True) + EPSILON)
        n = v * rstd
        N2F[r, :] = n
        RS[r, 1:2] = rstd
        N2[c, r, :] = (n * vrow(GAIN2) + vrow(SHIFT2)).astype(LOW)

    n2_c = [copy(N2.at[c], N2.at[c], cdev)]
    start(n2_c)
    landed(n2_c)
    all_in(fw)

    parts = [GPR.at[b, pl.ds(i * half, half)] for b in range(2) for i in range(2)]
    root = math.sqrt(2.0 / math.pi)

    @pl.loop(0, nrb * 2)
    def _(k):
        @pl.when(k == 1)
        def _():
            two_go(pw, 1)

        b, i = k // nrb, k % nrb
        h, off = i // (half // rblk), i % (half // rblk)
        rows = pl.ds(pl.multiple_of(off * rblk, rblk), rblk)
        flat = pl.ds(pl.multiple_of(i * rblk, rblk), rblk)
        u = dot(N2[h, rows, :], Wf[b].reshape(width, width)) + VF[pl.ds(FCB + b, 1), :]
        uu = u * u
        a = 0.5 * jnp.tanh(u * (root + (root * 0.044715) * uu)) + 0.5
        H[b, flat, :] = (u * a).astype(LOW)
        GPR[b, flat, :] = a * (1.0 + (1.0 - a) * (u * (2.0 * root + (2.0 * root * 0.134145) * uu)))

    def weight_grad(left_t, right, G, first, last):
        @pl.loop(0, 2)
        def _(b):
            g = dot(left_t[...], right[b, :, first:last])
            G[b, :, :, :, first:last] = g.astype(LOW).reshape(ZN, XN, width // GROUPS, last - first)

    every = pl.ds(0, width)
    by_rows = [pairs[0] + (pl.ds(0, third), every), pairs[1] + (pl.ds(third, 2 * third), every)]

    def reduce_copies(G, plan, A1, B1, A2, B2, R3):
        steps = []
        for a, b, r, cols in plan:
            one = [
                copy(G.at[:, :, ox, a, cols], A1.at[:, :, r, cols], xdev),
                copy(G.at[oy, :, :, b, cols], B1.at[:, :, r, cols], ydev),
            ]
            two = [
                copy(G.at[oy, :, x, a, cols], A2.at[:, r, cols], ydev),
                copy(G.at[y, :, ox, b, cols], B2.at[:, r, cols], xdev),
            ]
            q = pl.ds(a.start, a.size + b.size)
            three = [
                Group(
                    [(G.at[y, (z + k) % ZN, x, q, cols], R3.at[k - 1, q, cols], zdev(k)) for k in range(1, ZN)],
                    R3.at[:, q, cols],
                )
            ]
            steps.append((a, b, r, cols, one, two, three))

        def add(target, source):
            target[...] = (target[...].astype(FULL) + source[...].astype(FULL)).astype(LOW)

        def go(i):
            start(steps[i][4])

        def second(i):
            a, b, r, cols, one, two, three = steps[i]
            landed(one[:1])

            @pl.loop(0, ZN)
            def _(k):
                add(G.at[oy, k, x, a, cols], A1.at[oy, k, r, cols])

            start(two[:1])
            landed(one[1:])

            @pl.loop(0, ZN)
            def _(k):
                add(G.at[y, k, ox, b, cols], B1.at[k, ox, r, cols])

            start(two[1:])

            @pl.loop(0, ZN)
            def _(k):
                add(G.at[y, k, x, a, cols], A1.at[y, k, r, cols])
                add(G.at[y, k, x, b, cols], B1.at[k, x, r, cols])

        def third_step(i):
            a, b, r, cols, one, two, three = steps[i]
            landed(two)

            @pl.loop(0, ZN)
            def _(k):
                add(G.at[y, k, x, a, cols], A2.at[k, r, cols])
                add(G.at[y, k, x, b, cols], B2.at[k, r, cols])

            start(three)

        def last(i, out):
            a, b, r, cols, one, two, three = steps[i]
            landed(three)
            for q in (a, b):
                v = G[y, z, x, q, cols].astype(FULL)
                for k in range(ZN - 1):
                    v = v + R3[k, q, cols].astype(FULL)
                out[q, cols] = v

        return go, second, third_step, last

    def reduce_wide(G, plan, A1, B1, A2, B2, A3, B3, EA, EB):
        steps = []
        for a, b, r, cols in plan:
            one = [
                copy(G.at[oy, :, :, a, cols], A1.at[:, :, r, cols], ydev),
                copy(G.at[:, :, ox, b, cols], B1.at[:, :, r, cols], xdev),
            ]
            two = [
                ZReduce(
                    lambda i, a=a, cols=cols: G.at[y, i, :, a, cols],
                    lambda k, r=r, cols=cols: A2.at[k, :, r, cols],
                    EA.at[:, r, cols],
                ),
                ZReduce(
                    lambda i, b=b, cols=cols: G.at[:, i, x, b, cols],
                    lambda k, r=r, cols=cols: B2.at[k, :, r, cols],
                    EB.at[:, r, cols],
                ),
            ]
            three = [
                copy(G.at[y, z, ox, a, cols], A3.at[r, cols], xdev),
                copy(G.at[oy, z, x, b, cols], B3.at[r, cols], ydev),
            ]
            steps.append((a, b, r, cols, one, two, three))

        def add(target, sources):
            v = target[...].astype(FULL)
            for source in sources:
                v = v + source[...].astype(FULL)
            target[...] = v.astype(LOW)

        def go(i):
            start(steps[i][4])

        def second(i):
            a, b, r, cols, one, two, three = steps[i]
            landed(one)

            @pl.loop(0, ZN)
            def _(k):
                for j in range(2):
                    add(G.at[y, k, j, a, cols], [A1.at[k, j, r, cols]])
                    add(G.at[j, k, x, b, cols], [B1.at[j, k, r, cols]])

            start(two)

        def middle(i):
            for m in steps[i][5]:
                m.middle()

        def third_step(i):
            a, b, r, cols, one, two, three = steps[i]
            landed(two)
            for j in range(2):
                add(G.at[y, z, j, a, cols], [A2.at[k, j, r, cols] for k in range(ZN - 1)])
                add(G.at[j, z, x, b, cols], [B2.at[k, j, r, cols] for k in range(ZN - 1)])
            start(three)

        def last(i, out):
            a, b, r, cols, one, two, three = steps[i]
            landed(three)
            for q, R in ((a, A3), (b, B3)):
                out[q, cols] = G[y, z, x, q, cols].astype(FULL) + R[r, cols].astype(FULL)

        return go, second, third_step, last, middle

    rp = reduce_wide(Gp, by_rows, RpA1, RpB1, RpA2, RpB2, RpA3, RpB3, RpEA, RpEB)
    rf = reduce_copies(Gf, by_rows, RfA1, RfB1, RfA2, RfB2, Rf3)
    weight_grad(T0, H, Gp, 0, width)
    rp[0](0)
    transpose_all(N2, T1)
    all_in(pw)
    rp[0](1)


    def pair_nt(A, W, columns):
        def block(flat):
            return dot_nt(A[0, flat, :columns], W[0].reshape(width, W.shape[-1])) + dot_nt(
                A[1, flat, :columns], W[1].reshape(width, W.shape[-1])
            )

        return block

    @pl.loop(0, 4)
    def _(k):
        b, h = k // 2, k % 2
        flat = pl.ds(pl.multiple_of(h * half, half), half)
        g = (dot(COT[h], Wp[b].reshape(width, width)) * GPR[b, flat, :]).astype(LOW)
        PG[b, flat, :] = g
        VG[pl.ds(FCB + b, 1), :] += jnp.sum(g.astype(FULL), axis=0, keepdims=True)

    p2_c = [copy(parts[3], V1, cdev)]
    split_rows(pair_nt(PG, Wf, width), parts[3], parts[0], p2_c)
    rp[1](0)
    weight_grad(T1, PG, Gf, 0, width)
    rf[0](0)
    rf[0](1)
    landed(p2_c)

    sent(n2_c)

    def norm_back(dy, n, rstd, gain):
        e = dy * gain
        return (e - jnp.mean(e, axis=-1, keepdims=True) - n * jnp.mean(e * n, axis=-1, keepdims=True)) * rstd

    def add_row(i, v):
        VG[i : i + 1, :] += jnp.sum(v, axis=0, keepdims=True)

    @pl.loop(0, half // 128)
    def _(i):
        r = row_tile(i)
        dy = GPR[0, r, :] + V1[r, :]
        n = N2F[r, :]
        add_row(GAIN2, dy * n)
        add_row(SHIFT2, dy)
        cot = COT[c, r, :].astype(FULL)
        add_row(PROJB, cot)
        g = cot + norm_back(dy, n, RS[r, 1:2], vrow(GAIN2))
        N2F[r, :] = g
        low = g.astype(LOW)
        add_row(OUTB, low.astype(FULL))
        N2[c, r, :] = low

    ag_c = [copy(N2.at[c], N2.at[c], cdev)]
    start(ag_c)

    def vector_copies(first, last):
        r = pl.ds(first, last - first)
        over_z = [Group([(VG.at[r], VZ.at[k - 1, r], zdev(k)) for k in range(1, ZN)], VZ.at[:, r])]
        mine = VO.at[(y * 2 + x) * 2 + c, r]
        return r, over_z, mine, [Group([(mine, mine, d) for d in near], VO.at[pl.ds(0, 7), r])]

    def vector_second(v):
        r, over_z, mine, over_near = v
        landed(over_z)
        mine[...] = VG[r, :] + VZ[0, r, :] + VZ[1, r, :] + VZ[2, r, :]
        start(over_near)

    def vector_last(v):
        r, over_z, mine, over_near = v
        landed(over_near)
        for core in range(2):
            vo_ref[core, r, :] = (VO[core, r, :] + VO[2 + core, r, :]) + (VO[4 + core, r, :] + VO[6 + core, r, :])

    late = vector_copies(0, 4)
    er = pl.ds(8, VEC - 8)
    early = [
        [Group([(VG.at[er], VZ.at[k - 1, er], zdev(k)) for k in range(1, ZN)], VZ.at[:, er])],
        [copy(VO.at[0, er], VO.at[1, er], xdev)],
        [copy(VO.at[2, er], VO.at[3, er], ydev)],
        [copy(vo_ref.at[c, er], vo_ref.at[c, er], cdev)],
    ]
    start(early[0])

    def early_hop(i):
        landed(early[i])
        if i == 0:
            VO[0, er, :] = VG[er, :] + VZ[0, er, :] + VZ[1, er, :] + VZ[2, er, :]
        elif i == 1:
            VO[2, er, :] = VO[0, er, :] + VO[1, er, :]
        else:
            vo_ref[c, er, :] = VO[2, er, :] + VO[3, er, :]
        start(early[i + 1])

    pm_c = [copy(parts[1], V0, cdev)]
    split_rows(pair_nt(H, Wp, width), parts[1], MID, pm_c, MID)
    rp[1](1)
    transpose_all(N1, T1)
    landed(ag_c)

    @pl.loop(0, nrb)
    def _(i):
        h, off = i // (half // rblk), i % (half // rblk)
        rows = pl.ds(pl.multiple_of(off * rblk, rblk), rblk)
        flat = pl.ds(pl.multiple_of(i * rblk, rblk), rblk)
        g = dot(N2[h, rows, :], Wo[...].reshape(width, Wo.shape[-1])).astype(LOW)
        row = lax.broadcasted_iota(jnp.int32, (8, 128), 0)
        lane = lax.broadcasted_iota(jnp.int32, (8, 128), 1)
        pick = jnp.where(lane // HD == row, 1.0, 0.0).astype(LOW)
        for p in range(3):
            gp = tile(g, p)
            DO[p, flat, :] = gp
            prod = gp.astype(FULL) * CTX[p, flat, :].astype(FULL)
            high = prod.astype(LOW)
            rest = (prod - high.astype(FULL)).astype(LOW)
            d = dot_nt(pick, high) + dot_nt(pick, rest)
            for e in range(2):
                DELR[2 * p + e, :, flat] = d[e : e + 1, :]

    transpose_all(N2, T0)

    @pl.loop(0, 2)
    def _(m):
        rows = pl.ds(pl.multiple_of(m * (width // 2), width // 2), width // 2)
        g = dot(T0[rows, :], wide(CTX, pl.ds(0, seq_len)))
        g = g.astype(LOW).reshape(ZN // 2, XN, 2, width // (2 * GROUPS), Wo.shape[-1])
        Go[pl.ds(m * (ZN // 2), ZN // 2)] = g

    ro = [
        [copy(Go.at[:, :, oy, oa], Ro1A, ydev), copy(Go.at[:, ox, :, ob], Ro1B, xdev)],
        [copy(Go.at[:, ox, y, oa], Ro2A, xdev), copy(Go.at[:, x, oy, ob], Ro2B, ydev)],
        [Group([(Go.at[(z + k) % ZN, x, y], Ro3.at[k - 1], zdev(k)) for k in range(1, ZN)], Ro3)],
        [Group([(go_ref.at[t], go_ref.at[t], d) for d in (cdev, ydev, gdev)], go_ref.at[pl.ds(0, 3)])],
    ]

    def ro_second():
        landed(ro[0])

        @pl.loop(0, ZN)
        def _(k):
            for i in range(XN):
                Go[k, i, y, oa] = (Go[k, i, y, oa].astype(FULL) + Ro1A[k, i].astype(FULL)).astype(LOW)
                Go[k, x, i, ob] = (Go[k, x, i, ob].astype(FULL) + Ro1B[k, i].astype(FULL)).astype(LOW)

        start(ro[1])

    def ro_third():
        landed(ro[1])

        @pl.loop(0, ZN)
        def _(k):
            Go[k, x, y, oa] = (Go[k, x, y, oa].astype(FULL) + Ro2A[k].astype(FULL)).astype(LOW)
            Go[k, x, y, ob] = (Go[k, x, y, ob].astype(FULL) + Ro2B[k].astype(FULL)).astype(LOW)

        start(ro[2])

    def ro_last():
        landed(ro[2])
        v = Go[z, x, y].astype(FULL)
        for k in range(ZN - 1):
            v = v + Ro3[k].astype(FULL)
        go_ref[t] = v
        start(ro[3])

    def attention_back(p, plan):
        DQ[...] = jnp.zeros(DQ.shape, FULL)
        for b in range(nrb):
            rows = pl.ds(b * rblk, rblk)
            first = 0 if b * rblk < half else b * rblk
            n = seq_len - first
            keys, values = KP[p, rows, :], VP[p, rows, :]
            queries, grads = QP[p, first:, :], DO[p, first:, :]
            key = b * rblk + lax.broadcasted_iota(jnp.int32, (rblk, 1), 0)
            limit = jnp.where(key < prefix, 0, key)
            shut = (b + 1) * rblk - first
            query = first + lax.broadcasted_iota(jnp.int32, (rblk, shut), 1)
            dk, dv = [], []
            for e in range(2):
                ke, ve = lane_part(keys, e), lane_part(values, e)
                sc = dot_nt(ke, queries) - LSER[2 * p + e, :, first:]
                head = jnp.where(query >= limit, sc[:, :shut], -1e30)
                w = jnp.exp(jnp.concatenate([head, sc[:, shut:]], axis=1) if shut < n else head)
                dw = dot_nt(ve, grads) - DELR[2 * p + e, :, first:]
                ds = (w * dw).astype(LOW)
                dv.append(dot(w.astype(LOW), grads))
                dk.append(dot(ds, queries))
                DQ[first:, :] += dot_tn(ds, ke)
            KP[p, rows, :] = jnp.where(low_lanes(dk[0]), dk[0], dk[1]).astype(LOW)
            VP[p, rows, :] = jnp.where(low_lanes(dv[0]), dv[0], dv[1]).astype(LOW)
            meanwhile(p, b, plan)
        QP[p, :, :] = (DQ[...] * 0.125).astype(LOW)

    away = {
        (0, 0): [lambda: rp[4](0), lambda: rf[1](0)],
        (0, 3): [lambda: start(ro[0]), lambda: early_hop(0)],
        (1, 0): [lambda: rf[1](1)],
        (1, 1): [lambda: rp[4](1)],
        (1, 2): [lambda: rf[2](0)],
        (1, 3): [lambda: early_hop(1)],
    }

    @pl.loop(0, 2)
    def _(p):
        attention_back(p, away)

    packed = Wq.shape[-1]
    sent_all(fw)

    @pl.loop(0, nrb)
    def _(i):
        flat = pl.ds(pl.multiple_of(i * rblk, rblk), rblk)
        for b in range(2):
            for k, ref in enumerate((QP, KP, VP)):
                g = ref[b, flat, :]
                H[b, flat, k * 128 : (k + 1) * 128] = g
                VG[QKVB + b : QKVB + b + 1, k * 128 : (k + 1) * 128] += jnp.sum(g.astype(FULL), axis=0, keepdims=True)

    by_lanes = [(pl.ds(0, hr), pl.ds(hr, hr), pl.ds(0, hr), pl.ds(0, 384))]
    rest = pl.ds(384, packed - 384)
    by_lanes += [pairs[1] + (pl.ds(third, 2 * third), rest), pairs[0] + (pl.ds(0, third), rest)]
    weight_grad(T1, H, Wf, 0, 384)
    rq = reduce_copies(Wf, by_lanes, RqA1, RqB1, RqA2, RqB2, Rq3)
    rq[0](0)
    landed(pm_c)

    @pl.loop(0, half // 128)
    def _(i):
        r = row_tile(i)
        TOK[r, :] = (MID[r, :] + (V0[r, :] + vrow(PROJB))).astype(LOW)

    out_c = [pltpu.make_async_copy(TOK, bo_h, ls.at[0]), pltpu.make_async_copy(N1.at[c], ig_h, ls.at[1])]
    out_c[0].start()

    away = {
        (2, 0): [lambda: rf[2](1)],
        (2, 1): [lambda: early_hop(2), ro_second],
        (2, 3): [lambda: rp[2](0)],
    }
    attention_back(2, away)

    @pl.loop(0, nrb)
    def _(i):
        flat = pl.ds(pl.multiple_of(i * rblk, rblk), rblk)
        q, k, v = (ref[2, flat, :].astype(FULL) for ref in (QP, KP, VP))
        first = low_lanes(q)
        packs = (
            (jnp.where(first, q, roll(k)), jnp.where(first, v, 0.0)),
            (jnp.where(first, roll(q), k), jnp.where(first, roll(v), 0.0)),
        )
        for b in range(2):
            for j in range(2):
                at_j = slice(384 + 128 * j, 512 + 128 * j)
                H[b, flat, at_j] = packs[b][j].astype(LOW)
                VG[QKVB + b : QKVB + b + 1, at_j] += jnp.sum(packs[b][j], axis=0, keepdims=True)

    weight_grad(T1, H, Wf, 384, packed)
    rq[0](1)
    rq[0](2)
    rq[1](0)

    p1_c = [copy(parts[1], V1, cdev)]
    sent(pm_c)
    split_rows(pair_nt(H, Wq, packed), parts[1], parts[2], p1_c)
    rp[2](1)
    ro_third()
    landed(p1_c)

    sent(n1_c)

    @pl.loop(0, half // 128)
    def _(i):
        r = row_tile(i)
        dy = GPR[1, r, :] + V1[r, :]
        n = N1F[r, :]
        add_row(GAIN1, dy * n)
        add_row(SHIFT1, dy)
        N1[c, r, :] = (N2F[r, :] + norm_back(dy, n, RS[r, 0:1], vrow(GAIN1))).astype(LOW)

    out_c[1].start()

    start(late[1])
    rq[2](0)
    rq[1](1)
    rq[1](2)
    gp_ref, gf_ref = MID.at[pl.ds(0, 2 * hr)], MID.at[pl.ds(2 * hr, 2 * hr)]
    out_c += [pltpu.make_async_copy(gp_ref, gp_h, ls.at[2]), pltpu.make_async_copy(gf_ref, gf_h, ls.at[3])]
    rp[3](0, gp_ref)
    rp[3](1, gp_ref)
    out_c[2].start()
    rf[3](0, gf_ref)
    rf[3](1, gf_ref)
    out_c[3].start()
    rq[2](1)
    rq[2](2)
    vector_second(late)
    ro_last()
    landed(early[3])
    landed(ro[3])
    out_c += [
        pltpu.make_async_copy(a, b, ls.at[4 + i]) for i, (a, b) in enumerate(((go_ref, go_h), (gq_ref, gq_h), (vo_ref, vo_h)))
    ]
    out_c[4].start()
    rq[3](0, gq_ref)
    vector_last(late)
    out_c[6].start()
    rq[3](1, gq_ref)
    rq[3](2, gq_ref)
    out_c[5].start()

    waited = {id(m) for m in n2_c + pm_c + n1_c}
    for step in fw:
        for group in step:
            waited |= {id(m) for m in group}
    sent([m for m in pending if id(m) not in waited])
    for cp in out_c:
        cp.wait()


def gather_groups(v, axis, repeat, groups):
    if repeat == 1:
        return v
    return lax.all_gather(v, "dp", axis=axis, axis_index_groups=groups, tiled=True)


def scatter_groups(v, axis, repeat, groups):
    if repeat == 1:
        return v
    return lax.psum_scatter(v, "dp", scatter_dimension=axis, axis_index_groups=groups, tiled=True)


def on_device(
    dp_size,
    tokens,
    prefix,
    cotangent,
    first_gain,
    first_shift,
    qkv_weight,
    qv_bias,
    out_weight,
    out_bias,
    second_gain,
    second_shift,
    fc_weight,
    fc_bias,
    proj_weight,
    proj_bias,
):
    repeat = dp_size // GROUPS
    groups = [[g * repeat + i for i in range(repeat)] for g in range(GROUPS)]
    half, width = tokens.shape
    seq_len = 2 * half

    def whole(v, axis):
        return gather_groups(v.astype(LOW), axis, repeat, groups).astype(FULL) if repeat > 1 else v

    params = [
        whole(first_gain, 0), whole(first_shift, 0), whole(qkv_weight, 1), whole(qv_bias, 1), whole(out_weight, 1),
        whole(out_bias, 0), whole(second_gain, 0), whole(second_shift, 0), whole(fc_weight, 0), whole(fc_bias, 0),
        whole(proj_weight, 1), whole(proj_bias, 0),
    ]
    params[4], params[10] = params[4].T, params[10].T
    rows = params[8].shape[0]
    cols = params[2].shape[2]
    units = params[8].shape[1]
    pair = 2 * HD
    packed, own = 3 * cols + HD, 2 * cols
    hr = rows // 2
    ANY = pl.BlockSpec(memory_space=pl.ANY)

    def reduce_space(lanes):
        return [
            pltpu.VMEM((2, ZN, hr, lanes), LOW),
            pltpu.VMEM((ZN, XN, hr, lanes), LOW),
            pltpu.VMEM((ZN, hr, lanes), LOW),
            pltpu.VMEM((ZN, hr, lanes), LOW),
            pltpu.VMEM((ZN - 1, rows, lanes), LOW),
        ]

    token_low = pltpu.VMEM((2, half, width), LOW)
    token_full = pltpu.VMEM((half, width), FULL)
    unit_low = pltpu.VMEM((2, seq_len, width), LOW)
    heads = pltpu.VMEM((3, seq_len, pair), LOW)
    scratch = (
        [
            pltpu.VMEM((2, ZN, XN, rows, packed), LOW),
            pltpu.VMEM((ZN, XN, 2, hr, own), LOW),
            pltpu.VMEM((2, ZN, XN, rows, width), LOW),
            pltpu.VMEM((2, ZN, XN, rows, width), LOW),
            pltpu.VMEM((ZN, XN, 2, hr, own), LOW),
            pltpu.VMEM((2, ZN, XN, rows, width), LOW),
            pltpu.VMEM((2, ZN, XN, rows, width), LOW),
        ]
        + reduce_space(packed)
        + reduce_space(width)
        + [
            pltpu.VMEM((ZN, XN, hr, width), LOW),
            pltpu.VMEM((2, ZN, hr, width), LOW),
            pltpu.VMEM((ZN - 1, XN, hr, width), LOW),
            pltpu.VMEM((ZN - 1, 2, hr, width), LOW),
            pltpu.VMEM((hr, width), LOW),
            pltpu.VMEM((hr, width), LOW),
            pltpu.VMEM((XN, hr, width), LOW),
            pltpu.VMEM((2, hr, width), LOW),
        ]
        + [
            pltpu.VMEM((ZN, XN, hr // 3 * 2, own), LOW),
            pltpu.VMEM((ZN, 2, hr // 3, own), LOW),
            pltpu.VMEM((ZN, hr // 3 * 2, own), LOW),
            pltpu.VMEM((ZN, hr // 3, own), LOW),
            pltpu.VMEM((ZN - 1, hr, own), LOW),
        ]
        + [
            pltpu.VMEM((half, width), LOW),
            token_low,
            token_full,
            token_full,
            pltpu.VMEM((half, 128), FULL),
            token_low,
            token_low,
            pltpu.VMEM((width, seq_len), LOW),
            pltpu.VMEM((width, seq_len), LOW),
        ]
        + [heads] * 5
        + [
            pltpu.VMEM((seq_len, pair), FULL),
            pltpu.VMEM((6, 1, seq_len), FULL),
            pltpu.VMEM((6, 1, seq_len), FULL),
        ]
        + [token_full] * 3
        + [unit_low, pltpu.VMEM((2, seq_len, width), FULL), unit_low]
        + [
            pltpu.VMEM((8, rows), FULL),
            pltpu.VMEM((2, rows), FULL),
            pltpu.VMEM((1, 4 * rows), FULL),
            pltpu.VMEM((3, rows, cols), FULL),
            pltpu.VMEM((2, hr, own), LOW),
            pltpu.VMEM((3, half, pair), LOW),
            pltpu.VMEM((ZN, XN, 2, hr, own), LOW),
            pltpu.VMEM((GROUPS, VEC, 128), LOW),
            pltpu.VMEM((VEC, width), FULL),
            pltpu.VMEM((VEC, width), FULL),
            pltpu.VMEM((ZN - 1, VEC, width), FULL),
        ]
        + [
            pltpu.VMEM((8, VEC, width), FULL),
            pltpu.VMEM((rows, packed), FULL),
            pltpu.VMEM((4, hr, own), FULL),
            pltpu.VMEM((2, VEC, width), FULL),
            pltpu.SMEM(prefix.shape, prefix.dtype),
        ]
        + [
            pltpu.SemaphoreType.DMA((SEMS,)),
            pltpu.SemaphoreType.DMA((SEMS,)),
            pltpu.SemaphoreType.DMA((16,)),
        ]
    )
    out_shape = [
        jax.ShapeDtypeStruct((half, width), LOW),
        jax.ShapeDtypeStruct((half, width), LOW),
        jax.ShapeDtypeStruct((rows, packed), FULL),
        jax.ShapeDtypeStruct((4, hr, own), FULL),
        jax.ShapeDtypeStruct((rows, width), FULL),
        jax.ShapeDtypeStruct((rows, width), FULL),
        jax.ShapeDtypeStruct((2, VEC, width), FULL),
    ]
    grown = pl.pallas_call(
        functools.partial(block_kernel, repeat, seq_len),
        out_shape=out_shape,
        in_specs=[ANY] * 15,
        out_specs=[ANY] * 7,
        scratch_shapes=scratch,
        compiler_params=pltpu.CompilerParams(
            collective_id=0, has_side_effects=True, vmem_limit_bytes=62 * 1024 * 1024
        ),
    )(tokens, prefix, cotangent, *params)

    vector = jax.ShapeDtypeStruct((rows,), FULL)
    results = pl.pallas_call(
        functools.partial(unpack_kernel, repeat),
        out_shape=[
            out_shape[0],
            out_shape[1],
            vector,
            vector,
            jax.ShapeDtypeStruct((3, rows, cols), FULL),
            jax.ShapeDtypeStruct((2, rows), FULL),
            jax.ShapeDtypeStruct((rows, width), FULL),
            vector,
            vector,
            vector,
            jax.ShapeDtypeStruct((rows, units), FULL),
            jax.ShapeDtypeStruct((4 * rows,), FULL),
            jax.ShapeDtypeStruct((rows, units), FULL),
            vector,
        ],
        in_specs=[ANY] * 7,
        out_specs=[ANY] * 14,
        scratch_shapes=[
            pltpu.VMEM((rows, packed), FULL),
            pltpu.VMEM((4, hr, own), FULL),
            pltpu.VMEM((2, VEC, width), FULL),
            pltpu.VMEM((3, rows, cols), FULL),
            pltpu.VMEM((rows, width), FULL),
            pltpu.VMEM((half, width), LOW),
            pltpu.VMEM((half, width), LOW),
            pltpu.VMEM((rows, units), FULL),
            pltpu.VMEM((rows, units), FULL),
            pltpu.VMEM((8, rows), FULL),
            pltpu.VMEM((2, rows), FULL),
            pltpu.VMEM((1, 4 * rows), FULL),
            pltpu.SemaphoreType.DMA((21,)),
        ],
        compiler_params=pltpu.CompilerParams(vmem_limit_bytes=62 * 1024 * 1024),
    )(*grown)
    results = [v.T if i in (6, 12) else v for i, v in enumerate(results)]
    along = (None, None, 0, 0, 1, 1, 1, 0, 0, 0, 0, 0, 1, 0)
    return tuple(
        v if repeat == 1 or axis is None else scatter_groups(v, axis, repeat, groups)
        for v, axis in zip(results, along, strict=True)
    )


def unpack_kernel(
    repeat, bo, ig, gq_h, go_h, gf, gp, vo_h,
    bo_out, ig_out, gain1, shift1, wq_h, qvb_h, wo_h, outb, gain2, shift2, wf, fcb_h, wp, projb,
    gq, go, vo, wq, wo, b1, b2, w1, w2, sv, sq, sf, sems,
):
    moves = [(vo_h, vo), (gq_h, gq), (go_h, go), (ig, b2), (bo, b1), (gf, w1), (gp, w2)]
    moves += [(wq, wq_h), (wo, wo_h), (b2, ig_out), (b1, bo_out), (w1, wf), (w2, wp)]
    vectors = ((GAIN1, gain1), (SHIFT1, shift1), (OUTB, outb), (GAIN2, gain2), (SHIFT2, shift2), (PROJB, projb))
    moves += [(sv.at[j], out) for j, (_, out) in enumerate(vectors)] + [(sq, qvb_h), (sf.at[0], fcb_h)]
    moves = [pltpu.make_async_copy(a, b, sems.at[i]) for i, (a, b) in enumerate(moves)]
    for cp in moves[:7]:
        cp.start()
    for i in range(3, 7):
        moves[i].wait()
        moves[i + 6].start()
    moves[1].wait()
    for k in range(3):
        wq[k] = jnp.concatenate(
            [gq[:, k * 128 : (k + 1) * 128], gq[:, 384 + k * HD : 384 + (k + 1) * HD]], axis=1
        )
    moves[7].start()
    moves[2].wait()
    m = [jnp.concatenate([go[core], go[2 + core]], axis=0) for core in range(2)]
    wo[...] = jnp.concatenate(
        [
            v
            for b in range(2)
            for core in range(2)
            for v in (m[core][:, b * 128 : (b + 1) * 128], m[core][:, 256 + b * HD : 256 + (b + 1) * HD])
        ],
        axis=1,
    )
    moves[8].start()
    moves[0].wait()
    s = lax.axis_index("dp") // repeat
    width = vo.shape[2]
    n = sv.shape[1]
    both = pltpu.roll(vo[0] + vo[1], (GROUPS - s) % GROUPS * n, 1)
    for j, (i, _) in enumerate(vectors):
        sv[j : j + 1, :] = both[i : i + 1, :n]
    owner = s // 2
    core, b, odd = owner % 2, owner // 2, s % 2
    place = lax.broadcasted_iota(jnp.int32, (1, width), 1)

    def lanes(v, first, last, shift):
        v = jnp.where((place >= first) & (place < last), v, 0.0)
        return pltpu.roll(v, shift % width, 1) if shift % width else v

    row = vo[core, pl.ds(QKVB + b, 1), :]
    q = lanes(row, 0, 128, 0) + lanes(row, 384, 448, -256)
    v = lanes(row, 256, 384, -256) + lanes(row, 512, 576, -384)
    back = (width - odd * n) % width
    sq[0:1, :] = pltpu.roll(q, back, 1)[:, :n]
    sq[1:2, :] = pltpu.roll(v, back, 1)[:, :n]
    row = vo[core, pl.ds(FCB + b, 1), :]
    sf[...] = pltpu.roll(row, odd * (width // 2), 1)[:, : width // 2]
    for i in range(13, 21):
        moves[i].start()
    for i in range(7, 21):
        moves[i].wait()


def solution(mesh):
    placed = (
        P(("dp", "tensor"), None),
        P("dp"),
        P(("dp", "tensor"), None),
        P("dp"),
        P("dp"),
        P(None, "dp", "tensor"),
        P(None, "dp"),
        P(None, "dp"),
        P("dp"),
        P("dp"),
        P("dp"),
        P("dp", "tensor"),
        P("dp"),
        P("tensor", "dp"),
        P("dp"),
    )
    return jax.shard_map(
        functools.partial(on_device, mesh.shape["dp"]),
        mesh=mesh,
        in_specs=placed,
        out_specs=(placed[0], placed[0]) + placed[3:],
        check_vma=False,
    )
```

```python
import functools
import math

import jax
import jax.numpy as jnp
from jax import lax
from jax.experimental import pallas as pl
from jax.experimental.pallas import tpu as pltpu
from jax.sharding import PartitionSpec as P

MESH = pl.DeviceIdType.MESH
LOW, FULL = jnp.bfloat16, jnp.float32
EPSILON = 1e-05
HD = 64
GROUPS, ZN, XN = 8, 4, 2
SEMS = 145
VEC = 16

GAIN1, SHIFT1, QKVB, OUTB, GAIN2, SHIFT2, PROJB, FCB = 0, 1, 2, 8, 9, 10, 11, 12


def dot(a, b):
    return jnp.dot(a, b, preferred_element_type=FULL)


def dot_nt(a, b):
    return lax.dot_general(a, b, (((1,), (1,)), ((), ())), preferred_element_type=FULL)


def dot_tn(a, b):
    return lax.dot_general(a, b, (((0,), (0,)), ((), ())), preferred_element_type=FULL)


def block_kernel(repeat, seq_len, *refs):
    (
        tok_h, prefix_h, cot_h, gain1_h, shift1_h, wq_h, qvb_h, wo_h, outb_h,
        gain2_h, shift2_h, wf_h, fcb_h, wp_h, projb_h,
        bo_h, ig_h, gq_h, go_h, gf_h, gp_h, vo_h,
        Wq, Wo, Wf, Wp, Go, Gp, Gf,
        RqA1, RqB1, RqA2, RqB2, Rq3,
        RfA1, RfB1, RfA2, RfB2, Rf3,
        RpA1, RpB1, RpA2, RpB2, RpA3, RpB3, RpEA, RpEB,
        Ro1A, Ro1B, Ro2A, Ro2B, Ro3,
        TOK, COT, N1F, N2F, RS, N1, N2, T0, T1,
        QP, KP, VP, CTX, DO, DQ, LSER, DELR,
        MID, V0, V1, H, GPR, PG,
        SV, SB, SC, SQ, SW, CTXP, WOP,
        VR, VF, VG, VZ, VO, gq_ref, go_ref, vo_ref, prefix_s,
        ss, rs, ls,
    ) = refs
    half = seq_len // 2
    width = TOK.shape[1]
    rblk = 256
    nrb = seq_len // rblk
    dp = lax.axis_index("dp")
    t = lax.axis_index("tensor")
    s, sub = dp // repeat, dp % repeat
    z, x = s // XN, s % XN
    y, c = t // 2, t % 2
    oy, oc, ox = 1 - y, 1 - c, 1 - x

    def at(zz, xx, tt):
        return ((zz * XN + xx) * repeat + sub, tt)

    def zdev(k):
        return at((z + k) % ZN, x, t)

    xdev = at(z, ox, t)
    ydev = at(z, x, oy * 2 + c)
    cdev = at(z, x, y * 2 + oc)
    gdev = at(z, x, oy * 2 + oc)
    near = [xdev, ydev, cdev, gdev] + [at(z, ox, i * 2 + j) for i, j in ((y, oc), (oy, c), (oy, oc))]
    others = [(((s + k) % GROUPS) * repeat + sub, t) for k in range(1, GROUPS)]

    count = [0]
    pending = []

    class Copy:
        def __init__(self, src, dst, dev, recv=None, alone=True):
            self.k = count[0]
            count[0] += 1
            self.parts = src, dst, dev, self.k if recv is None else recv.k
            if alone:
                pending.append(self)

        def made(self):
            src, dst, dev, recv = self.parts
            return pltpu.make_async_remote_copy(
                src_ref=src, dst_ref=dst, send_sem=ss.at[self.k], recv_sem=rs.at[recv],
                device_id=dev, device_id_type=MESH,
            )

        def start(self):
            self.made().start()

        def landed(self):
            self.made().wait_recv()

        def sent(self):
            self.made().wait_send()

    class Group:
        def __init__(self, moves, every):
            k = count[0]
            count[0] += 1
            self.moves = [Copy(*m, alone=False) for m in moves]
            for m in self.moves:
                m.k, m.parts = k, m.parts[:3] + (k,)
            count[0] = k + 1
            self.every = Copy(every, every, moves[0][2], alone=False)
            self.every.k, self.every.parts = k, self.every.parts[:3] + (k,)
            count[0] = k + 1
            pending.append(self)

        def start(self):
            for m in self.moves:
                m.start()

        def landed(self):
            self.every.landed()

        def sent(self):
            self.every.sent()

    class ZGather:
        def __init__(self, block):
            self.to = [Copy(block(z), block(z), zdev(k), alone=False) for k in range(1, ZN)]
            self.up = Copy(block(0), block(0), at(3, x, t), self.to[2], False)
            self.down = Copy(block(3), block(3), at(0, x, t), self.to[0], False)
            pending.append(self)

        def each(self, act):
            act(self.to[1])
            pl.when(z != 3)(lambda: act(self.to[0]))
            pl.when(z != 0)(lambda: act(self.to[2]))

        def start(self):
            self.each(lambda m: m.start())

        def middle(self):
            def go_on(onward):
                landed(self.to[1:2])
                onward.start()

            pl.when(z == 2)(lambda: go_on(self.up))
            pl.when(z == 1)(lambda: go_on(self.down))

        def landed(self):
            pl.when((z == 0) | (z == 3))(self.to[1].landed)
            self.to[0].landed()
            self.to[2].landed()

        def sent(self):
            self.each(lambda m: m.sent())
            pl.when(z == 2)(self.up.sent)
            pl.when(z == 1)(self.down.sent)

    class ZReduce:
        def __init__(self, block, arrived, extra):
            self.block, self.extra = block, extra
            self.to = [Copy(block((z + k) % ZN), arrived(k - 1), zdev(k), alone=False) for k in range(1, ZN)]
            self.up = Copy(block(3), extra, at(1, x, t), alone=False)
            self.down = Copy(block(0), extra, at(2, x, t), alone=False)
            pending.append(self)

            def none(slot):
                arrived(slot)[...] = jnp.zeros(extra.shape, LOW)

            pl.when(z == 0)(lambda: none(0))
            pl.when(z == 3)(lambda: none(2))

        def start(self):
            pl.when(z != 3)(self.to[0].start)
            pl.when(z != 0)(self.to[2].start)
            pl.when(z == 0)(self.up.start)
            pl.when(z == 3)(self.down.start)
            pl.when((z == 0) | (z == 3))(self.to[1].start)

        def middle(self):
            def go_on(arrival, owner):
                landed([arrival])
                target = self.block(owner)
                target[...] = (target[...].astype(FULL) + self.extra[...].astype(FULL)).astype(LOW)
                self.to[1].start()

            pl.when(z == 1)(lambda: go_on(self.up, 3))
            pl.when(z == 2)(lambda: go_on(self.down, 0))

        def landed(self):
            self.to[1].landed()
            pl.when(z != 0)(self.to[0].landed)
            pl.when(z != 3)(self.to[2].landed)

        def sent(self):
            self.to[1].sent()
            pl.when(z != 3)(self.to[0].sent)
            pl.when(z != 0)(self.to[2].sent)
            pl.when(z == 0)(self.up.sent)
            pl.when(z == 3)(self.down.sent)

    def copy(src, dst, dev):
        return Copy(src, dst, dev)

    def start(moves):
        for m in moves:
            m.start()

    def landed(moves):
        for m in moves:
            m.landed()

    def sent(moves):
        for m in moves:
            m.sent()

    barrier = pltpu.get_barrier_semaphore()
    peers = others + [d for i, d in enumerate(near) if i != 0]
    for d in peers:
        pl.semaphore_signal(barrier, inc=1, device_id=d, device_id_type=MESH)

    SO, SF, SP = (GPR.at[0, pl.ds(i * wo_h.shape[0], wo_h.shape[0])] for i in range(3))
    brought = [
        (wq_h, SQ), (qvb_h, SB), (fcb_h, SC.at[0]),
        (gain1_h, SV.at[0]), (shift1_h, SV.at[1]), (outb_h, SV.at[2]),
        (gain2_h, SV.at[3]), (shift2_h, SV.at[4]), (projb_h, SV.at[5]),
        (wo_h, SO), (tok_h, TOK), (cot_h, COT.at[c]), (wf_h, SF), (wp_h, SP),
        (prefix_h, prefix_s),
    ]
    local = [pltpu.make_async_copy(a, b, ls.at[i]) for i, (a, b) in enumerate(brought)]
    for cp in local:
        cp.start()

    lanes96 = SV.shape[1]
    VG[...] = jnp.zeros(VG.shape, FULL)
    for cp in local[1:9]:
        cp.wait()
    VG[0:6, :lanes96] = SV[0:6, :]
    VG[6:8, :lanes96] = SB[...]
    for j in range(4):
        VG[8 + j : 9 + j, :lanes96] = SC[:, j * lanes96 : (j + 1) * lanes96]
    VR[s] = VG[:, :128].astype(LOW)
    VG[...] = jnp.zeros(VG.shape, FULL)
    local[0].wait()
    q3 = SQ[...]
    Wq[y, z, x] = jnp.concatenate(
        [q3[0, :, :128], q3[1, :, :128], q3[2, :, :128]]
        + [q3[k, :, 128:] for k in range(3)]
        + [jnp.zeros((q3.shape[1], HD), FULL)],
        axis=1,
    ).astype(LOW)
    pl.semaphore_wait(barrier, len(peers))

    vec_c = [Group([(VR.at[s], VR.at[s], d) for d in others], VR.at[pl.ds(0, GROUPS - 1)])]
    cot_c = [copy(COT.at[c], COT.at[c], cdev)]
    hr = wq_h.shape[1] // 2
    third = hr // 3
    pairs = (
        (pl.ds(0, third), pl.ds(third, third)),
        (pl.ds(2 * third, 2 * third), pl.ds(4 * third, 2 * third)),
    )

    thin = [(pl.ds(2 * i * third, third), pl.ds((2 * i + 1) * third, third)) for i in range(3)]

    def gather(W, pairs):
        steps = []
        for a, b in pairs:
            r = pl.ds(a.start, a.size + b.size)
            mine = W.at[y, z, x, r]
            zs = [Group([(mine, mine, zdev(k)) for k in range(1, ZN)], W.at[y, pl.ds(0, ZN - 1), x, r])]
            one = [
                copy(W.at[y, :, x, a], W.at[y, :, x, a], xdev),
                copy(W.at[y, :, x, b], W.at[y, :, x, b], ydev),
            ]
            two = [
                copy(W.at[y, :, :, a], W.at[y, :, :, a], ydev),
                copy(W.at[:, :, x, b], W.at[:, :, x, b], xdev),
            ]
            steps.append((zs, one, two))
        return steps

    def gather_wide(W):
        steps = []
        for a, b in pairs:
            near = [
                copy(W.at[y, z, x, a], W.at[y, z, x, a], xdev),
                copy(W.at[y, z, x, b], W.at[y, z, x, b], ydev),
            ]
            zs = [ZGather(lambda i, a=a: W.at[y, i, :, a]), ZGather(lambda i, b=b: W.at[:, i, x, b])]
            far = [
                copy(W.at[y, :, :, a], W.at[y, :, :, a], ydev),
                copy(W.at[:, :, x, b], W.at[:, :, x, b], xdev),
            ]
            steps.append((near, zs, far))
        return steps

    oa, ob = pl.ds(0, 2 * third), pl.ds(2 * third, third)
    ow = [
        (
            [Group([(Wo.at[z, x, y], Wo.at[z, x, y], zdev(k)) for k in range(1, ZN)], Wo.at[pl.ds(0, ZN - 1), x, y])],
            [
                copy(Wo.at[:, x, y, oa], Wo.at[:, x, y, oa], xdev),
                copy(Wo.at[:, x, y, ob], Wo.at[:, x, y, ob], ydev),
            ],
            [
                copy(Wo.at[:, :, y, oa], Wo.at[:, :, y, oa], ydev),
                copy(Wo.at[:, x, :, ob], Wo.at[:, x, :, ob], xdev),
            ],
        )
    ]
    qw, pw, fw = gather(Wq, thin), gather_wide(Wp), gather(Wf, thin)

    def z_go(w, i):
        start(w[i][0])

    def one_go(w, i):
        landed(w[i][0])
        start(w[i][1])

    def two_go(w, i):
        n = len(w[i][1]) // len(w[i][2])
        for k, after in enumerate(w[i][2]):
            landed(w[i][1][k * n : (k + 1) * n])
            start([after])

    def all_in(w):
        for step in w:
            landed(step[2])

    def sent_all(w):
        for step in w:
            for group in step:
                sent(group)

    start(vec_c)
    z_go(qw, 0)
    local[9].wait()
    turned = pltpu.roll(SO[...], (width - c * (width // 4)) % width, 1)
    last = jnp.concatenate([turned[:, 128:192], turned[:, 512:576]], axis=1)
    mine = jnp.concatenate([turned[:, 0:128], turned[:, 384:512], last], axis=1).astype(LOW)
    SW[0] = mine[: SW.shape[1]]
    SW[1] = mine[SW.shape[1] :]
    Wo[z, x, y] = SW[y]
    local[12].wait()
    Wf[y, z, x] = SF[...].astype(LOW)
    local[13].wait()
    Wp[y, z, x] = SP[...].astype(LOW)
    local[10].wait()
    local[11].wait()
    local[14].wait()
    z_go(pw, 0)
    z_go(pw, 1)
    start(cot_c)

    def row_tile(i, n=128):
        return pl.ds(pl.multiple_of(i * n, n), n)

    @pl.loop(0, half // 128)
    def _(i):
        r = row_tile(i)
        v = TOK[r, :].astype(FULL)
        v = v - jnp.mean(v, axis=-1, keepdims=True)
        rstd = lax.rsqrt(jnp.mean(v * v, axis=-1, keepdims=True) + EPSILON)
        N1F[r, :] = v * rstd
        RS[r, 0:1] = rstd

    z_go(qw, 1)
    landed(vec_c)

    def widen(v):
        return jnp.concatenate([v, jnp.zeros((v.shape[0], width - v.shape[1]), FULL)], axis=1)

    pieces = [widen(VR[g].astype(FULL)) for g in range(GROUPS)]
    plain = pieces[0]
    for g in range(1, GROUPS):
        plain = plain + pltpu.roll(pieces[g], g * lanes96, 1)
    VF[GAIN1 : SHIFT1 + 1, :] = plain[0:2]
    VF[OUTB : PROJB + 1, :] = plain[2:6]
    place = lax.broadcasted_iota(jnp.int32, (1, width), 1)

    def lanes(v, first, last, shift):
        v = jnp.where((place >= first) & (place < last), v, 0.0)
        return pltpu.roll(v, shift % width, 1) if shift % width else v

    for b in range(2):
        a0, a1 = (widen(VR[2 * (2 * b + c) + i].astype(FULL)) for i in range(2))
        a1 = pltpu.roll(a1, lanes96, 1)
        qb, vb = a0[6:7] + a1[6:7], a0[7:8] + a1[7:8]
        VF[QKVB + b : QKVB + b + 1, :] = (
            lanes(qb, 0, 128, 0) + lanes(qb, 128, 192, 256) + lanes(vb, 0, 128, 256) + lanes(vb, 128, 192, 384)
        )
        a1 = pltpu.roll(a1, 3 * lanes96, 1)
        row = a0[8:9] + a1[8:9]
        for j in range(1, 4):
            row = row + pltpu.roll(a0[8 + j : 9 + j] + a1[8 + j : 9 + j], j * lanes96, 1)
        VF[FCB + b : FCB + b + 1, :] = row

    def vrow(i):
        return VF[i : i + 1, :]

    @pl.loop(0, half // 128)
    def _(i):
        r = row_tile(i)
        N1[c, r, :] = (N1F[r, :] * vrow(GAIN1) + vrow(SHIFT1)).astype(LOW)

    n1_c = [copy(N1.at[c], N1.at[c], cdev)]
    start(n1_c)

    def transpose_all(source, target):
        @pl.loop(0, nrb)
        def _(i):
            h, off = i // (half // rblk), i % (half // rblk)
            rows = pl.ds(pl.multiple_of(off * rblk, rblk), rblk)
            cols = pl.ds(pl.multiple_of(i * rblk, rblk), rblk)
            for k in range(width // rblk):
                target[k * rblk : (k + 1) * rblk, cols] = source[h, rows, k * rblk : (k + 1) * rblk].T

    landed(cot_c)
    one_go(qw, 0)
    transpose_all(COT, T0)
    one_go(qw, 1)
    z_go(qw, 2)
    two_go(qw, 0)
    z_go(fw, 0)
    two_go(qw, 1)
    z_go(ow, 0)
    one_go(qw, 2)
    z_go(fw, 1)
    landed(n1_c)
    two_go(qw, 2)
    z_go(fw, 2)
    one_go(fw, 0)
    all_in(qw)

    def low_lanes(v):
        return lax.broadcasted_iota(jnp.int32, v.shape, 1) < HD

    def tile(v, i):
        return v[:, i * 128 : (i + 1) * 128]

    def roll(v):
        return pltpu.roll(v, HD, 1)

    @pl.loop(0, nrb)
    def _(i):
        h, off = i // (half // rblk), i % (half // rblk)
        rows = pl.ds(pl.multiple_of(off * rblk, rblk), rblk)
        out = pl.ds(pl.multiple_of(i * rblk, rblk), rblk)
        n = N1[h, rows, :]
        got = []
        for b in range(2):
            got.append(dot(n, Wq[b].reshape(width, Wq.shape[-1])) + VF[QKVB + b : QKVB + b + 1, : Wq.shape[-1]])
            QP[b, out, :] = (tile(got[b], 0).astype(LOW).astype(FULL) * 0.125).astype(LOW)
            KP[b, out, :] = tile(got[b], 1).astype(LOW)
            VP[b, out, :] = tile(got[b], 2).astype(LOW)
        first = low_lanes(tile(got[0], 3))
        q = jnp.where(first, tile(got[0], 3), roll(tile(got[1], 3)))
        QP[2, out, :] = (q.astype(LOW).astype(FULL) * 0.125).astype(LOW)
        KP[2, out, :] = jnp.where(first, roll(tile(got[0], 3)), tile(got[1], 3)).astype(LOW)
        VP[2, out, :] = jnp.where(first, tile(got[0], 4), roll(tile(got[1], 4))).astype(LOW)

        @pl.when(i == 0)
        def _():
            one_go(ow, 0)
            one_go(fw, 1)
            one_go(pw, 0)

        @pl.when(i == 2)
        def _():
            two_go(fw, 0)

    prefix = prefix_s[y]
    LSEC = DQ
    LSEC[...] = jnp.zeros(LSEC.shape, FULL)

    def lane_part(v, e):
        lane = lax.broadcasted_iota(jnp.int32, v.shape, 1)
        keep = lane < HD if e == 0 else lane >= HD
        return jnp.where(keep, v, jnp.zeros_like(v))

    def meanwhile(p, b, plan):
        for (pp, bb), steps in plan.items():
            if bb != b:
                continue
            if isinstance(p, int):
                for step in steps:
                    step()
            else:

                @pl.when(p == pp)
                def _(steps=steps):
                    for step in steps:
                        step()

    ctx_c = [copy(CTX.at[p, pl.ds(oc * half, half)], CTXP.at[p], cdev) for p in range(3)]
    wo_c = [copy(Wo, WOP, cdev)]

    def share_out():
        all_in(ow)
        start(wo_c)

    def pass_on(i):
        for m in pw[i][1]:
            m.middle()

    fetch = {
        (0, 0): [lambda: one_go(fw, 2), lambda: two_go(ow, 0)],
        (0, 1): [lambda: two_go(fw, 1), lambda: one_go(pw, 1)],
        (0, 3): [lambda: start(ctx_c[0:1])],
        (1, 1): [lambda: pass_on(0)],
        (1, 2): [lambda: two_go(fw, 2)],
        (1, 3): [lambda: start(ctx_c[1:2])],
        (2, 0): [lambda: two_go(pw, 0)],
        (2, 1): [share_out],
        (2, 3): [lambda: start(ctx_c[2:3]), lambda: pass_on(1)],
    }

    @pl.loop(0, 3)
    def _(p):
        for b in range(nrb):
            rows = pl.ds(b * rblk, rblk)
            cols = max(half, (b + 1) * rblk)
            q = QP[p, rows, :]
            keys, values = KP[p, :cols, :], VP[p, :cols, :]
            query = b * rblk + lax.broadcasted_iota(jnp.int32, (rblk, 1), 0)
            limit = jnp.maximum(prefix - 1, query)
            free = b * rblk
            key = free + lax.broadcasted_iota(jnp.int32, (rblk, cols - free), 1)
            parts = []
            for e in range(2):
                sc = dot_nt(lane_part(q, e), keys)
                tail = jnp.where(key <= limit, sc[:, free:], -1e30)
                sc = jnp.concatenate([sc[:, :free], tail], axis=1) if free else tail
                peak = jnp.max(sc, axis=-1, keepdims=True)
                w = jnp.exp(sc - peak)
                total = jnp.sum(w, axis=-1, keepdims=True)
                parts.append(dot(w.astype(LOW), values) * (1.0 / total))
                lane = lax.broadcasted_iota(jnp.int32, (rblk, 128), 1)
                LSEC[rows, :] = jnp.where(lane == 2 * p + e, peak + jnp.log(total), LSEC[rows, :])
            CTX[p, rows, :] = jnp.where(low_lanes(parts[0]), parts[0], parts[1]).astype(LOW)
            meanwhile(p, b, fetch)

    for b in range(nrb):
        lt = LSEC[b * rblk : (b + 1) * rblk, :].T
        for h in range(6):
            LSER[h, :, b * rblk : (b + 1) * rblk] = lt[h : h + 1, :]
    def wide(ref, rows):
        return jnp.concatenate([ref[0, rows, :], ref[1, rows, :], ref[2, rows, :]], axis=1)

    def split_rows(make_block, away, home, copies, plus=None):
        per = half // rblk
        for which, target in ((oc, away), (c, home)):

            @pl.loop(0, per)
            def _(j):
                rows = pl.ds(pl.multiple_of(j * rblk, rblk), rblk)
                block = make_block(pl.ds(pl.multiple_of((which * per + j) * rblk, rblk), rblk))
                target[rows, :] = block if plus is None or target is away else block + plus[rows, :]

            if target is away:
                start(copies)

    parts = [GPR.at[b, pl.ds(i * half, half)] for b in range(2) for i in range(2)]
    landed(wo_c)
    landed(ctx_c)

    @pl.loop(0, half // rblk)
    def _(j):
        r = pl.ds(pl.multiple_of(j * rblk, rblk), rblk)
        flat = pl.ds(pl.multiple_of((c * (half // rblk) + j) * rblk, rblk), rblk)
        o = dot_nt(wide(CTX, flat), Wo[...].reshape(width, Wo.shape[-1]))
        o = o + dot_nt(wide(CTXP, r), WOP[...].reshape(width, Wo.shape[-1]))
        m = TOK[r, :].astype(FULL) + (o + vrow(OUTB))
        MID[r, :] = m
        v = m - jnp.mean(m, axis=-1, keepdims=True)
        rstd = lax.rsqrt(jnp.mean(v * v, axis=-1, keepdims=True) + EPSILON)
        n = v * rstd
        N2F[r, :] = n
        RS[r, 1:2] = rstd
        N2[c, r, :] = (n * vrow(GAIN2) + vrow(SHIFT2)).astype(LOW)

    n2_c = [copy(N2.at[c], N2.at[c], cdev)]
    start(n2_c)
    landed(n2_c)
    all_in(fw)

    parts = [GPR.at[b, pl.ds(i * half, half)] for b in range(2) for i in range(2)]
    root = math.sqrt(2.0 / math.pi)

    @pl.loop(0, nrb * 2)
    def _(k):
        @pl.when(k == 1)
        def _():
            two_go(pw, 1)

        b, i = k // nrb, k % nrb
        h, off = i // (half // rblk), i % (half // rblk)
        rows = pl.ds(pl.multiple_of(off * rblk, rblk), rblk)
        flat = pl.ds(pl.multiple_of(i * rblk, rblk), rblk)
        u = dot(N2[h, rows, :], Wf[b].reshape(width, width)) + VF[pl.ds(FCB + b, 1), :]
        uu = u * u
        a = 0.5 * jnp.tanh(u * (root + (root * 0.044715) * uu)) + 0.5
        H[b, flat, :] = (u * a).astype(LOW)
        GPR[b, flat, :] = a * (1.0 + (1.0 - a) * (u * (2.0 * root + (2.0 * root * 0.134145) * uu)))

    def weight_grad(left_t, right, G, first, last):
        @pl.loop(0, 2)
        def _(b):
            g = dot(left_t[...], right[b, :, first:last])
            G[b, :, :, :, first:last] = g.astype(LOW).reshape(ZN, XN, width // GROUPS, last - first)

    every = pl.ds(0, width)
    by_rows = [pairs[0] + (pl.ds(0, third), every), pairs[1] + (pl.ds(third, 2 * third), every)]

    def reduce_copies(G, plan, A1, B1, A2, B2, R3):
        steps = []
        for a, b, r, cols in plan:
            one = [
                copy(G.at[:, :, ox, a, cols], A1.at[:, :, r, cols], xdev),
                copy(G.at[oy, :, :, b, cols], B1.at[:, :, r, cols], ydev),
            ]
            two = [
                copy(G.at[oy, :, x, a, cols], A2.at[:, r, cols], ydev),
                copy(G.at[y, :, ox, b, cols], B2.at[:, r, cols], xdev),
            ]
            q = pl.ds(a.start, a.size + b.size)
            three = [
                Group(
                    [(G.at[y, (z + k) % ZN, x, q, cols], R3.at[k - 1, q, cols], zdev(k)) for k in range(1, ZN)],
                    R3.at[:, q, cols],
                )
            ]
            steps.append((a, b, r, cols, one, two, three))

        def add(target, source):
            target[...] = (target[...].astype(FULL) + source[...].astype(FULL)).astype(LOW)

        def go(i):
            start(steps[i][4])

        def second(i):
            a, b, r, cols, one, two, three = steps[i]
            landed(one[:1])

            @pl.loop(0, ZN)
            def _(k):
                add(G.at[oy, k, x, a, cols], A1.at[oy, k, r, cols])

            start(two[:1])
            landed(one[1:])

            @pl.loop(0, ZN)
            def _(k):
                add(G.at[y, k, ox, b, cols], B1.at[k, ox, r, cols])

            start(two[1:])

            @pl.loop(0, ZN)
            def _(k):
                add(G.at[y, k, x, a, cols], A1.at[y, k, r, cols])
                add(G.at[y, k, x, b, cols], B1.at[k, x, r, cols])

        def third_step(i):
            a, b, r, cols, one, two, three = steps[i]
            landed(two)

            @pl.loop(0, ZN)
            def _(k):
                add(G.at[y, k, x, a, cols], A2.at[k, r, cols])
                add(G.at[y, k, x, b, cols], B2.at[k, r, cols])

            start(three)

        def last(i, out):
            a, b, r, cols, one, two, three = steps[i]
            landed(three)
            for q in (a, b):
                v = G[y, z, x, q, cols].astype(FULL)
                for k in range(ZN - 1):
                    v = v + R3[k, q, cols].astype(FULL)
                out[q, cols] = v

        return go, second, third_step, last

    def reduce_wide(G, plan, A1, B1, A2, B2, A3, B3, EA, EB):
        steps = []
        for a, b, r, cols in plan:
            one = [
                copy(G.at[oy, :, :, a, cols], A1.at[:, :, r, cols], ydev),
                copy(G.at[:, :, ox, b, cols], B1.at[:, :, r, cols], xdev),
            ]
            two = [
                ZReduce(
                    lambda i, a=a, cols=cols: G.at[y, i, :, a, cols],
                    lambda k, r=r, cols=cols: A2.at[k, :, r, cols],
                    EA.at[:, r, cols],
                ),
                ZReduce(
                    lambda i, b=b, cols=cols: G.at[:, i, x, b, cols],
                    lambda k, r=r, cols=cols: B2.at[k, :, r, cols],
                    EB.at[:, r, cols],
                ),
            ]
            three = [
                copy(G.at[y, z, ox, a, cols], A3.at[r, cols], xdev),
                copy(G.at[oy, z, x, b, cols], B3.at[r, cols], ydev),
            ]
            steps.append((a, b, r, cols, one, two, three))

        def add(target, sources):
            v = target[...].astype(FULL)
            for source in sources:
                v = v + source[...].astype(FULL)
            target[...] = v.astype(LOW)

        def go(i):
            start(steps[i][4])

        def second(i):
            a, b, r, cols, one, two, three = steps[i]
            landed(one)

            @pl.loop(0, ZN)
            def _(k):
                for j in range(2):
                    add(G.at[y, k, j, a, cols], [A1.at[k, j, r, cols]])
                    add(G.at[j, k, x, b, cols], [B1.at[j, k, r, cols]])

            start(two)

        def middle(i):
            for m in steps[i][5]:
                m.middle()

        def third_step(i):
            a, b, r, cols, one, two, three = steps[i]
            landed(two)
            for j in range(2):
                add(G.at[y, z, j, a, cols], [A2.at[k, j, r, cols] for k in range(ZN - 1)])
                add(G.at[j, z, x, b, cols], [B2.at[k, j, r, cols] for k in range(ZN - 1)])
            start(three)

        def last(i, out):
            a, b, r, cols, one, two, three = steps[i]
            landed(three)
            for q, R in ((a, A3), (b, B3)):
                out[q, cols] = G[y, z, x, q, cols].astype(FULL) + R[r, cols].astype(FULL)

        return go, second, third_step, last, middle

    rp = reduce_wide(Gp, by_rows, RpA1, RpB1, RpA2, RpB2, RpA3, RpB3, RpEA, RpEB)
    rf = reduce_copies(Gf, by_rows, RfA1, RfB1, RfA2, RfB2, Rf3)
    weight_grad(T0, H, Gp, 0, width)
    rp[0](0)
    transpose_all(N2, T1)
    all_in(pw)
    rp[0](1)


    def pair_nt(A, W, columns):
        def block(flat):
            return dot_nt(A[0, flat, :columns], W[0].reshape(width, W.shape[-1])) + dot_nt(
                A[1, flat, :columns], W[1].reshape(width, W.shape[-1])
            )

        return block

    @pl.loop(0, 4)
    def _(k):
        b, h = k // 2, k % 2
        flat = pl.ds(pl.multiple_of(h * half, half), half)
        g = (dot(COT[h], Wp[b].reshape(width, width)) * GPR[b, flat, :]).astype(LOW)
        PG[b, flat, :] = g
        VG[pl.ds(FCB + b, 1), :] += jnp.sum(g.astype(FULL), axis=0, keepdims=True)

    p2_c = [copy(parts[3], V1, cdev)]
    split_rows(pair_nt(PG, Wf, width), parts[3], parts[0], p2_c)
    rp[1](0)
    weight_grad(T1, PG, Gf, 0, width)
    rf[0](0)
    rf[0](1)
    landed(p2_c)

    sent(n2_c)

    def norm_back(dy, n, rstd, gain):
        e = dy * gain
        return (e - jnp.mean(e, axis=-1, keepdims=True) - n * jnp.mean(e * n, axis=-1, keepdims=True)) * rstd

    def add_row(i, v):
        VG[i : i + 1, :] += jnp.sum(v, axis=0, keepdims=True)

    @pl.loop(0, half // 128)
    def _(i):
        r = row_tile(i)
        dy = GPR[0, r, :] + V1[r, :]
        n = N2F[r, :]
        add_row(GAIN2, dy * n)
        add_row(SHIFT2, dy)
        cot = COT[c, r, :].astype(FULL)
        add_row(PROJB, cot)
        g = cot + norm_back(dy, n, RS[r, 1:2], vrow(GAIN2))
        N2F[r, :] = g
        low = g.astype(LOW)
        add_row(OUTB, low.astype(FULL))
        N2[c, r, :] = low

    ag_c = [copy(N2.at[c], N2.at[c], cdev)]
    start(ag_c)

    def vector_copies(first, last):
        r = pl.ds(first, last - first)
        over_z = [Group([(VG.at[r], VZ.at[k - 1, r], zdev(k)) for k in range(1, ZN)], VZ.at[:, r])]
        mine = VO.at[(y * 2 + x) * 2 + c, r]
        return r, over_z, mine, [Group([(mine, mine, d) for d in near], VO.at[pl.ds(0, 7), r])]

    def vector_second(v):
        r, over_z, mine, over_near = v
        landed(over_z)
        mine[...] = VG[r, :] + VZ[0, r, :] + VZ[1, r, :] + VZ[2, r, :]
        start(over_near)

    def vector_last(v):
        r, over_z, mine, over_near = v
        landed(over_near)
        for core in range(2):
            vo_ref[core, r, :] = (VO[core, r, :] + VO[2 + core, r, :]) + (VO[4 + core, r, :] + VO[6 + core, r, :])

    late = vector_copies(0, 4)
    er = pl.ds(8, VEC - 8)
    early = [
        [Group([(VG.at[er], VZ.at[k - 1, er], zdev(k)) for k in range(1, ZN)], VZ.at[:, er])],
        [copy(VO.at[0, er], VO.at[1, er], xdev)],
        [copy(VO.at[2, er], VO.at[3, er], ydev)],
        [copy(vo_ref.at[c, er], vo_ref.at[c, er], cdev)],
    ]
    start(early[0])

    def early_hop(i):
        landed(early[i])
        if i == 0:
            VO[0, er, :] = VG[er, :] + VZ[0, er, :] + VZ[1, er, :] + VZ[2, er, :]
        elif i == 1:
            VO[2, er, :] = VO[0, er, :] + VO[1, er, :]
        else:
            vo_ref[c, er, :] = VO[2, er, :] + VO[3, er, :]
        start(early[i + 1])

    pm_c = [copy(parts[1], V0, cdev)]
    split_rows(pair_nt(H, Wp, width), parts[1], MID, pm_c, MID)
    rp[1](1)
    transpose_all(N1, T1)
    landed(ag_c)

    @pl.loop(0, nrb)
    def _(i):
        h, off = i // (half // rblk), i % (half // rblk)
        rows = pl.ds(pl.multiple_of(off * rblk, rblk), rblk)
        flat = pl.ds(pl.multiple_of(i * rblk, rblk), rblk)
        g = dot(N2[h, rows, :], Wo[...].reshape(width, Wo.shape[-1])).astype(LOW)
        row = lax.broadcasted_iota(jnp.int32, (8, 128), 0)
        lane = lax.broadcasted_iota(jnp.int32, (8, 128), 1)
        pick = jnp.where(lane // HD == row, 1.0, 0.0).astype(LOW)
        for p in range(3):
            gp = tile(g, p)
            DO[p, flat, :] = gp
            prod = gp.astype(FULL) * CTX[p, flat, :].astype(FULL)
            high = prod.astype(LOW)
            rest = (prod - high.astype(FULL)).astype(LOW)
            d = dot_nt(pick, high) + dot_nt(pick, rest)
            for e in range(2):
                DELR[2 * p + e, :, flat] = d[e : e + 1, :]

    transpose_all(N2, T0)

    @pl.loop(0, 2)
    def _(m):
        rows = pl.ds(pl.multiple_of(m * (width // 2), width // 2), width // 2)
        g = dot(T0[rows, :], wide(CTX, pl.ds(0, seq_len)))
        g = g.astype(LOW).reshape(ZN // 2, XN, 2, width // (2 * GROUPS), Wo.shape[-1])
        Go[pl.ds(m * (ZN // 2), ZN // 2)] = g

    ro = [
        [copy(Go.at[:, :, oy, oa], Ro1A, ydev), copy(Go.at[:, ox, :, ob], Ro1B, xdev)],
        [copy(Go.at[:, ox, y, oa], Ro2A, xdev), copy(Go.at[:, x, oy, ob], Ro2B, ydev)],
        [Group([(Go.at[(z + k) % ZN, x, y], Ro3.at[k - 1], zdev(k)) for k in range(1, ZN)], Ro3)],
        [Group([(go_ref.at[t], go_ref.at[t], d) for d in (cdev, ydev, gdev)], go_ref.at[pl.ds(0, 3)])],
    ]

    def ro_second():
        landed(ro[0])

        @pl.loop(0, ZN)
        def _(k):
            for i in range(XN):
                Go[k, i, y, oa] = (Go[k, i, y, oa].astype(FULL) + Ro1A[k, i].astype(FULL)).astype(LOW)
                Go[k, x, i, ob] = (Go[k, x, i, ob].astype(FULL) + Ro1B[k, i].astype(FULL)).astype(LOW)

        start(ro[1])

    def ro_third():
        landed(ro[1])

        @pl.loop(0, ZN)
        def _(k):
            Go[k, x, y, oa] = (Go[k, x, y, oa].astype(FULL) + Ro2A[k].astype(FULL)).astype(LOW)
            Go[k, x, y, ob] = (Go[k, x, y, ob].astype(FULL) + Ro2B[k].astype(FULL)).astype(LOW)

        start(ro[2])

    def ro_last():
        landed(ro[2])
        v = Go[z, x, y].astype(FULL)
        for k in range(ZN - 1):
            v = v + Ro3[k].astype(FULL)
        go_ref[t] = v
        start(ro[3])

    def attention_back(p, plan):
        DQ[...] = jnp.zeros(DQ.shape, FULL)
        for b in range(nrb):
            rows = pl.ds(b * rblk, rblk)
            first = 0 if b * rblk < half else b * rblk
            n = seq_len - first
            keys, values = KP[p, rows, :], VP[p, rows, :]
            queries, grads = QP[p, first:, :], DO[p, first:, :]
            key = b * rblk + lax.broadcasted_iota(jnp.int32, (rblk, 1), 0)
            limit = jnp.where(key < prefix, 0, key)
            shut = (b + 1) * rblk - first
            query = first + lax.broadcasted_iota(jnp.int32, (rblk, shut), 1)
            dk, dv = [], []
            for e in range(2):
                ke, ve = lane_part(keys, e), lane_part(values, e)
                sc = dot_nt(ke, queries) - LSER[2 * p + e, :, first:]
                head = jnp.where(query >= limit, sc[:, :shut], -1e30)
                w = jnp.exp(jnp.concatenate([head, sc[:, shut:]], axis=1) if shut < n else head)
                dw = dot_nt(ve, grads) - DELR[2 * p + e, :, first:]
                ds = (w * dw).astype(LOW)
                dv.append(dot(w.astype(LOW), grads))
                dk.append(dot(ds, queries))
                DQ[first:, :] += dot_tn(ds, ke)
            KP[p, rows, :] = jnp.where(low_lanes(dk[0]), dk[0], dk[1]).astype(LOW)
            VP[p, rows, :] = jnp.where(low_lanes(dv[0]), dv[0], dv[1]).astype(LOW)
            meanwhile(p, b, plan)
        QP[p, :, :] = (DQ[...] * 0.125).astype(LOW)

    away = {
        (0, 0): [lambda: rp[4](0), lambda: rf[1](0)],
        (0, 3): [lambda: start(ro[0]), lambda: early_hop(0)],
        (1, 0): [lambda: rf[1](1)],
        (1, 1): [lambda: rp[4](1)],
        (1, 2): [lambda: rf[2](0)],
        (1, 3): [lambda: early_hop(1)],
    }

    @pl.loop(0, 2)
    def _(p):
        attention_back(p, away)

    packed = Wq.shape[-1]
    sent_all(fw)

    @pl.loop(0, nrb)
    def _(i):
        flat = pl.ds(pl.multiple_of(i * rblk, rblk), rblk)
        for b in range(2):
            for k, ref in enumerate((QP, KP, VP)):
                g = ref[b, flat, :]
                H[b, flat, k * 128 : (k + 1) * 128] = g
                VG[QKVB + b : QKVB + b + 1, k * 128 : (k + 1) * 128] += jnp.sum(g.astype(FULL), axis=0, keepdims=True)

    main, rest = pl.ds(0, 384), pl.ds(384, packed - 384)
    by_lanes = [pairs[0] + (pl.ds(0, third), main), pairs[1] + (pl.ds(third, 2 * third), main)]
    by_lanes += [pairs[1] + (pl.ds(third, 2 * third), rest), pairs[0] + (pl.ds(0, third), rest)]
    weight_grad(T1, H, Wf, 0, 384)
    rq = reduce_copies(Wf, by_lanes, RqA1, RqB1, RqA2, RqB2, Rq3)
    rq[0](0)
    rq[0](1)
    landed(pm_c)

    @pl.loop(0, half // 128)
    def _(i):
        r = row_tile(i)
        TOK[r, :] = (MID[r, :] + (V0[r, :] + vrow(PROJB))).astype(LOW)

    out_c = [pltpu.make_async_copy(TOK, bo_h, ls.at[0]), pltpu.make_async_copy(N1.at[c], ig_h, ls.at[1])]
    out_c[0].start()

    away = {
        (2, 0): [lambda: rf[2](1)],
        (2, 1): [lambda: early_hop(2), ro_second],
        (2, 3): [lambda: rp[2](0), lambda: rq[1](0)],
    }
    attention_back(2, away)

    @pl.loop(0, nrb)
    def _(i):
        flat = pl.ds(pl.multiple_of(i * rblk, rblk), rblk)
        q, k, v = (ref[2, flat, :].astype(FULL) for ref in (QP, KP, VP))
        first = low_lanes(q)
        packs = (
            (jnp.where(first, q, roll(k)), jnp.where(first, v, 0.0)),
            (jnp.where(first, roll(q), k), jnp.where(first, roll(v), 0.0)),
        )
        for b in range(2):
            for j in range(2):
                at_j = slice(384 + 128 * j, 512 + 128 * j)
                H[b, flat, at_j] = packs[b][j].astype(LOW)
                VG[QKVB + b : QKVB + b + 1, at_j] += jnp.sum(packs[b][j], axis=0, keepdims=True)

    weight_grad(T1, H, Wf, 384, packed)
    rq[0](2)
    rq[0](3)
    rq[1](1)

    p1_c = [copy(parts[1], V1, cdev)]
    sent(pm_c)
    split_rows(pair_nt(H, Wq, packed), parts[1], parts[2], p1_c)
    rq[2](0)
    rp[2](1)
    ro_third()
    landed(p1_c)

    sent(n1_c)

    @pl.loop(0, half // 128)
    def _(i):
        r = row_tile(i)
        dy = GPR[1, r, :] + V1[r, :]
        n = N1F[r, :]
        add_row(GAIN1, dy * n)
        add_row(SHIFT1, dy)
        N1[c, r, :] = (N2F[r, :] + norm_back(dy, n, RS[r, 0:1], vrow(GAIN1))).astype(LOW)

    out_c[1].start()

    start(late[1])
    rq[2](1)
    rq[1](2)
    rq[1](3)
    gp_ref, gf_ref = MID.at[pl.ds(0, 2 * hr)], MID.at[pl.ds(2 * hr, 2 * hr)]
    out_c += [pltpu.make_async_copy(gp_ref, gp_h, ls.at[2]), pltpu.make_async_copy(gf_ref, gf_h, ls.at[3])]
    rp[3](0, gp_ref)
    rp[3](1, gp_ref)
    out_c[2].start()
    rf[3](0, gf_ref)
    rf[3](1, gf_ref)
    out_c[3].start()
    rq[2](2)
    rq[2](3)
    vector_second(late)
    ro_last()
    landed(early[3])
    landed(ro[3])
    out_c += [
        pltpu.make_async_copy(a, b, ls.at[4 + i]) for i, (a, b) in enumerate(((go_ref, go_h), (gq_ref, gq_h), (vo_ref, vo_h)))
    ]
    out_c[4].start()
    rq[3](0, gq_ref)
    rq[3](1, gq_ref)
    vector_last(late)
    out_c[6].start()
    rq[3](2, gq_ref)
    rq[3](3, gq_ref)
    out_c[5].start()

    waited = {id(m) for m in n2_c + pm_c + n1_c}
    for step in fw:
        for group in step:
            waited |= {id(m) for m in group}
    sent([m for m in pending if id(m) not in waited])
    for cp in out_c:
        cp.wait()


def gather_groups(v, axis, repeat, groups):
    if repeat == 1:
        return v
    return lax.all_gather(v, "dp", axis=axis, axis_index_groups=groups, tiled=True)


def scatter_groups(v, axis, repeat, groups):
    if repeat == 1:
        return v
    return lax.psum_scatter(v, "dp", scatter_dimension=axis, axis_index_groups=groups, tiled=True)


def on_device(
    dp_size,
    tokens,
    prefix,
    cotangent,
    first_gain,
    first_shift,
    qkv_weight,
    qv_bias,
    out_weight,
    out_bias,
    second_gain,
    second_shift,
    fc_weight,
    fc_bias,
    proj_weight,
    proj_bias,
):
    repeat = dp_size // GROUPS
    groups = [[g * repeat + i for i in range(repeat)] for g in range(GROUPS)]
    half, width = tokens.shape
    seq_len = 2 * half

    def whole(v, axis):
        return gather_groups(v.astype(LOW), axis, repeat, groups).astype(FULL) if repeat > 1 else v

    params = [
        whole(first_gain, 0), whole(first_shift, 0), whole(qkv_weight, 1), whole(qv_bias, 1), whole(out_weight, 1),
        whole(out_bias, 0), whole(second_gain, 0), whole(second_shift, 0), whole(fc_weight, 0), whole(fc_bias, 0),
        whole(proj_weight, 1), whole(proj_bias, 0),
    ]
    params[4], params[10] = params[4].T, params[10].T
    rows = params[8].shape[0]
    cols = params[2].shape[2]
    units = params[8].shape[1]
    pair = 2 * HD
    packed, own = 3 * cols + HD, 2 * cols
    hr = rows // 2
    ANY = pl.BlockSpec(memory_space=pl.ANY)

    def reduce_space(lanes):
        return [
            pltpu.VMEM((2, ZN, hr, lanes), LOW),
            pltpu.VMEM((ZN, XN, hr, lanes), LOW),
            pltpu.VMEM((ZN, hr, lanes), LOW),
            pltpu.VMEM((ZN, hr, lanes), LOW),
            pltpu.VMEM((ZN - 1, rows, lanes), LOW),
        ]

    token_low = pltpu.VMEM((2, half, width), LOW)
    token_full = pltpu.VMEM((half, width), FULL)
    unit_low = pltpu.VMEM((2, seq_len, width), LOW)
    heads = pltpu.VMEM((3, seq_len, pair), LOW)
    scratch = (
        [
            pltpu.VMEM((2, ZN, XN, rows, packed), LOW),
            pltpu.VMEM((ZN, XN, 2, hr, own), LOW),
            pltpu.VMEM((2, ZN, XN, rows, width), LOW),
            pltpu.VMEM((2, ZN, XN, rows, width), LOW),
            pltpu.VMEM((ZN, XN, 2, hr, own), LOW),
            pltpu.VMEM((2, ZN, XN, rows, width), LOW),
            pltpu.VMEM((2, ZN, XN, rows, width), LOW),
        ]
        + reduce_space(packed)
        + reduce_space(width)
        + [
            pltpu.VMEM((ZN, XN, hr, width), LOW),
            pltpu.VMEM((2, ZN, hr, width), LOW),
            pltpu.VMEM((ZN - 1, XN, hr, width), LOW),
            pltpu.VMEM((ZN - 1, 2, hr, width), LOW),
            pltpu.VMEM((hr, width), LOW),
            pltpu.VMEM((hr, width), LOW),
            pltpu.VMEM((XN, hr, width), LOW),
            pltpu.VMEM((2, hr, width), LOW),
        ]
        + [
            pltpu.VMEM((ZN, XN, hr // 3 * 2, own), LOW),
            pltpu.VMEM((ZN, 2, hr // 3, own), LOW),
            pltpu.VMEM((ZN, hr // 3 * 2, own), LOW),
            pltpu.VMEM((ZN, hr // 3, own), LOW),
            pltpu.VMEM((ZN - 1, hr, own), LOW),
        ]
        + [
            pltpu.VMEM((half, width), LOW),
            token_low,
            token_full,
            token_full,
            pltpu.VMEM((half, 128), FULL),
            token_low,
            token_low,
            pltpu.VMEM((width, seq_len), LOW),
            pltpu.VMEM((width, seq_len), LOW),
        ]
        + [heads] * 5
        + [
            pltpu.VMEM((seq_len, pair), FULL),
            pltpu.VMEM((6, 1, seq_len), FULL),
            pltpu.VMEM((6, 1, seq_len), FULL),
        ]
        + [token_full] * 3
        + [unit_low, pltpu.VMEM((2, seq_len, width), FULL), unit_low]
        + [
            pltpu.VMEM((8, rows), FULL),
            pltpu.VMEM((2, rows), FULL),
            pltpu.VMEM((1, 4 * rows), FULL),
            pltpu.VMEM((3, rows, cols), FULL),
            pltpu.VMEM((2, hr, own), LOW),
            pltpu.VMEM((3, half, pair), LOW),
            pltpu.VMEM((ZN, XN, 2, hr, own), LOW),
            pltpu.VMEM((GROUPS, VEC, 128), LOW),
            pltpu.VMEM((VEC, width), FULL),
            pltpu.VMEM((VEC, width), FULL),
            pltpu.VMEM((ZN - 1, VEC, width), FULL),
        ]
        + [
            pltpu.VMEM((8, VEC, width), FULL),
            pltpu.VMEM((rows, packed), FULL),
            pltpu.VMEM((4, hr, own), FULL),
            pltpu.VMEM((2, VEC, width), FULL),
            pltpu.SMEM(prefix.shape, prefix.dtype),
        ]
        + [
            pltpu.SemaphoreType.DMA((SEMS,)),
            pltpu.SemaphoreType.DMA((SEMS,)),
            pltpu.SemaphoreType.DMA((16,)),
        ]
    )
    out_shape = [
        jax.ShapeDtypeStruct((half, width), LOW),
        jax.ShapeDtypeStruct((half, width), LOW),
        jax.ShapeDtypeStruct((rows, packed), FULL),
        jax.ShapeDtypeStruct((4, hr, own), FULL),
        jax.ShapeDtypeStruct((rows, width), FULL),
        jax.ShapeDtypeStruct((rows, width), FULL),
        jax.ShapeDtypeStruct((2, VEC, width), FULL),
    ]
    grown = pl.pallas_call(
        functools.partial(block_kernel, repeat, seq_len),
        out_shape=out_shape,
        in_specs=[ANY] * 15,
        out_specs=[ANY] * 7,
        scratch_shapes=scratch,
        compiler_params=pltpu.CompilerParams(
            collective_id=0, has_side_effects=True, vmem_limit_bytes=62 * 1024 * 1024
        ),
    )(tokens, prefix, cotangent, *params)

    vector = jax.ShapeDtypeStruct((rows,), FULL)
    results = pl.pallas_call(
        functools.partial(unpack_kernel, repeat),
        out_shape=[
            out_shape[0],
            out_shape[1],
            vector,
            vector,
            jax.ShapeDtypeStruct((3, rows, cols), FULL),
            jax.ShapeDtypeStruct((2, rows), FULL),
            jax.ShapeDtypeStruct((rows, width), FULL),
            vector,
            vector,
            vector,
            jax.ShapeDtypeStruct((rows, units), FULL),
            jax.ShapeDtypeStruct((4 * rows,), FULL),
            jax.ShapeDtypeStruct((rows, units), FULL),
            vector,
        ],
        in_specs=[ANY] * 7,
        out_specs=[ANY] * 14,
        scratch_shapes=[
            pltpu.VMEM((rows, packed), FULL),
            pltpu.VMEM((4, hr, own), FULL),
            pltpu.VMEM((2, VEC, width), FULL),
            pltpu.VMEM((3, rows, cols), FULL),
            pltpu.VMEM((rows, width), FULL),
            pltpu.VMEM((half, width), LOW),
            pltpu.VMEM((half, width), LOW),
            pltpu.VMEM((rows, units), FULL),
            pltpu.VMEM((rows, units), FULL),
            pltpu.VMEM((8, rows), FULL),
            pltpu.VMEM((2, rows), FULL),
            pltpu.VMEM((1, 4 * rows), FULL),
            pltpu.SemaphoreType.DMA((21,)),
        ],
        compiler_params=pltpu.CompilerParams(vmem_limit_bytes=62 * 1024 * 1024),
    )(*grown)
    results = [v.T if i in (6, 12) else v for i, v in enumerate(results)]
    along = (None, None, 0, 0, 1, 1, 1, 0, 0, 0, 0, 0, 1, 0)
    return tuple(
        v if repeat == 1 or axis is None else scatter_groups(v, axis, repeat, groups)
        for v, axis in zip(results, along, strict=True)
    )


def unpack_kernel(
    repeat, bo, ig, gq_h, go_h, gf, gp, vo_h,
    bo_out, ig_out, gain1, shift1, wq_h, qvb_h, wo_h, outb, gain2, shift2, wf, fcb_h, wp, projb,
    gq, go, vo, wq, wo, b1, b2, w1, w2, sv, sq, sf, sems,
):
    moves = [(vo_h, vo), (gq_h, gq), (go_h, go), (ig, b2), (bo, b1), (gf, w1), (gp, w2)]
    moves += [(wq, wq_h), (wo, wo_h), (b2, ig_out), (b1, bo_out), (w1, wf), (w2, wp)]
    vectors = ((GAIN1, gain1), (SHIFT1, shift1), (OUTB, outb), (GAIN2, gain2), (SHIFT2, shift2), (PROJB, projb))
    moves += [(sv.at[j], out) for j, (_, out) in enumerate(vectors)] + [(sq, qvb_h), (sf.at[0], fcb_h)]
    moves = [pltpu.make_async_copy(a, b, sems.at[i]) for i, (a, b) in enumerate(moves)]
    for cp in moves[:7]:
        cp.start()
    moves[1].wait()
    for k in range(3):
        wq[k] = jnp.concatenate(
            [gq[:, k * 128 : (k + 1) * 128], gq[:, 384 + k * HD : 384 + (k + 1) * HD]], axis=1
        )
    moves[7].start()
    for i in (3, 4):
        moves[i].wait()
        moves[i + 6].start()
    moves[2].wait()
    m = [jnp.concatenate([go[core], go[2 + core]], axis=0) for core in range(2)]
    wo[...] = jnp.concatenate(
        [
            v
            for b in range(2)
            for core in range(2)
            for v in (m[core][:, b * 128 : (b + 1) * 128], m[core][:, 256 + b * HD : 256 + (b + 1) * HD])
        ],
        axis=1,
    )
    moves[8].start()
    for i in (5, 6):
        moves[i].wait()
        moves[i + 6].start()
    moves[0].wait()
    s = lax.axis_index("dp") // repeat
    width = vo.shape[2]
    n = sv.shape[1]
    both = pltpu.roll(vo[0] + vo[1], (GROUPS - s) % GROUPS * n, 1)
    for j, (i, _) in enumerate(vectors):
        sv[j : j + 1, :] = both[i : i + 1, :n]
    owner = s // 2
    core, b, odd = owner % 2, owner // 2, s % 2
    place = lax.broadcasted_iota(jnp.int32, (1, width), 1)

    def lanes(v, first, last, shift):
        v = jnp.where((place >= first) & (place < last), v, 0.0)
        return pltpu.roll(v, shift % width, 1) if shift % width else v

    row = vo[core, pl.ds(QKVB + b, 1), :]
    q = lanes(row, 0, 128, 0) + lanes(row, 384, 448, -256)
    v = lanes(row, 256, 384, -256) + lanes(row, 512, 576, -384)
    back = (width - odd * n) % width
    sq[0:1, :] = pltpu.roll(q, back, 1)[:, :n]
    sq[1:2, :] = pltpu.roll(v, back, 1)[:, :n]
    row = vo[core, pl.ds(FCB + b, 1), :]
    sf[...] = pltpu.roll(row, odd * (width // 2), 1)[:, : width // 2]
    for i in range(13, 21):
        moves[i].start()
    for i in range(7, 21):
        moves[i].wait()


def solution(mesh):
    placed = (
        P(("dp", "tensor"), None),
        P("dp"),
        P(("dp", "tensor"), None),
        P("dp"),
        P("dp"),
        P(None, "dp", "tensor"),
        P(None, "dp"),
        P(None, "dp"),
        P("dp"),
        P("dp"),
        P("dp"),
        P("dp", "tensor"),
        P("dp"),
        P("tensor", "dp"),
        P("dp"),
    )
    return jax.shard_map(
        functools.partial(on_device, mesh.shape["dp"]),
        mesh=mesh,
        in_specs=placed,
        out_specs=(placed[0], placed[0]) + placed[3:],
        check_vma=False,
    )
```

```python
import functools
import math

import jax
import jax.numpy as jnp
from jax import lax
from jax.experimental import pallas as pl
from jax.experimental.pallas import tpu as pltpu
from jax.sharding import PartitionSpec as P

MESH = pl.DeviceIdType.MESH
LOW, FULL = jnp.bfloat16, jnp.float32
EPSILON = 1e-05
HD = 64
GROUPS, ZN, XN = 8, 4, 2
SEMS = 145
VEC = 16

GAIN1, SHIFT1, QKVB, OUTB, GAIN2, SHIFT2, PROJB, FCB = 0, 1, 2, 8, 9, 10, 11, 12


def dot(a, b):
    return jnp.dot(a, b, preferred_element_type=FULL)


def dot_nt(a, b):
    return lax.dot_general(a, b, (((1,), (1,)), ((), ())), preferred_element_type=FULL)


def dot_tn(a, b):
    return lax.dot_general(a, b, (((0,), (0,)), ((), ())), preferred_element_type=FULL)


def block_kernel(repeat, seq_len, *refs):
    (
        tok_h, prefix_h, cot_h, gain1_h, shift1_h, wq_h, qvb_h, wo_h, outb_h,
        gain2_h, shift2_h, wf_h, fcb_h, wp_h, projb_h,
        bo_h, ig_h, gq_h, go_h, gf_h, gp_h, vo_h,
        Wq, Wo, Wf, Wp, Go, Gp, Gf,
        RqA1, RqB1, RqA2, RqB2, Rq3,
        RfA1, RfB1, RfA2, RfB2, Rf3,
        RpA1, RpB1, RpA2, RpB2, RpA3, RpB3, RpEA, RpEB,
        Ro1A, Ro1B, Ro2A, Ro2B, Ro3,
        TOK, COT, N1F, N2F, RS, N1, N2, T0, T1,
        QP, KP, VP, CTX, DO, DQ, LSER, DELR,
        MID, V0, V1, H, GPR, PG,
        SV, SB, SC, SQ, SW, CTXP, WOP,
        VR, VF, VG, VZ, VO, gq_ref, go_ref, vo_ref, prefix_s,
        ss, rs, ls,
    ) = refs
    half = seq_len // 2
    width = TOK.shape[1]
    rblk = 256
    nrb = seq_len // rblk
    dp = lax.axis_index("dp")
    t = lax.axis_index("tensor")
    s, sub = dp // repeat, dp % repeat
    z, x = s // XN, s % XN
    y, c = t // 2, t % 2
    oy, oc, ox = 1 - y, 1 - c, 1 - x

    def at(zz, xx, tt):
        return ((zz * XN + xx) * repeat + sub, tt)

    def zdev(k):
        return at((z + k) % ZN, x, t)

    xdev = at(z, ox, t)
    ydev = at(z, x, oy * 2 + c)
    cdev = at(z, x, y * 2 + oc)
    gdev = at(z, x, oy * 2 + oc)
    near = [xdev, ydev, cdev, gdev] + [at(z, ox, i * 2 + j) for i, j in ((y, oc), (oy, c), (oy, oc))]
    others = [(((s + k) % GROUPS) * repeat + sub, t) for k in range(1, GROUPS)]

    count = [0]
    pending = []

    class Copy:
        def __init__(self, src, dst, dev, recv=None, alone=True):
            self.k = count[0]
            count[0] += 1
            self.parts = src, dst, dev, self.k if recv is None else recv.k
            if alone:
                pending.append(self)

        def made(self):
            src, dst, dev, recv = self.parts
            return pltpu.make_async_remote_copy(
                src_ref=src, dst_ref=dst, send_sem=ss.at[self.k], recv_sem=rs.at[recv],
                device_id=dev, device_id_type=MESH,
            )

        def start(self):
            self.made().start()

        def landed(self):
            self.made().wait_recv()

        def sent(self):
            self.made().wait_send()

    class Group:
        def __init__(self, moves, every):
            k = count[0]
            count[0] += 1
            self.moves = [Copy(*m, alone=False) for m in moves]
            for m in self.moves:
                m.k, m.parts = k, m.parts[:3] + (k,)
            count[0] = k + 1
            self.every = Copy(every, every, moves[0][2], alone=False)
            self.every.k, self.every.parts = k, self.every.parts[:3] + (k,)
            count[0] = k + 1
            pending.append(self)

        def start(self):
            for m in self.moves:
                m.start()

        def landed(self):
            self.every.landed()

        def sent(self):
            self.every.sent()

    class ZGather:
        def __init__(self, block):
            self.to = [Copy(block(z), block(z), zdev(k), alone=False) for k in range(1, ZN)]
            self.up = Copy(block(0), block(0), at(3, x, t), self.to[2], False)
            self.down = Copy(block(3), block(3), at(0, x, t), self.to[0], False)
            pending.append(self)

        def each(self, act):
            act(self.to[1])
            pl.when(z != 3)(lambda: act(self.to[0]))
            pl.when(z != 0)(lambda: act(self.to[2]))

        def start(self):
            self.each(lambda m: m.start())

        def middle(self):
            def go_on(onward):
                landed(self.to[1:2])
                onward.start()

            pl.when(z == 2)(lambda: go_on(self.up))
            pl.when(z == 1)(lambda: go_on(self.down))

        def landed(self):
            pl.when((z == 0) | (z == 3))(self.to[1].landed)
            self.to[0].landed()
            self.to[2].landed()

        def sent(self):
            self.each(lambda m: m.sent())
            pl.when(z == 2)(self.up.sent)
            pl.when(z == 1)(self.down.sent)

    class ZReduce:
        def __init__(self, block, arrived, extra):
            self.block, self.extra = block, extra
            self.to = [Copy(block((z + k) % ZN), arrived(k - 1), zdev(k), alone=False) for k in range(1, ZN)]
            self.up = Copy(block(3), extra, at(1, x, t), alone=False)
            self.down = Copy(block(0), extra, at(2, x, t), alone=False)
            pending.append(self)

            def none(slot):
                arrived(slot)[...] = jnp.zeros(extra.shape, LOW)

            pl.when(z == 0)(lambda: none(0))
            pl.when(z == 3)(lambda: none(2))

        def start(self):
            pl.when(z != 3)(self.to[0].start)
            pl.when(z != 0)(self.to[2].start)
            pl.when(z == 0)(self.up.start)
            pl.when(z == 3)(self.down.start)
            pl.when((z == 0) | (z == 3))(self.to[1].start)

        def middle(self):
            def go_on(arrival, owner):
                landed([arrival])
                target = self.block(owner)
                target[...] = (target[...].astype(FULL) + self.extra[...].astype(FULL)).astype(LOW)
                self.to[1].start()

            pl.when(z == 1)(lambda: go_on(self.up, 3))
            pl.when(z == 2)(lambda: go_on(self.down, 0))

        def landed(self):
            self.to[1].landed()
            pl.when(z != 0)(self.to[0].landed)
            pl.when(z != 3)(self.to[2].landed)

        def sent(self):
            self.to[1].sent()
            pl.when(z != 3)(self.to[0].sent)
            pl.when(z != 0)(self.to[2].sent)
            pl.when(z == 0)(self.up.sent)
            pl.when(z == 3)(self.down.sent)

    def copy(src, dst, dev):
        return Copy(src, dst, dev)

    def start(moves):
        for m in moves:
            m.start()

    def landed(moves):
        for m in moves:
            m.landed()

    def sent(moves):
        for m in moves:
            m.sent()

    barrier = pltpu.get_barrier_semaphore()
    peers = others + [d for i, d in enumerate(near) if i != 0]
    for d in peers:
        pl.semaphore_signal(barrier, inc=1, device_id=d, device_id_type=MESH)

    SO, SF, SP = (GPR.at[0, pl.ds(i * wo_h.shape[0], wo_h.shape[0])] for i in range(3))
    brought = [
        (wq_h, SQ), (qvb_h, SB), (fcb_h, SC.at[0]),
        (gain1_h, SV.at[0]), (shift1_h, SV.at[1]), (outb_h, SV.at[2]),
        (gain2_h, SV.at[3]), (shift2_h, SV.at[4]), (projb_h, SV.at[5]),
        (wo_h, SO), (tok_h, TOK), (cot_h, COT.at[c]), (wf_h, SF), (wp_h, SP),
        (prefix_h, prefix_s),
    ]
    local = [pltpu.make_async_copy(a, b, ls.at[i]) for i, (a, b) in enumerate(brought)]
    for cp in local:
        cp.start()

    lanes96 = SV.shape[1]
    VG[...] = jnp.zeros(VG.shape, FULL)
    for cp in local[1:9]:
        cp.wait()
    VG[0:6, :lanes96] = SV[0:6, :]
    VG[6:8, :lanes96] = SB[...]
    for j in range(4):
        VG[8 + j : 9 + j, :lanes96] = SC[:, j * lanes96 : (j + 1) * lanes96]
    VR[s] = VG[:, :128].astype(LOW)
    VG[...] = jnp.zeros(VG.shape, FULL)
    local[0].wait()
    q3 = SQ[...]
    Wq[y, z, x] = jnp.concatenate(
        [q3[0, :, :128], q3[1, :, :128], q3[2, :, :128]]
        + [q3[k, :, 128:] for k in range(3)]
        + [jnp.zeros((q3.shape[1], HD), FULL)],
        axis=1,
    ).astype(LOW)
    pl.semaphore_wait(barrier, len(peers))

    vec_c = [Group([(VR.at[s], VR.at[s], d) for d in others], VR.at[pl.ds(0, GROUPS - 1)])]
    cot_c = [copy(COT.at[c], COT.at[c], cdev)]
    hr = wq_h.shape[1] // 2
    third = hr // 3
    pairs = (
        (pl.ds(0, third), pl.ds(third, third)),
        (pl.ds(2 * third, 2 * third), pl.ds(4 * third, 2 * third)),
    )

    thin = [(pl.ds(2 * i * third, third), pl.ds((2 * i + 1) * third, third)) for i in range(3)]

    def gather(W, pairs):
        steps = []
        for a, b in pairs:
            r = pl.ds(a.start, a.size + b.size)
            mine = W.at[y, z, x, r]
            zs = [Group([(mine, mine, zdev(k)) for k in range(1, ZN)], W.at[y, pl.ds(0, ZN - 1), x, r])]
            one = [
                copy(W.at[y, :, x, a], W.at[y, :, x, a], xdev),
                copy(W.at[y, :, x, b], W.at[y, :, x, b], ydev),
            ]
            two = [
                copy(W.at[y, :, :, a], W.at[y, :, :, a], ydev),
                copy(W.at[:, :, x, b], W.at[:, :, x, b], xdev),
            ]
            steps.append((zs, one, two))
        return steps

    def gather_wide(W):
        steps = []
        for a, b in pairs:
            near = [
                copy(W.at[y, z, x, a], W.at[y, z, x, a], xdev),
                copy(W.at[y, z, x, b], W.at[y, z, x, b], ydev),
            ]
            zs = [ZGather(lambda i, a=a: W.at[y, i, :, a]), ZGather(lambda i, b=b: W.at[:, i, x, b])]
            far = [
                copy(W.at[y, :, :, a], W.at[y, :, :, a], ydev),
                copy(W.at[:, :, x, b], W.at[:, :, x, b], xdev),
            ]
            steps.append((near, zs, far))
        return steps

    oa, ob = pl.ds(0, 2 * third), pl.ds(2 * third, third)
    ow = [
        (
            [Group([(Wo.at[z, x, y], Wo.at[z, x, y], zdev(k)) for k in range(1, ZN)], Wo.at[pl.ds(0, ZN - 1), x, y])],
            [
                copy(Wo.at[:, x, y, oa], Wo.at[:, x, y, oa], xdev),
                copy(Wo.at[:, x, y, ob], Wo.at[:, x, y, ob], ydev),
            ],
            [
                copy(Wo.at[:, :, y, oa], Wo.at[:, :, y, oa], ydev),
                copy(Wo.at[:, x, :, ob], Wo.at[:, x, :, ob], xdev),
            ],
        )
    ]
    qw, pw, fw = gather(Wq, thin), gather_wide(Wp), gather(Wf, thin)

    def z_go(w, i):
        start(w[i][0])

    def one_go(w, i):
        landed(w[i][0])
        start(w[i][1])

    def two_go(w, i):
        n = len(w[i][1]) // len(w[i][2])
        for k, after in enumerate(w[i][2]):
            landed(w[i][1][k * n : (k + 1) * n])
            start([after])

    def all_in(w):
        for step in w:
            landed(step[2])

    def sent_all(w):
        for step in w:
            for group in step:
                sent(group)

    start(vec_c)
    z_go(qw, 0)
    local[9].wait()
    turned = pltpu.roll(SO[...], (width - c * (width // 4)) % width, 1)
    last = jnp.concatenate([turned[:, 128:192], turned[:, 512:576]], axis=1)
    mine = jnp.concatenate([turned[:, 0:128], turned[:, 384:512], last], axis=1).astype(LOW)
    SW[0] = mine[: SW.shape[1]]
    SW[1] = mine[SW.shape[1] :]
    Wo[z, x, y] = SW[y]
    local[12].wait()
    Wf[y, z, x] = SF[...].astype(LOW)
    local[13].wait()
    Wp[y, z, x] = SP[...].astype(LOW)
    local[10].wait()
    local[11].wait()
    local[14].wait()
    z_go(pw, 0)
    z_go(pw, 1)
    start(cot_c)

    def row_tile(i, n=128):
        return pl.ds(pl.multiple_of(i * n, n), n)

    @pl.loop(0, half // 128)
    def _(i):
        r = row_tile(i)
        v = TOK[r, :].astype(FULL)
        v = v - jnp.mean(v, axis=-1, keepdims=True)
        rstd = lax.rsqrt(jnp.mean(v * v, axis=-1, keepdims=True) + EPSILON)
        N1F[r, :] = v * rstd
        RS[r, 0:1] = rstd

    z_go(qw, 1)
    landed(vec_c)

    def widen(v):
        return jnp.concatenate([v, jnp.zeros((v.shape[0], width - v.shape[1]), FULL)], axis=1)

    pieces = [widen(VR[g].astype(FULL)) for g in range(GROUPS)]
    plain = pieces[0]
    for g in range(1, GROUPS):
        plain = plain + pltpu.roll(pieces[g], g * lanes96, 1)
    VF[GAIN1 : SHIFT1 + 1, :] = plain[0:2]
    VF[OUTB : PROJB + 1, :] = plain[2:6]
    place = lax.broadcasted_iota(jnp.int32, (1, width), 1)

    def lanes(v, first, last, shift):
        v = jnp.where((place >= first) & (place < last), v, 0.0)
        return pltpu.roll(v, shift % width, 1) if shift % width else v

    for b in range(2):
        a0, a1 = (widen(VR[2 * (2 * b + c) + i].astype(FULL)) for i in range(2))
        a1 = pltpu.roll(a1, lanes96, 1)
        qb, vb = a0[6:7] + a1[6:7], a0[7:8] + a1[7:8]
        VF[QKVB + b : QKVB + b + 1, :] = (
            lanes(qb, 0, 128, 0) + lanes(qb, 128, 192, 256) + lanes(vb, 0, 128, 256) + lanes(vb, 128, 192, 384)
        )
        a1 = pltpu.roll(a1, 3 * lanes96, 1)
        row = a0[8:9] + a1[8:9]
        for j in range(1, 4):
            row = row + pltpu.roll(a0[8 + j : 9 + j] + a1[8 + j : 9 + j], j * lanes96, 1)
        VF[FCB + b : FCB + b + 1, :] = row

    def vrow(i):
        return VF[i : i + 1, :]

    @pl.loop(0, half // 128)
    def _(i):
        r = row_tile(i)
        N1[c, r, :] = (N1F[r, :] * vrow(GAIN1) + vrow(SHIFT1)).astype(LOW)

    n1_c = [copy(N1.at[c], N1.at[c], cdev)]
    start(n1_c)

    def transpose_all(source, target):
        @pl.loop(0, nrb)
        def _(i):
            h, off = i // (half // rblk), i % (half // rblk)
            rows = pl.ds(pl.multiple_of(off * rblk, rblk), rblk)
            cols = pl.ds(pl.multiple_of(i * rblk, rblk), rblk)
            for k in range(width // rblk):
                target[k * rblk : (k + 1) * rblk, cols] = source[h, rows, k * rblk : (k + 1) * rblk].T

    landed(cot_c)
    one_go(qw, 0)
    transpose_all(COT, T0)
    one_go(qw, 1)
    z_go(qw, 2)
    two_go(qw, 0)
    z_go(fw, 0)
    two_go(qw, 1)
    z_go(ow, 0)
    one_go(qw, 2)
    z_go(fw, 1)
    landed(n1_c)
    two_go(qw, 2)
    z_go(fw, 2)
    one_go(fw, 0)
    all_in(qw)

    def low_lanes(v):
        return lax.broadcasted_iota(jnp.int32, v.shape, 1) < HD

    def tile(v, i):
        return v[:, i * 128 : (i + 1) * 128]

    def roll(v):
        return pltpu.roll(v, HD, 1)

    @pl.loop(0, nrb)
    def _(i):
        h, off = i // (half // rblk), i % (half // rblk)
        rows = pl.ds(pl.multiple_of(off * rblk, rblk), rblk)
        out = pl.ds(pl.multiple_of(i * rblk, rblk), rblk)
        n = N1[h, rows, :]
        got = []
        for b in range(2):
            got.append(dot(n, Wq[b].reshape(width, Wq.shape[-1])) + VF[QKVB + b : QKVB + b + 1, : Wq.shape[-1]])
            QP[b, out, :] = (tile(got[b], 0).astype(LOW).astype(FULL) * 0.125).astype(LOW)
            KP[b, out, :] = tile(got[b], 1).astype(LOW)
            VP[b, out, :] = tile(got[b], 2).astype(LOW)
        first = low_lanes(tile(got[0], 3))
        q = jnp.where(first, tile(got[0], 3), roll(tile(got[1], 3)))
        QP[2, out, :] = (q.astype(LOW).astype(FULL) * 0.125).astype(LOW)
        KP[2, out, :] = jnp.where(first, roll(tile(got[0], 3)), tile(got[1], 3)).astype(LOW)
        VP[2, out, :] = jnp.where(first, tile(got[0], 4), roll(tile(got[1], 4))).astype(LOW)

        @pl.when(i == 0)
        def _():
            one_go(ow, 0)
            one_go(fw, 1)
            one_go(pw, 0)

        @pl.when(i == 2)
        def _():
            two_go(fw, 0)

    prefix = prefix_s[y]
    LSEC = DQ
    LSEC[...] = jnp.zeros(LSEC.shape, FULL)

    def lane_part(v, e):
        lane = lax.broadcasted_iota(jnp.int32, v.shape, 1)
        keep = lane < HD if e == 0 else lane >= HD
        return jnp.where(keep, v, jnp.zeros_like(v))

    def meanwhile(p, b, plan):
        for (pp, bb), steps in plan.items():
            if bb != b:
                continue
            if isinstance(p, int):
                for step in steps:
                    step()
            else:

                @pl.when(p == pp)
                def _(steps=steps):
                    for step in steps:
                        step()

    ctx_c = [copy(CTX.at[p, pl.ds(oc * half, half)], CTXP.at[p], cdev) for p in range(3)]
    wo_c = [copy(Wo, WOP, cdev)]

    def share_out():
        all_in(ow)
        start(wo_c)

    def pass_on(i):
        for m in pw[i][1]:
            m.middle()

    fetch = {
        (0, 0): [lambda: one_go(fw, 2), lambda: two_go(ow, 0)],
        (0, 1): [lambda: two_go(fw, 1), lambda: one_go(pw, 1)],
        (0, 3): [lambda: start(ctx_c[0:1])],
        (1, 1): [lambda: pass_on(0)],
        (1, 2): [lambda: two_go(fw, 2)],
        (1, 3): [lambda: start(ctx_c[1:2])],
        (2, 0): [lambda: two_go(pw, 0)],
        (2, 1): [share_out],
        (2, 3): [lambda: start(ctx_c[2:3]), lambda: pass_on(1)],
    }

    @pl.loop(0, 3)
    def _(p):
        for b in range(nrb):
            rows = pl.ds(b * rblk, rblk)
            cols = max(half, (b + 1) * rblk)
            q = QP[p, rows, :]
            keys, values = KP[p, :cols, :], VP[p, :cols, :]
            query = b * rblk + lax.broadcasted_iota(jnp.int32, (rblk, 1), 0)
            limit = jnp.maximum(prefix - 1, query)
            free = b * rblk
            key = free + lax.broadcasted_iota(jnp.int32, (rblk, cols - free), 1)
            parts = []
            for e in range(2):
                sc = dot_nt(lane_part(q, e), keys)
                tail = jnp.where(key <= limit, sc[:, free:], -1e30)
                sc = jnp.concatenate([sc[:, :free], tail], axis=1) if free else tail
                peak = jnp.max(sc, axis=-1, keepdims=True)
                w = jnp.exp(sc - peak)
                total = jnp.sum(w, axis=-1, keepdims=True)
                parts.append(dot(w.astype(LOW), values) * (1.0 / total))
                lane = lax.broadcasted_iota(jnp.int32, (rblk, 128), 1)
                LSEC[rows, :] = jnp.where(lane == 2 * p + e, peak + jnp.log(total), LSEC[rows, :])
            CTX[p, rows, :] = jnp.where(low_lanes(parts[0]), parts[0], parts[1]).astype(LOW)
            meanwhile(p, b, fetch)

    for b in range(nrb):
        lt = LSEC[b * rblk : (b + 1) * rblk, :].T
        for h in range(6):
            LSER[h, :, b * rblk : (b + 1) * rblk] = lt[h : h + 1, :]
    def wide(ref, rows):
        return jnp.concatenate([ref[0, rows, :], ref[1, rows, :], ref[2, rows, :]], axis=1)

    def split_rows(make_block, away, home, copies, plus=None):
        per = half // rblk
        for which, target in ((oc, away), (c, home)):

            @pl.loop(0, per)
            def _(j):
                rows = pl.ds(pl.multiple_of(j * rblk, rblk), rblk)
                block = make_block(pl.ds(pl.multiple_of((which * per + j) * rblk, rblk), rblk))
                target[rows, :] = block if plus is None or target is away else block + plus[rows, :]

            if target is away:
                start(copies)

    parts = [GPR.at[b, pl.ds(i * half, half)] for b in range(2) for i in range(2)]
    landed(wo_c)
    landed(ctx_c)

    @pl.loop(0, half // rblk)
    def _(j):
        r = pl.ds(pl.multiple_of(j * rblk, rblk), rblk)
        flat = pl.ds(pl.multiple_of((c * (half // rblk) + j) * rblk, rblk), rblk)
        o = dot_nt(wide(CTX, flat), Wo[...].reshape(width, Wo.shape[-1]))
        o = o + dot_nt(wide(CTXP, r), WOP[...].reshape(width, Wo.shape[-1]))
        m = TOK[r, :].astype(FULL) + (o + vrow(OUTB))
        MID[r, :] = m
        v = m - jnp.mean(m, axis=-1, keepdims=True)
        rstd = lax.rsqrt(jnp.mean(v * v, axis=-1, keepdims=True) + EPSILON)
        n = v * rstd
        N2F[r, :] = n
        RS[r, 1:2] = rstd
        N2[c, r, :] = (n * vrow(GAIN2) + vrow(SHIFT2)).astype(LOW)

    n2_c = [copy(N2.at[c], N2.at[c], cdev)]
    start(n2_c)
    landed(n2_c)
    all_in(fw)

    parts = [GPR.at[b, pl.ds(i * half, half)] for b in range(2) for i in range(2)]
    root = math.sqrt(2.0 / math.pi)

    @pl.loop(0, nrb * 2)
    def _(k):
        @pl.when(k == 0)
        def _():
            two_go(pw, 1)

        b, i = k // nrb, k % nrb
        h, off = i // (half // rblk), i % (half // rblk)
        rows = pl.ds(pl.multiple_of(off * rblk, rblk), rblk)
        flat = pl.ds(pl.multiple_of(i * rblk, rblk), rblk)
        u = dot(N2[h, rows, :], Wf[b].reshape(width, width)) + VF[pl.ds(FCB + b, 1), :]
        uu = u * u
        a = 0.5 * jnp.tanh(u * (root + (root * 0.044715) * uu)) + 0.5
        H[b, flat, :] = (u * a).astype(LOW)
        GPR[b, flat, :] = a * (1.0 + (1.0 - a) * (u * (2.0 * root + (2.0 * root * 0.134145) * uu)))

    def weight_grad(left_t, right, G, first, last):
        @pl.loop(0, 2)
        def _(b):
            g = dot(left_t[...], right[b, :, first:last])
            G[b, :, :, :, first:last] = g.astype(LOW).reshape(ZN, XN, width // GROUPS, last - first)

    every = pl.ds(0, width)
    by_rows = [pairs[0] + (pl.ds(0, third), every), pairs[1] + (pl.ds(third, 2 * third), every)]

    def reduce_copies(G, plan, A1, B1, A2, B2, R3):
        steps = []
        for a, b, r, cols in plan:
            one = [
                copy(G.at[:, :, ox, a, cols], A1.at[:, :, r, cols], xdev),
                copy(G.at[oy, :, :, b, cols], B1.at[:, :, r, cols], ydev),
            ]
            two = [
                copy(G.at[oy, :, x, a, cols], A2.at[:, r, cols], ydev),
                copy(G.at[y, :, ox, b, cols], B2.at[:, r, cols], xdev),
            ]
            q = pl.ds(a.start, a.size + b.size)
            three = [
                Group(
                    [(G.at[y, (z + k) % ZN, x, q, cols], R3.at[k - 1, q, cols], zdev(k)) for k in range(1, ZN)],
                    R3.at[:, q, cols],
                )
            ]
            steps.append((a, b, r, cols, one, two, three))

        def add(target, source):
            target[...] = (target[...].astype(FULL) + source[...].astype(FULL)).astype(LOW)

        def go(i):
            start(steps[i][4])

        def second(i):
            a, b, r, cols, one, two, three = steps[i]
            landed(one[:1])

            @pl.loop(0, ZN)
            def _(k):
                add(G.at[oy, k, x, a, cols], A1.at[oy, k, r, cols])

            start(two[:1])
            landed(one[1:])

            @pl.loop(0, ZN)
            def _(k):
                add(G.at[y, k, ox, b, cols], B1.at[k, ox, r, cols])

            start(two[1:])

            @pl.loop(0, ZN)
            def _(k):
                add(G.at[y, k, x, a, cols], A1.at[y, k, r, cols])
                add(G.at[y, k, x, b, cols], B1.at[k, x, r, cols])

        def third_step(i):
            a, b, r, cols, one, two, three = steps[i]
            landed(two)

            @pl.loop(0, ZN)
            def _(k):
                add(G.at[y, k, x, a, cols], A2.at[k, r, cols])
                add(G.at[y, k, x, b, cols], B2.at[k, r, cols])

            start(three)

        def last(i, out):
            a, b, r, cols, one, two, three = steps[i]
            landed(three)
            for q in (a, b):
                v = G[y, z, x, q, cols].astype(FULL)
                for k in range(ZN - 1):
                    v = v + R3[k, q, cols].astype(FULL)
                out[q, cols] = v

        return go, second, third_step, last

    def reduce_wide(G, plan, A1, B1, A2, B2, A3, B3, EA, EB):
        steps = []
        for a, b, r, cols in plan:
            one = [
                copy(G.at[oy, :, :, a, cols], A1.at[:, :, r, cols], ydev),
                copy(G.at[:, :, ox, b, cols], B1.at[:, :, r, cols], xdev),
            ]
            two = [
                ZReduce(
                    lambda i, a=a, cols=cols: G.at[y, i, :, a, cols],
                    lambda k, r=r, cols=cols: A2.at[k, :, r, cols],
                    EA.at[:, r, cols],
                ),
                ZReduce(
                    lambda i, b=b, cols=cols: G.at[:, i, x, b, cols],
                    lambda k, r=r, cols=cols: B2.at[k, :, r, cols],
                    EB.at[:, r, cols],
                ),
            ]
            three = [
                copy(G.at[y, z, ox, a, cols], A3.at[r, cols], xdev),
                copy(G.at[oy, z, x, b, cols], B3.at[r, cols], ydev),
            ]
            steps.append((a, b, r, cols, one, two, three))

        def add(target, sources):
            v = target[...].astype(FULL)
            for source in sources:
                v = v + source[...].astype(FULL)
            target[...] = v.astype(LOW)

        def go(i):
            start(steps[i][4])

        def second(i):
            a, b, r, cols, one, two, three = steps[i]
            landed(one)

            @pl.loop(0, ZN)
            def _(k):
                for j in range(2):
                    add(G.at[y, k, j, a, cols], [A1.at[k, j, r, cols]])
                    add(G.at[j, k, x, b, cols], [B1.at[j, k, r, cols]])

            start(two)

        def middle(i):
            for m in steps[i][5]:
                m.middle()

        def third_step(i):
            a, b, r, cols, one, two, three = steps[i]
            landed(two)
            for j in range(2):
                add(G.at[y, z, j, a, cols], [A2.at[k, j, r, cols] for k in range(ZN - 1)])
                add(G.at[j, z, x, b, cols], [B2.at[k, j, r, cols] for k in range(ZN - 1)])
            start(three)

        def last(i, out):
            a, b, r, cols, one, two, three = steps[i]
            landed(three)
            for q, R in ((a, A3), (b, B3)):
                out[q, cols] = G[y, z, x, q, cols].astype(FULL) + R[r, cols].astype(FULL)

        return go, second, third_step, last, middle

    rp = reduce_wide(Gp, by_rows, RpA1, RpB1, RpA2, RpB2, RpA3, RpB3, RpEA, RpEB)
    rf = reduce_copies(Gf, by_rows, RfA1, RfB1, RfA2, RfB2, Rf3)
    weight_grad(T0, H, Gp, 0, width)
    rp[0](0)
    transpose_all(N2, T1)
    all_in(pw)
    rp[0](1)


    def pair_nt(A, W, columns):
        def block(flat):
            return dot_nt(A[0, flat, :columns], W[0].reshape(width, W.shape[-1])) + dot_nt(
                A[1, flat, :columns], W[1].reshape(width, W.shape[-1])
            )

        return block

    @pl.loop(0, 4)
    def _(k):
        b, h = k // 2, k % 2
        flat = pl.ds(pl.multiple_of(h * half, half), half)
        g = (dot(COT[h], Wp[b].reshape(width, width)) * GPR[b, flat, :]).astype(LOW)
        PG[b, flat, :] = g
        VG[pl.ds(FCB + b, 1), :] += jnp.sum(g.astype(FULL), axis=0, keepdims=True)

    p2_c = [copy(parts[3], V1, cdev)]
    split_rows(pair_nt(PG, Wf, width), parts[3], parts[0], p2_c)
    rp[1](0)
    weight_grad(T1, PG, Gf, 0, width)
    rf[0](0)
    rf[0](1)
    landed(p2_c)

    sent(n2_c)

    def norm_back(dy, n, rstd, gain):
        e = dy * gain
        return (e - jnp.mean(e, axis=-1, keepdims=True) - n * jnp.mean(e * n, axis=-1, keepdims=True)) * rstd

    def add_row(i, v):
        VG[i : i + 1, :] += jnp.sum(v, axis=0, keepdims=True)

    @pl.loop(0, half // 128)
    def _(i):
        r = row_tile(i)
        dy = GPR[0, r, :] + V1[r, :]
        n = N2F[r, :]
        add_row(GAIN2, dy * n)
        add_row(SHIFT2, dy)
        cot = COT[c, r, :].astype(FULL)
        add_row(PROJB, cot)
        g = cot + norm_back(dy, n, RS[r, 1:2], vrow(GAIN2))
        N2F[r, :] = g
        low = g.astype(LOW)
        add_row(OUTB, low.astype(FULL))
        N2[c, r, :] = low

    ag_c = [copy(N2.at[c], N2.at[c], cdev)]
    start(ag_c)

    def vector_copies(first, last):
        r = pl.ds(first, last - first)
        over_z = [Group([(VG.at[r], VZ.at[k - 1, r], zdev(k)) for k in range(1, ZN)], VZ.at[:, r])]
        mine = VO.at[(y * 2 + x) * 2 + c, r]
        return r, over_z, mine, [Group([(mine, mine, d) for d in near], VO.at[pl.ds(0, 7), r])]

    def vector_second(v):
        r, over_z, mine, over_near = v
        landed(over_z)
        mine[...] = VG[r, :] + VZ[0, r, :] + VZ[1, r, :] + VZ[2, r, :]
        start(over_near)

    def vector_last(v):
        r, over_z, mine, over_near = v
        landed(over_near)
        for core in range(2):
            vo_ref[core, r, :] = (VO[core, r, :] + VO[2 + core, r, :]) + (VO[4 + core, r, :] + VO[6 + core, r, :])

    late = vector_copies(0, 4)
    er = pl.ds(8, VEC - 8)
    early = [
        [Group([(VG.at[er], VZ.at[k - 1, er], zdev(k)) for k in range(1, ZN)], VZ.at[:, er])],
        [copy(VO.at[0, er], VO.at[1, er], xdev)],
        [copy(VO.at[2, er], VO.at[3, er], ydev)],
        [copy(vo_ref.at[c, er], vo_ref.at[c, er], cdev)],
    ]
    start(early[0])

    def early_hop(i):
        landed(early[i])
        if i == 0:
            VO[0, er, :] = VG[er, :] + VZ[0, er, :] + VZ[1, er, :] + VZ[2, er, :]
        elif i == 1:
            VO[2, er, :] = VO[0, er, :] + VO[1, er, :]
        else:
            vo_ref[c, er, :] = VO[2, er, :] + VO[3, er, :]
        start(early[i + 1])

    pm_c = [copy(parts[1], V0, cdev)]
    split_rows(pair_nt(H, Wp, width), parts[1], MID, pm_c, MID)
    rp[1](1)
    transpose_all(N1, T1)
    landed(ag_c)

    @pl.loop(0, nrb)
    def _(i):
        h, off = i // (half // rblk), i % (half // rblk)
        rows = pl.ds(pl.multiple_of(off * rblk, rblk), rblk)
        flat = pl.ds(pl.multiple_of(i * rblk, rblk), rblk)
        g = dot(N2[h, rows, :], Wo[...].reshape(width, Wo.shape[-1])).astype(LOW)
        row = lax.broadcasted_iota(jnp.int32, (8, 128), 0)
        lane = lax.broadcasted_iota(jnp.int32, (8, 128), 1)
        pick = jnp.where(lane // HD == row, 1.0, 0.0).astype(LOW)
        for p in range(3):
            gp = tile(g, p)
            DO[p, flat, :] = gp
            prod = gp.astype(FULL) * CTX[p, flat, :].astype(FULL)
            high = prod.astype(LOW)
            rest = (prod - high.astype(FULL)).astype(LOW)
            d = dot_nt(pick, high) + dot_nt(pick, rest)
            for e in range(2):
                DELR[2 * p + e, :, flat] = d[e : e + 1, :]

    transpose_all(N2, T0)

    @pl.loop(0, 2)
    def _(m):
        rows = pl.ds(pl.multiple_of(m * (width // 2), width // 2), width // 2)
        g = dot(T0[rows, :], wide(CTX, pl.ds(0, seq_len)))
        g = g.astype(LOW).reshape(ZN // 2, XN, 2, width // (2 * GROUPS), Wo.shape[-1])
        Go[pl.ds(m * (ZN // 2), ZN // 2)] = g

    ro = [
        [copy(Go.at[:, :, oy, oa], Ro1A, ydev), copy(Go.at[:, ox, :, ob], Ro1B, xdev)],
        [copy(Go.at[:, ox, y, oa], Ro2A, xdev), copy(Go.at[:, x, oy, ob], Ro2B, ydev)],
        [Group([(Go.at[(z + k) % ZN, x, y], Ro3.at[k - 1], zdev(k)) for k in range(1, ZN)], Ro3)],
        [Group([(go_ref.at[t], go_ref.at[t], d) for d in (cdev, ydev, gdev)], go_ref.at[pl.ds(0, 3)])],
    ]

    def ro_second():
        landed(ro[0])

        @pl.loop(0, ZN)
        def _(k):
            for i in range(XN):
                Go[k, i, y, oa] = (Go[k, i, y, oa].astype(FULL) + Ro1A[k, i].astype(FULL)).astype(LOW)
                Go[k, x, i, ob] = (Go[k, x, i, ob].astype(FULL) + Ro1B[k, i].astype(FULL)).astype(LOW)

        start(ro[1])

    def ro_third():
        landed(ro[1])

        @pl.loop(0, ZN)
        def _(k):
            Go[k, x, y, oa] = (Go[k, x, y, oa].astype(FULL) + Ro2A[k].astype(FULL)).astype(LOW)
            Go[k, x, y, ob] = (Go[k, x, y, ob].astype(FULL) + Ro2B[k].astype(FULL)).astype(LOW)

        start(ro[2])

    def ro_last():
        landed(ro[2])
        v = Go[z, x, y].astype(FULL)
        for k in range(ZN - 1):
            v = v + Ro3[k].astype(FULL)
        go_ref[t] = v
        start(ro[3])

    def attention_back(p, plan):
        DQ[...] = jnp.zeros(DQ.shape, FULL)
        for b in range(nrb):
            rows = pl.ds(b * rblk, rblk)
            first = 0 if b * rblk < half else b * rblk
            n = seq_len - first
            keys, values = KP[p, rows, :], VP[p, rows, :]
            queries, grads = QP[p, first:, :], DO[p, first:, :]
            key = b * rblk + lax.broadcasted_iota(jnp.int32, (rblk, 1), 0)
            limit = jnp.where(key < prefix, 0, key)
            shut = (b + 1) * rblk - first
            query = first + lax.broadcasted_iota(jnp.int32, (rblk, shut), 1)
            dk, dv = [], []
            for e in range(2):
                ke, ve = lane_part(keys, e), lane_part(values, e)
                sc = dot_nt(ke, queries) - LSER[2 * p + e, :, first:]
                head = jnp.where(query >= limit, sc[:, :shut], -1e30)
                w = jnp.exp(jnp.concatenate([head, sc[:, shut:]], axis=1) if shut < n else head)
                dw = dot_nt(ve, grads) - DELR[2 * p + e, :, first:]
                ds = (w * dw).astype(LOW)
                dv.append(dot(w.astype(LOW), grads))
                dk.append(dot(ds, queries))
                DQ[first:, :] += dot_tn(ds, ke)
            KP[p, rows, :] = jnp.where(low_lanes(dk[0]), dk[0], dk[1]).astype(LOW)
            VP[p, rows, :] = jnp.where(low_lanes(dv[0]), dv[0], dv[1]).astype(LOW)
            meanwhile(p, b, plan)
        QP[p, :, :] = (DQ[...] * 0.125).astype(LOW)

    away = {
        (0, 0): [lambda: rp[4](0), lambda: rf[1](0)],
        (0, 3): [lambda: start(ro[0]), lambda: early_hop(0)],
        (1, 0): [lambda: rf[1](1)],
        (1, 1): [lambda: rp[4](1)],
        (1, 2): [lambda: rf[2](0)],
        (1, 3): [lambda: early_hop(1)],
    }

    @pl.loop(0, 2)
    def _(p):
        attention_back(p, away)

    packed = Wq.shape[-1]
    sent_all(fw)

    @pl.loop(0, nrb)
    def _(i):
        flat = pl.ds(pl.multiple_of(i * rblk, rblk), rblk)
        for b in range(2):
            for k, ref in enumerate((QP, KP, VP)):
                g = ref[b, flat, :]
                H[b, flat, k * 128 : (k + 1) * 128] = g
                VG[QKVB + b : QKVB + b + 1, k * 128 : (k + 1) * 128] += jnp.sum(g.astype(FULL), axis=0, keepdims=True)

    main, rest = pl.ds(0, 384), pl.ds(384, packed - 384)
    by_lanes = [pairs[0] + (pl.ds(0, third), main), pairs[1] + (pl.ds(third, 2 * third), main)]
    by_lanes += [pairs[1] + (pl.ds(third, 2 * third), rest), pairs[0] + (pl.ds(0, third), rest)]
    weight_grad(T1, H, Wf, 0, 384)
    rq = reduce_copies(Wf, by_lanes, RqA1, RqB1, RqA2, RqB2, Rq3)
    rq[0](0)
    rq[0](1)
    landed(pm_c)

    @pl.loop(0, half // 128)
    def _(i):
        r = row_tile(i)
        TOK[r, :] = (MID[r, :] + (V0[r, :] + vrow(PROJB))).astype(LOW)

    out_c = [pltpu.make_async_copy(TOK, bo_h, ls.at[0]), pltpu.make_async_copy(N1.at[c], ig_h, ls.at[1])]
    out_c[0].start()

    away = {
        (2, 0): [lambda: rf[2](1)],
        (2, 1): [lambda: early_hop(2), ro_second],
        (2, 3): [lambda: rp[2](0), lambda: rq[1](0)],
    }
    attention_back(2, away)

    @pl.loop(0, nrb)
    def _(i):
        flat = pl.ds(pl.multiple_of(i * rblk, rblk), rblk)
        q, k, v = (ref[2, flat, :].astype(FULL) for ref in (QP, KP, VP))
        first = low_lanes(q)
        packs = (
            (jnp.where(first, q, roll(k)), jnp.where(first, v, 0.0)),
            (jnp.where(first, roll(q), k), jnp.where(first, roll(v), 0.0)),
        )
        for b in range(2):
            for j in range(2):
                at_j = slice(384 + 128 * j, 512 + 128 * j)
                H[b, flat, at_j] = packs[b][j].astype(LOW)
                VG[QKVB + b : QKVB + b + 1, at_j] += jnp.sum(packs[b][j], axis=0, keepdims=True)

    weight_grad(T1, H, Wf, 384, packed)
    rq[0](2)
    rq[0](3)
    rq[1](1)

    p1_c = [copy(parts[1], V1, cdev)]
    sent(pm_c)
    split_rows(pair_nt(H, Wq, packed), parts[1], parts[2], p1_c)
    rq[2](0)
    rp[2](1)
    ro_third()
    landed(p1_c)

    sent(n1_c)

    @pl.loop(0, half // 128)
    def _(i):
        r = row_tile(i)
        dy = GPR[1, r, :] + V1[r, :]
        n = N1F[r, :]
        add_row(GAIN1, dy * n)
        add_row(SHIFT1, dy)
        N1[c, r, :] = (N2F[r, :] + norm_back(dy, n, RS[r, 0:1], vrow(GAIN1))).astype(LOW)

    out_c[1].start()

    start(late[1])
    rq[2](1)
    rq[1](2)
    rq[1](3)
    gp_ref, gf_ref = MID.at[pl.ds(0, 2 * hr)], MID.at[pl.ds(2 * hr, 2 * hr)]
    out_c += [pltpu.make_async_copy(gp_ref, gp_h, ls.at[2]), pltpu.make_async_copy(gf_ref, gf_h, ls.at[3])]
    rp[3](0, gp_ref)
    rp[3](1, gp_ref)
    out_c[2].start()
    rf[3](0, gf_ref)
    rf[3](1, gf_ref)
    out_c[3].start()
    rq[2](2)
    rq[2](3)
    vector_second(late)
    ro_last()
    landed(early[3])
    out_c += [
        pltpu.make_async_copy(a, b, ls.at[4 + i]) for i, (a, b) in enumerate(((go_ref, go_h), (gq_ref, gq_h), (vo_ref, vo_h)))
    ]
    rq[3](0, gq_ref)
    rq[3](1, gq_ref)
    landed(ro[3])
    out_c[4].start()
    vector_last(late)
    out_c[6].start()
    rq[3](2, gq_ref)
    rq[3](3, gq_ref)
    out_c[5].start()

    waited = {id(m) for m in n2_c + pm_c + n1_c}
    for step in fw:
        for group in step:
            waited |= {id(m) for m in group}
    sent([m for m in pending if id(m) not in waited])
    for cp in out_c:
        cp.wait()


def gather_groups(v, axis, repeat, groups):
    if repeat == 1:
        return v
    return lax.all_gather(v, "dp", axis=axis, axis_index_groups=groups, tiled=True)


def scatter_groups(v, axis, repeat, groups):
    if repeat == 1:
        return v
    return lax.psum_scatter(v, "dp", scatter_dimension=axis, axis_index_groups=groups, tiled=True)


def on_device(
    dp_size,
    tokens,
    prefix,
    cotangent,
    first_gain,
    first_shift,
    qkv_weight,
    qv_bias,
    out_weight,
    out_bias,
    second_gain,
    second_shift,
    fc_weight,
    fc_bias,
    proj_weight,
    proj_bias,
):
    repeat = dp_size // GROUPS
    groups = [[g * repeat + i for i in range(repeat)] for g in range(GROUPS)]
    half, width = tokens.shape
    seq_len = 2 * half

    def whole(v, axis):
        return gather_groups(v.astype(LOW), axis, repeat, groups).astype(FULL) if repeat > 1 else v

    params = [
        whole(first_gain, 0), whole(first_shift, 0), whole(qkv_weight, 1), whole(qv_bias, 1), whole(out_weight, 1),
        whole(out_bias, 0), whole(second_gain, 0), whole(second_shift, 0), whole(fc_weight, 0), whole(fc_bias, 0),
        whole(proj_weight, 1), whole(proj_bias, 0),
    ]
    params[4], params[10] = params[4].T, params[10].T
    rows = params[8].shape[0]
    cols = params[2].shape[2]
    units = params[8].shape[1]
    pair = 2 * HD
    packed, own = 3 * cols + HD, 2 * cols
    hr = rows // 2
    ANY = pl.BlockSpec(memory_space=pl.ANY)

    def reduce_space(lanes):
        return [
            pltpu.VMEM((2, ZN, hr, lanes), LOW),
            pltpu.VMEM((ZN, XN, hr, lanes), LOW),
            pltpu.VMEM((ZN, hr, lanes), LOW),
            pltpu.VMEM((ZN, hr, lanes), LOW),
            pltpu.VMEM((ZN - 1, rows, lanes), LOW),
        ]

    token_low = pltpu.VMEM((2, half, width), LOW)
    token_full = pltpu.VMEM((half, width), FULL)
    unit_low = pltpu.VMEM((2, seq_len, width), LOW)
    heads = pltpu.VMEM((3, seq_len, pair), LOW)
    scratch = (
        [
            pltpu.VMEM((2, ZN, XN, rows, packed), LOW),
            pltpu.VMEM((ZN, XN, 2, hr, own), LOW),
            pltpu.VMEM((2, ZN, XN, rows, width), LOW),
            pltpu.VMEM((2, ZN, XN, rows, width), LOW),
            pltpu.VMEM((ZN, XN, 2, hr, own), LOW),
            pltpu.VMEM((2, ZN, XN, rows, width), LOW),
            pltpu.VMEM((2, ZN, XN, rows, width), LOW),
        ]
        + reduce_space(packed)
        + reduce_space(width)
        + [
            pltpu.VMEM((ZN, XN, hr, width), LOW),
            pltpu.VMEM((2, ZN, hr, width), LOW),
            pltpu.VMEM((ZN - 1, XN, hr, width), LOW),
            pltpu.VMEM((ZN - 1, 2, hr, width), LOW),
            pltpu.VMEM((hr, width), LOW),
            pltpu.VMEM((hr, width), LOW),
            pltpu.VMEM((XN, hr, width), LOW),
            pltpu.VMEM((2, hr, width), LOW),
        ]
        + [
            pltpu.VMEM((ZN, XN, hr // 3 * 2, own), LOW),
            pltpu.VMEM((ZN, 2, hr // 3, own), LOW),
            pltpu.VMEM((ZN, hr // 3 * 2, own), LOW),
            pltpu.VMEM((ZN, hr // 3, own), LOW),
            pltpu.VMEM((ZN - 1, hr, own), LOW),
        ]
        + [
            pltpu.VMEM((half, width), LOW),
            token_low,
            token_full,
            token_full,
            pltpu.VMEM((half, 128), FULL),
            token_low,
            token_low,
            pltpu.VMEM((width, seq_len), LOW),
            pltpu.VMEM((width, seq_len), LOW),
        ]
        + [heads] * 5
        + [
            pltpu.VMEM((seq_len, pair), FULL),
            pltpu.VMEM((6, 1, seq_len), FULL),
            pltpu.VMEM((6, 1, seq_len), FULL),
        ]
        + [token_full] * 3
        + [unit_low, pltpu.VMEM((2, seq_len, width), FULL), unit_low]
        + [
            pltpu.VMEM((8, rows), FULL),
            pltpu.VMEM((2, rows), FULL),
            pltpu.VMEM((1, 4 * rows), FULL),
            pltpu.VMEM((3, rows, cols), FULL),
            pltpu.VMEM((2, hr, own), LOW),
            pltpu.VMEM((3, half, pair), LOW),
            pltpu.VMEM((ZN, XN, 2, hr, own), LOW),
            pltpu.VMEM((GROUPS, VEC, 128), LOW),
            pltpu.VMEM((VEC, width), FULL),
            pltpu.VMEM((VEC, width), FULL),
            pltpu.VMEM((ZN - 1, VEC, width), FULL),
        ]
        + [
            pltpu.VMEM((8, VEC, width), FULL),
            pltpu.VMEM((rows, packed), FULL),
            pltpu.VMEM((4, hr, own), FULL),
            pltpu.VMEM((2, VEC, width), FULL),
            pltpu.SMEM(prefix.shape, prefix.dtype),
        ]
        + [
            pltpu.SemaphoreType.DMA((SEMS,)),
            pltpu.SemaphoreType.DMA((SEMS,)),
            pltpu.SemaphoreType.DMA((16,)),
        ]
    )
    out_shape = [
        jax.ShapeDtypeStruct((half, width), LOW),
        jax.ShapeDtypeStruct((half, width), LOW),
        jax.ShapeDtypeStruct((rows, packed), FULL),
        jax.ShapeDtypeStruct((4, hr, own), FULL),
        jax.ShapeDtypeStruct((rows, width), FULL),
        jax.ShapeDtypeStruct((rows, width), FULL),
        jax.ShapeDtypeStruct((2, VEC, width), FULL),
    ]
    grown = pl.pallas_call(
        functools.partial(block_kernel, repeat, seq_len),
        out_shape=out_shape,
        in_specs=[ANY] * 15,
        out_specs=[ANY] * 7,
        scratch_shapes=scratch,
        compiler_params=pltpu.CompilerParams(
            collective_id=0, has_side_effects=True, vmem_limit_bytes=62 * 1024 * 1024
        ),
    )(tokens, prefix, cotangent, *params)

    vector = jax.ShapeDtypeStruct((rows,), FULL)
    results = pl.pallas_call(
        functools.partial(unpack_kernel, repeat),
        out_shape=[
            out_shape[0],
            out_shape[1],
            vector,
            vector,
            jax.ShapeDtypeStruct((3, rows, cols), FULL),
            jax.ShapeDtypeStruct((2, rows), FULL),
            jax.ShapeDtypeStruct((rows, width), FULL),
            vector,
            vector,
            vector,
            jax.ShapeDtypeStruct((rows, units), FULL),
            jax.ShapeDtypeStruct((4 * rows,), FULL),
            jax.ShapeDtypeStruct((rows, units), FULL),
            vector,
        ],
        in_specs=[ANY] * 7,
        out_specs=[ANY] * 14,
        scratch_shapes=[
            pltpu.VMEM((rows, packed), FULL),
            pltpu.VMEM((4, hr, own), FULL),
            pltpu.VMEM((2, VEC, width), FULL),
            pltpu.VMEM((3, rows, cols), FULL),
            pltpu.VMEM((rows, width), FULL),
            pltpu.VMEM((half, width), LOW),
            pltpu.VMEM((half, width), LOW),
            pltpu.VMEM((rows, units), FULL),
            pltpu.VMEM((rows, units), FULL),
            pltpu.VMEM((8, rows), FULL),
            pltpu.VMEM((2, rows), FULL),
            pltpu.VMEM((1, 4 * rows), FULL),
            pltpu.SemaphoreType.DMA((21,)),
        ],
        compiler_params=pltpu.CompilerParams(vmem_limit_bytes=62 * 1024 * 1024),
    )(*grown)
    results = [v.T if i in (6, 12) else v for i, v in enumerate(results)]
    along = (None, None, 0, 0, 1, 1, 1, 0, 0, 0, 0, 0, 1, 0)
    return tuple(
        v if repeat == 1 or axis is None else scatter_groups(v, axis, repeat, groups)
        for v, axis in zip(results, along, strict=True)
    )


def unpack_kernel(
    repeat, bo, ig, gq_h, go_h, gf, gp, vo_h,
    bo_out, ig_out, gain1, shift1, wq_h, qvb_h, wo_h, outb, gain2, shift2, wf, fcb_h, wp, projb,
    gq, go, vo, wq, wo, b1, b2, w1, w2, sv, sq, sf, sems,
):
    moves = [(vo_h, vo), (gq_h, gq), (go_h, go), (ig, b2), (bo, b1), (gf, w1), (gp, w2)]
    moves += [(wq, wq_h), (wo, wo_h), (b2, ig_out), (b1, bo_out), (w1, wf), (w2, wp)]
    vectors = ((GAIN1, gain1), (SHIFT1, shift1), (OUTB, outb), (GAIN2, gain2), (SHIFT2, shift2), (PROJB, projb))
    moves += [(sv.at[j], out) for j, (_, out) in enumerate(vectors)] + [(sq, qvb_h), (sf.at[0], fcb_h)]
    moves = [pltpu.make_async_copy(a, b, sems.at[i]) for i, (a, b) in enumerate(moves)]
    for cp in moves[:7]:
        cp.start()
    moves[1].wait()
    for k in range(3):
        wq[k] = jnp.concatenate(
            [gq[:, k * 128 : (k + 1) * 128], gq[:, 384 + k * HD : 384 + (k + 1) * HD]], axis=1
        )
    moves[7].start()
    for i in (3, 4):
        moves[i].wait()
        moves[i + 6].start()
    moves[2].wait()
    m = [jnp.concatenate([go[core], go[2 + core]], axis=0) for core in range(2)]
    wo[...] = jnp.concatenate(
        [
            v
            for b in range(2)
            for core in range(2)
            for v in (m[core][:, b * 128 : (b + 1) * 128], m[core][:, 256 + b * HD : 256 + (b + 1) * HD])
        ],
        axis=1,
    )
    moves[8].start()
    for i in (5, 6):
        moves[i].wait()
        moves[i + 6].start()
    moves[0].wait()
    s = lax.axis_index("dp") // repeat
    width = vo.shape[2]
    n = sv.shape[1]
    both = pltpu.roll(vo[0] + vo[1], (GROUPS - s) % GROUPS * n, 1)
    for j, (i, _) in enumerate(vectors):
        sv[j : j + 1, :] = both[i : i + 1, :n]
    owner = s // 2
    core, b, odd = owner % 2, owner // 2, s % 2
    place = lax.broadcasted_iota(jnp.int32, (1, width), 1)

    def lanes(v, first, last, shift):
        v = jnp.where((place >= first) & (place < last), v, 0.0)
        return pltpu.roll(v, shift % width, 1) if shift % width else v

    row = vo[core, pl.ds(QKVB + b, 1), :]
    q = lanes(row, 0, 128, 0) + lanes(row, 384, 448, -256)
    v = lanes(row, 256, 384, -256) + lanes(row, 512, 576, -384)
    back = (width - odd * n) % width
    sq[0:1, :] = pltpu.roll(q, back, 1)[:, :n]
    sq[1:2, :] = pltpu.roll(v, back, 1)[:, :n]
    row = vo[core, pl.ds(FCB + b, 1), :]
    sf[...] = pltpu.roll(row, odd * (width // 2), 1)[:, : width // 2]
    for i in range(13, 21):
        moves[i].start()
    for i in range(7, 21):
        moves[i].wait()


def solution(mesh):
    placed = (
        P(("dp", "tensor"), None),
        P("dp"),
        P(("dp", "tensor"), None),
        P("dp"),
        P("dp"),
        P(None, "dp", "tensor"),
        P(None, "dp"),
        P(None, "dp"),
        P("dp"),
        P("dp"),
        P("dp"),
        P("dp", "tensor"),
        P("dp"),
        P("tensor", "dp"),
        P("dp"),
    )
    return jax.shard_map(
        functools.partial(on_device, mesh.shape["dp"]),
        mesh=mesh,
        in_specs=placed,
        out_specs=(placed[0], placed[0]) + placed[3:],
        check_vma=False,
    )
```
